32 devices in a mesh: section: 2 (over core), fsdp: 8 (over z, y), dp: 2 (over x).
Axes of the slice: x: 2, y: 2, z: 4, core: 2. Of those that a mesh axis runs over, the one named last changes fastest.
Arguments:
- inputs: bfloat16 [4096, 1536], P(('fsdp', 'dp')), may hold values from -6 to 6
- seq_lengths: int32 [32, 3], P(('fsdp', 'dp')), may hold values from 1 to 64, 128 in all within a row
- norm_gain: float32 [2, 1536], P('section'), may hold values from 0.5 to 1.5
- in_w: bfloat16 [2, 1536, 6448], P('section', 'fsdp'), may hold values from -0.15625 to 0.15625
- conv_w: float32 [2, 4, 3328], P('section'), may hold values from -3 to 3
- conv_b: float32 [2, 3328], P('section'), may hold values from -1.5 to 1.5
- dt_bias: float32 [2, 48], P('section'), may hold values from -4 to -1
- a_log: float32 [2, 48], P('section'), may hold values from -2 to 1
- skip: float32 [2, 48], P('section'), may hold values from 0.5 to 1.5
- out_gain: float32 [2, 3072], P('section'), may hold values from 0.5 to 1.5
- out_w: bfloat16 [2, 3072, 1536], P('section', 'fsdp'), may hold values from -0.109375 to 0.109375
- cotangent: bfloat16 [4096, 1536], P(('fsdp', 'dp')), may hold values from -6 to 6
Outputs:
- phase_out: bfloat16 [2, 4096, 1536], P('section', ('fsdp', 'dp'))
- input_grad: bfloat16 [2, 4096, 1536], P('section', ('fsdp', 'dp'))
- grad_norm_gain: float32 [2, 1536], P('section')
- grad_in_w: float32 [2, 1536, 6448], P('section', 'fsdp')
- grad_conv_w: float32 [2, 4, 3328], P('section')
- grad_conv_b: float32 [2, 3328], P('section')
- grad_dt_bias: float32 [2, 48], P('section')
- grad_a_log: float32 [2, 48], P('section')
- grad_skip: float32 [2, 48], P('section')
- grad_out_gain: float32 [2, 3072], P('section')
- grad_out_w: float32 [2, 3072, 1536], P('section', 'fsdp')
The draws below stay inside these ranges and needn't reach their ends.
Inputs may be any that keep to these rules, and one draw needn't show every extreme that they name: `seq_lengths`: each row sums to 128; the largest entry of every row is exactly 64.
All inputs are finite; a program needn't handle non-finite values.
Results may differ from the reference program's by a relative error of at most 0.02.
The reference program's roundings to bfloat16 on the way count: a program that leaves them out, or rounds other values in their place, can miss the bound.
Values may be sent and summed in bfloat16 or wider, within the bound.
No kernel may reach another device: no remote copies, remote signals or barrier semaphores. Data moves between devices by JAX's collectives and lax.ppermute only.
A program may use at most 448 MiB of HBM per device.

```python
import math
import jax
import jax.numpy as jnp
import numpy as np
from jax import lax

D = 1536
HEADS = 48
CONV = 4
MB_TOK = 128
MICRO = 2
SEQS = 3
INNER = 3072
CONV_CH = 3328
PROJ = 6448
LONGEST = 64
TOKENS = 4096
N_FSDP = 8
N_DP = 2


def levels(key, dims, pieces, low, high):
    def one(dim, shards_of):
        draws = jax.random.uniform(jax.random.fold_in(jax.random.fold_in(key, 6), dim), (shards_of,), jnp.float32, low / len(pieces), high / len(pieces))
        return jnp.repeat(jnp.exp(draws), dims[dim] // shards_of).reshape((-1,) + (1,) * (len(dims) - dim - 1))

    loudness = one(*pieces[0])
    for cut in pieces[1:]:
        loudness = loudness * one(*cut)
    return loudness


def profile(amount, total, reach, slope):
    loads = [(1 << 20) // math.isqrt(standing ** slope) + 1 for standing in range(2, amount + 1)]
    spare, holding = total - reach - (amount - 1), [1] * (amount - 1)
    while spare > 0:
        movable = [i for i in range(amount - 1) if holding[i] < reach]
        pool, remaining = sum([loads[i] for i in movable]), spare
        for i in movable:
            extra = min(reach - holding[i], max(1, remaining * loads[i] // pool), spare)
            holding[i] = holding[i] + extra
            spare = spare - extra
    return np.array([reach] + holding)


def uneven_parts(stream_key, number_of, total, limit, slope):
    if number_of == 2:
        one = jax.random.randint(stream_key, (), max(1, total - limit), min(limit, total - 1) + 1)
        return jnp.stack([one, total - one])
    tallies = jnp.asarray(profile(number_of, total, limit, slope), jnp.int32)
    couples = (number_of - 1) // 2
    source_of, receiver = tallies[1:1 + 2 * couples:2], tallies[2:2 + 2 * couples:2]
    margin = jnp.minimum(source_of - 1, limit - receiver)
    passed = jax.random.randint(jax.random.fold_in(stream_key, 1), (couples,), 0, 1 << 20) % (margin + 1)
    tallies = tallies.at[1:1 + 2 * couples:2].set(source_of - passed).at[2:2 + 2 * couples:2].set(receiver + passed)
    return tallies[jax.random.permutation(jax.random.fold_in(stream_key, 2), number_of)]


def normal_values(key, shape, scale, bound, shards=(), held_as=jnp.bfloat16):
    array = scale * jax.random.normal(key, shape, jnp.float32)
    if shards:
        array = array * levels(key, shape, shards, -0.22, 0.18)
    return jnp.clip(array, -bound, bound).astype(held_as)


def setup_inputs(seed: int = 0) -> dict:
    key_of = jax.random.split(jax.random.key(seed), 13)
    return {
        "inputs": normal_values(key_of[0], (TOKENS, D), 1.0, 6.0, ((0, 16),)),
        "seq_lengths": jax.vmap(lambda own: uneven_parts(own, SEQS, MB_TOK, LONGEST, 0))(jax.random.split(key_of[1], (N_FSDP * N_DP * MICRO))).reshape((N_FSDP * N_DP * MICRO, SEQS)).astype(jnp.int32),
        "norm_gain": jnp.clip(1.0 + 0.1 * jax.random.normal(key_of[2], (2, D), jnp.float32), 0.5, 1.5),
        "in_w": normal_values(key_of[3], (2, D, PROJ), D ** -0.5, 0.15625, ((0, 2), (1, 8))),
        "conv_w": normal_values(key_of[4], (2, CONV, CONV_CH), CONV ** -0.5, 3.0, ((0, 2),), jnp.float32),
        "conv_b": normal_values(key_of[5], (2, CONV_CH), 0.3, 1.5, ((0, 2),), jnp.float32),
        "dt_bias": jnp.clip(-4.0 + 3.0 * jax.random.uniform(key_of[6], (2, HEADS), jnp.float32) ** levels(key_of[6], (2, HEADS), ((0, 2),), -0.2, 0.2), -4.0, -1.0),
        "a_log": jnp.clip(-2.0 + 3.0 * jax.random.uniform(key_of[7], (2, HEADS), jnp.float32) ** levels(key_of[7], (2, HEADS), ((0, 2),), -0.2, 0.2), -2.0, 1.0),
        "skip": jnp.clip(0.5 + 1.0 * jax.random.uniform(key_of[8], (2, HEADS), jnp.float32) ** levels(key_of[8], (2, HEADS), ((0, 2),), -0.2, 0.2), 0.5, 1.5),
        "out_gain": jnp.clip(1.0 + 0.1 * jax.random.normal(key_of[9], (2, INNER), jnp.float32), 0.5, 1.5),
        "out_w": normal_values(key_of[10], (2, INNER, D), INNER ** -0.5, 0.109375, ((0, 2), (1, 8))),
        "cotangent": normal_values(key_of[11], (TOKENS, D), 1.0, 6.0, ((0, 16),)),
    }


@jax.custom_vjp
def low(v):
    return lax.optimization_barrier(v.astype(jnp.bfloat16)).astype(jnp.float32)

@jax.custom_vjp
def low_back(v):
    return v

def low_keep(v):
    return (low(v), None)

def low_pass(kept, grad):
    return (grad,)

def back_keep(v):
    return (v, None)

def back_low(kept, grad):
    return (low(grad),)
low.defvjp(low_keep, low_pass)
low_back.defvjp(back_keep, back_low)

def segment_of(seq_lengths, length):
    ends = jnp.cumsum(seq_lengths).astype(jnp.int32)
    positions = jnp.arange(length, dtype=jnp.int32)
    return lax.optimization_barrier(jnp.sum((positions[:, None] >= ends[None, :]).astype(jnp.int32), axis=1)).astype(jnp.int32)

def mixer(resid, segment_ids, params):
    norm_gain, in_w, conv_w, conv_b, dt_bias, a_log, skip, out_gain, out_w = params
    highest = lax.Precision.HIGHEST
    length = resid.shape[0]
    inner = out_gain.shape[0]
    heads = a_log.shape[0]
    width_conv = conv_b.shape[0]
    state = (width_conv - inner) // 2
    head_dim = inner // heads
    taps = conv_w.shape[0]
    scaled = resid * lax.rsqrt(lax.optimization_barrier(jnp.mean(resid * resid, axis=-1, keepdims=True)) + 1e-05) * norm_gain
    projected = low_back(jnp.dot(low(scaled), in_w, precision=highest))
    gate_part = projected[:, :inner]
    conv_in = projected[:, inner:inner + width_conv]
    step_raw = projected[:, inner + width_conv:]
    padded = jnp.pad(conv_in, ((taps - 1, 0), (0, 0)))
    seg_pad = jnp.concatenate([jnp.full((taps - 1,), -1, jnp.int32), segment_ids])
    mixed = conv_b + conv_w[taps - 1] * conv_in
    for back in range(1, taps):
        begin = taps - 1 - back
        same = (seg_pad[begin:begin + length] == segment_ids)[:, None]
        mixed = mixed + conv_w[taps - 1 - back] * jnp.where(same, padded[begin:begin + length], 0.0)
    activated = jax.nn.silu(mixed)
    values = activated[:, :inner]
    in_state = activated[:, inner:inner + state]
    out_state = activated[:, inner + state:]
    step = jax.nn.softplus(step_raw + dt_bias)
    log_decay = jnp.cumsum(-jnp.exp(a_log) * step, axis=0)
    positions = jnp.arange(length, dtype=jnp.int32)
    allowed = (positions[:, None] >= positions[None, :]) & (segment_ids[:, None] == segment_ids[None, :])
    allowed = allowed[:, :, None]
    gap = log_decay[:, None, :] - log_decay[None, :, :]
    decay = jnp.where(allowed, jnp.exp(jnp.where(allowed, gap, -60.0)), 0.0)
    intersection = jnp.dot(low(out_state), low(in_state).T, precision=highest)
    weights = low(intersection[:, :, None] * decay * step[None, :, :])
    head_values = values.reshape(length, heads, head_dim)
    carried = jnp.einsum('ijh,jhp->ihp', weights, low(head_values), precision=highest)
    outputs = (carried + skip[:, None] * head_values).reshape(length, inner)
    gated = outputs * jax.nn.silu(gate_part)
    normed = gated * lax.rsqrt(lax.optimization_barrier(jnp.mean(gated * gated, axis=-1, keepdims=True)) + 1e-05) * out_gain
    branch = low_back(jnp.dot(low(normed), out_w, precision=highest))
    return resid + branch

def reference(inputs, seq_lengths, norm_gain, in_w, conv_w, conv_b, dt_bias, a_log, skip, out_gain, out_w, cotangent):
    stacked = (norm_gain, in_w, conv_w, conv_b, dt_bias, a_log, skip, out_gain, out_w)
    first = tuple((p[0].astype(jnp.float32) for p in stacked))
    second = tuple((p[1].astype(jnp.float32) for p in stacked))
    blocks = TOKENS // MB_TOK
    x_blocks = inputs.reshape(blocks, MB_TOK, D)
    cot_blocks = cotangent.reshape(blocks, MB_TOK, D)

    def one_block(carry, block):
        x_block, cot_block, lengths_block = block
        segment_ids = segment_of(lengths_block, MB_TOK)
        first_out, pull_first = jax.vjp(lambda u, prm: mixer(u, segment_ids, prm), x_block.astype(jnp.float32), first)
        sent = low(first_out)
        second_out, pull_second = jax.vjp(lambda u, prm: mixer(u, segment_ids, prm), sent, second)
        sent_grad, grads_second = pull_second(cot_block.astype(jnp.float32))
        back_grad = low(sent_grad)
        in_grad, grads_first = pull_first(back_grad)
        acc_first, acc_second = carry
        acc_first = jax.tree.map(lambda a, b: a + b, acc_first, grads_first)
        acc_second = jax.tree.map(lambda a, b: a + b, acc_second, grads_second)
        emitted = (sent.astype(jnp.bfloat16), second_out.astype(jnp.bfloat16), in_grad.astype(jnp.bfloat16), back_grad.astype(jnp.bfloat16))
        return ((acc_first, acc_second), emitted)
    zeros = tuple((jnp.zeros(p.shape, jnp.float32) for p in first))
    (acc_first, acc_second), emitted = lax.scan(one_block, (zeros, zeros), (x_blocks, cot_blocks, seq_lengths))
    sent_all, second_all, in_grad_all, back_all = emitted
    phase_out = jnp.stack([sent_all.reshape(TOKENS, D), second_all.reshape(TOKENS, D)])
    input_grad = jnp.stack([in_grad_all.reshape(TOKENS, D), back_all.reshape(TOKENS, D)])
    grads = tuple((jnp.stack([a, b]) for a, b in zip(acc_first, acc_second)))
    return (phase_out, input_grad, grads[0], grads[1], grads[2], grads[3], grads[4], grads[5], grads[6], grads[7], grads[8])
```

```python
import functools

import jax
import jax.numpy as jnp
from jax import lax
from jax.experimental import pallas as pl
from jax.experimental.pallas import tpu as pltpu
from jax.sharding import PartitionSpec as P

F32 = jnp.float32
BF16 = jnp.bfloat16
LANES = 128
HALF = 64
VMEM_LIMIT = 40 * 1024 * 1024


def dot(a, b, dims=((1,), (0,)), precision=None):
    return lax.dot_general(a, b, (dims, ((), ())), precision=precision, preferred_element_type=F32)


def dot_exact(a, b, dims=((1,), (0,))):
    return dot(a, b, dims, lax.Precision.HIGHEST)


def silu_parts(x):
    gate = 1.0 / (1.0 + jnp.exp(-x))
    return gate, x * gate


def softplus(x):
    return jnp.maximum(x, 0.0) + jnp.log1p(jnp.exp(-jnp.abs(x)))


def conv_mixed(conv_in, aux, conv_w, conv_b):
    taps = conv_w.shape[0]
    mixed = conv_b + conv_w[taps - 1 : taps] * conv_in
    shifted = []
    for back in range(1, taps):
        moved = pltpu.roll(conv_in, back, 0) * aux[:, back : back + 1]
        shifted.append(moved)
        mixed = mixed + conv_w[taps - 1 - back : taps - back] * moved
    return mixed, shifted


def conv_back(d_mixed, conv_in, shifted, aux, conv_w):
    taps = conv_w.shape[0]
    rows = d_mixed.shape[0]
    d_in = conv_w[taps - 1 : taps] * d_mixed
    d_w = [None] * taps
    d_w[taps - 1] = jnp.sum(d_mixed * conv_in, axis=0, keepdims=True)
    for back in range(1, taps):
        ahead = pltpu.roll(d_mixed, rows - back, 0) * aux[:, taps - 1 + back : taps + back]
        d_in = d_in + conv_w[taps - 1 - back : taps - back] * ahead
        d_w[taps - 1 - back] = jnp.sum(d_mixed * shifted[back - 1], axis=0, keepdims=True)
    return d_in, d_w, jnp.sum(d_mixed, axis=0, keepdims=True)


def decays(last, dt_bias, neg_rate, aux, seg_row):
    rows = last.shape[0]
    step = softplus(last + dt_bias)
    row = lax.broadcasted_iota(jnp.int32, (rows, rows), 0)
    col = lax.broadcasted_iota(jnp.int32, (rows, rows), 1)
    lower = row >= col
    log_decay = dot_exact(lower.astype(F32), neg_rate * step)
    allowed = lower & (aux[:, 0:1] == seg_row)
    return step, log_decay, allowed, lower


def pair_masks(rows):
    lane = lax.broadcasted_iota(jnp.int32, (rows, LANES), 1)
    return (lane < HALF).astype(F32), (lane >= HALF).astype(F32)


def ahead_kernel(heads, proj, bc, aux, seg_row, conv_w, conv_b, dt_bias, neg_rate, skip, *rest):
    outs_ref, gated_ref, square_ref = rest[-3:]
    rows = proj.shape[0]
    inner = heads * HALF
    aux_v = aux[...]
    values_mixed, _ = conv_mixed(proj[:, inner : 2 * inner], aux_v, conv_w[:, :inner], conv_b[:, :inner])
    _, values = silu_parts(values_mixed)
    state_mixed, _ = conv_mixed(bc[...], aux_v, conv_w[:, inner:], conv_b[:, inner:])
    _, state = silu_parts(state_mixed)
    in_state, out_state = state[:, :LANES].astype(BF16), state[:, LANES:].astype(BF16)
    step, log_decay, allowed, _ = decays(
        proj[:, 2 * inner :], dt_bias[...], neg_rate[...], aux_v, seg_row[0]
    )
    step_t, log_t = step.T, log_decay.T
    inter = dot(out_state, in_state, ((1,), (1,)))
    first, second = pair_masks(rows)
    squares = jnp.zeros((rows, 1), F32)
    for pair in range(heads // 2):
        weights = []
        for h in (2 * pair, 2 * pair + 1):
            gap = log_decay[:, h : h + 1] - log_t[h : h + 1]
            decay = jnp.exp(jnp.where(allowed, gap, -1e30))
            weights.append((inter * decay * step_t[h : h + 1]).astype(BF16))
        at = slice(pair * LANES, (pair + 1) * LANES)
        own = values[:, at]
        low = own.astype(BF16).astype(F32)
        both = jnp.concatenate([low * first, low * second], axis=0).astype(BF16)
        carried = dot(jnp.concatenate(weights, axis=1), both)
        outs = carried + skip[:, at] * own
        _, gate = silu_parts(proj[:, at])
        gated = outs * gate
        outs_ref[:, at] = outs
        gated_ref[:, at] = gated
        squares = squares + jnp.sum(gated * gated, axis=1, keepdims=True)
    square_ref[...] = jnp.broadcast_to(squares, square_ref.shape)


def back_kernel(
    heads, proj, bc, aux, seg_row, conv_w, conv_b, dt_bias, neg_rate, skip, out_gain, outs, d_normed, scale, *rest
):
    d_main_ref, d_dt_ref, d_state_ref, d_wide_ref, d_narrow_ref = rest[-5:]
    rows = proj.shape[0]
    inner = heads * HALF
    aux_v = aux[...]
    values_in = proj[:, inner : 2 * inner]
    values_mixed, values_shifted = conv_mixed(values_in, aux_v, conv_w[:, :inner], conv_b[:, :inner])
    values_gate, values = silu_parts(values_mixed)
    state_mixed, _ = conv_mixed(bc[...], aux_v, conv_w[:, inner:], conv_b[:, inner:])
    _, state = silu_parts(state_mixed)
    in_state, out_state = state[:, :LANES].astype(BF16), state[:, LANES:].astype(BF16)
    last = proj[:, 2 * inner :]
    step, log_decay, allowed, lower = decays(last, dt_bias[...], neg_rate[...], aux_v, seg_row[0])
    step_t, log_t = step.T, log_decay.T
    inter = dot(out_state, in_state, ((1,), (1,)))
    first, second = pair_masks(rows)
    lane = lax.broadcasted_iota(jnp.int32, (rows, LANES), 1)
    sub = lax.broadcasted_iota(jnp.int32, (LANES, rows), 0)
    inverse, shrink = scale[:, 0:1], scale[:, 1:2]
    d_inter = jnp.zeros((rows, rows), F32)
    row_sums = jnp.zeros((rows, LANES), F32)
    col_sums = jnp.zeros((LANES, rows), F32)
    d_skip, d_gain, d_values = [], [], []
    for pair in range(heads // 2):
        at = slice(pair * LANES, (pair + 1) * LANES)
        own = values[:, at]
        low = own.astype(BF16)
        gate_in = proj[:, at]
        sig, gate = silu_parts(gate_in)
        outs_at = outs[:, at]
        gated = outs_at * gate
        dn = d_normed[:, at]
        d_gain.append(jnp.sum(gated * inverse * dn, axis=0, keepdims=True))
        d_gated = inverse * (out_gain[:, at] * dn) - gated * shrink
        d_outs = d_gated * gate
        d_main_ref[:, at] = (d_gated * outs_at * (sig * (1.0 + gate_in * (1.0 - sig)))).astype(BF16)
        d_skip.append(jnp.sum(d_outs * own, axis=0, keepdims=True))
        d_both = jnp.concatenate([d_outs * first, d_outs * second], axis=0).astype(BF16)
        d_weights = dot(d_both, low, ((1,), (1,)))
        weights = []
        for k, h in enumerate((2 * pair, 2 * pair + 1)):
            gap = log_decay[:, h : h + 1] - log_t[h : h + 1]
            decay = jnp.exp(jnp.where(allowed, gap, -1e30))
            step_row = step_t[h : h + 1]
            weights.append((inter * decay * step_row).astype(BF16))
            part = d_weights[k * rows : (k + 1) * rows] * decay
            d_inter = d_inter + part * step_row
            part = part * inter
            col = jnp.sum(part, axis=0, keepdims=True)
            col_sums = jnp.where(sub == h, col, col_sums)
            row_sum = jnp.sum(part * step_row, axis=1, keepdims=True)
            row_sums = jnp.where(lane == h, row_sum, row_sums)
        d_low = dot(jnp.concatenate(weights, axis=0), d_both, ((0,), (0,)))
        d_values.append(skip[:, at] * d_outs + d_low)
    d_values = jnp.concatenate(d_values, axis=1)
    d_mixed = d_values * (values_gate * (1.0 + values_mixed * (1.0 - values_gate)))
    d_in, d_w, d_b = conv_back(d_mixed, values_in, values_shifted, aux_v, conv_w[:, :inner])
    d_main_ref[:, inner : 2 * inner] = d_in.astype(BF16)
    low_inter = d_inter.astype(BF16)
    d_state_ref[:, :LANES] = dot(low_inter, out_state, ((0,), (0,)))
    d_state_ref[:, LANES:] = dot(low_inter, in_state)
    direct = col_sums.T
    d_log = row_sums - direct * step
    d_pace = dot_exact(lower.astype(F32), d_log, ((0,), (0,)))
    d_step = direct + d_pace * neg_rate[...]
    d_last = jnp.where(lane < heads, d_step * (1.0 / (1.0 + jnp.exp(-(last + dt_bias[...])))), 0.0)
    d_dt_ref[...] = d_last
    wide = d_w + [d_b, jnp.concatenate(d_skip, axis=1), jnp.concatenate(d_gain, axis=1)]
    wide.append(jnp.zeros((d_wide_ref.shape[1] - len(wide), inner), F32))
    d_wide_ref[0] = jnp.concatenate(wide, axis=0)
    d_rate = jnp.sum(d_pace * neg_rate[...] * step, axis=0, keepdims=True)
    narrow = [
        jnp.sum(d_last, axis=0, keepdims=True),
        jnp.where(lane[:1] < heads, d_rate, 0.0),
        jnp.zeros((d_narrow_ref.shape[1] - 2, LANES), F32),
    ]
    d_narrow_ref[0] = jnp.concatenate(narrow, axis=0)


def state_back_kernel(d_act, last, aux, conv_w, conv_b, d_dt, proj_ref, d_proj_ref, d_sums_ref):
    aux_v = aux[...]
    last_v = last[...]
    mixed, shifted = conv_mixed(last_v, aux_v, conv_w[...], conv_b[...])
    sig, _ = silu_parts(mixed)
    d_mixed = d_act[...] * (sig * (1.0 + mixed * (1.0 - sig)))
    d_in, d_w, d_b = conv_back(d_mixed, last_v, shifted, aux_v, conv_w[...])
    lane = lax.broadcasted_iota(jnp.int32, last_v.shape, 1)
    d_proj_ref[...] = jnp.where(lane < HALF, d_dt[...], d_in).astype(BF16)
    sums = d_w + [d_b]
    sums.append(jnp.zeros((d_sums_ref.shape[0] - len(sums), LANES), F32))
    d_sums_ref[...] = jnp.concatenate(sums, axis=0)


def rows_spec(rows, width, at):
    return pl.BlockSpec((rows, width), lambda i: (i + at, 0))


def whole_spec(shape):
    return pl.BlockSpec(shape, lambda i: (0,) * len(shape))


def ahead_call(heads, rows, at, count, proj, bc, aux, seg_rows, params, previous):
    conv_w, conv_b, dt_bias, neg_rate, skip = params
    total = proj.shape[0]
    inner = heads * HALF
    ins = [
        rows_spec(rows, proj.shape[1], at),
        rows_spec(rows, bc.shape[1], at),
        rows_spec(rows, aux.shape[1], at),
        pl.BlockSpec((1, 1, rows), lambda i: (i + at, 0, 0)),
    ] + [whole_spec(p.shape) for p in params]
    args = [proj, bc, aux, seg_rows, conv_w, conv_b, dt_bias, neg_rate, skip]
    aliases = {}
    if previous is not None:
        aliases = {len(args) + k: k for k in range(3)}
        ins += [pl.BlockSpec(memory_space=pl.ANY)] * 3
        args += list(previous)
    return pl.pallas_call(
        functools.partial(ahead_kernel, heads),
        grid=(count,),
        in_specs=ins,
        out_specs=[rows_spec(rows, inner, at), rows_spec(rows, inner, at), rows_spec(rows, LANES, at)],
        out_shape=[
            jax.ShapeDtypeStruct((total, inner), F32),
            jax.ShapeDtypeStruct((total, inner), F32),
            jax.ShapeDtypeStruct((total, LANES), F32),
        ],
        input_output_aliases=aliases,
        compiler_params=pltpu.CompilerParams(vmem_limit_bytes=VMEM_LIMIT),
        cost_estimate=pl.CostEstimate(
            flops=count * 2_000_000_000, bytes_accessed=count * 2_000_000, transcendentals=count * 400_000
        ),
    )(*args)


def back_call(heads, rows, at, count, proj, bc, aux, seg_rows, params, out_gain, outs, d_normed, scale, previous):
    total = proj.shape[0]
    inner = heads * HALF
    ins = [
        rows_spec(rows, proj.shape[1], at),
        rows_spec(rows, bc.shape[1], at),
        rows_spec(rows, aux.shape[1], at),
        pl.BlockSpec((1, 1, rows), lambda i: (i + at, 0, 0)),
    ] + [whole_spec(p.shape) for p in params]
    ins += [
        whole_spec(out_gain.shape),
        rows_spec(rows, inner, at),
        rows_spec(rows, inner, at),
        rows_spec(rows, scale.shape[1], at),
    ]
    args = [proj, bc, aux, seg_rows, *params, out_gain, outs, d_normed, scale]
    aliases = {}
    if previous is not None:
        aliases = {len(args) + k: k for k in range(5)}
        ins += [pl.BlockSpec(memory_space=pl.ANY)] * 5
        args += list(previous)
    blocks = total // rows
    return pl.pallas_call(
        functools.partial(back_kernel, heads),
        grid=(count,),
        in_specs=ins,
        out_specs=[
            rows_spec(rows, 2 * inner, at),
            rows_spec(rows, LANES, at),
            rows_spec(rows, bc.shape[1], at),
            pl.BlockSpec((1, 8, inner), lambda i: (i + at, 0, 0)),
            pl.BlockSpec((1, 8, LANES), lambda i: (i + at, 0, 0)),
        ],
        out_shape=[
            jax.ShapeDtypeStruct((total, 2 * inner + LANES), BF16),
            jax.ShapeDtypeStruct((total, LANES), F32),
            jax.ShapeDtypeStruct((total, bc.shape[1]), F32),
            jax.ShapeDtypeStruct((blocks, 8, inner), F32),
            jax.ShapeDtypeStruct((blocks, 8, LANES), F32),
        ],
        input_output_aliases=aliases,
        compiler_params=pltpu.CompilerParams(vmem_limit_bytes=VMEM_LIMIT),
        cost_estimate=pl.CostEstimate(
            flops=count * 4_000_000_000, bytes_accessed=count * 3_000_000, transcendentals=count * 600_000
        ),
    )(*args)


def state_back_call(d_act, proj, aux, conv_w, conv_b, d_dt, d_proj):
    total = proj.shape[0]
    column = proj.shape[1] // LANES - 1
    last_spec = pl.BlockSpec((total, LANES), lambda i: (0, column))
    return pl.pallas_call(
        state_back_kernel,
        grid=(1,),
        in_specs=[
            whole_spec(d_act.shape),
            last_spec,
            whole_spec(aux.shape),
            whole_spec(conv_w.shape),
            whole_spec(conv_b.shape),
            whole_spec(d_dt.shape),
            pl.BlockSpec(memory_space=pl.ANY),
        ],
        out_specs=[last_spec, whole_spec((8, LANES))],
        out_shape=[jax.ShapeDtypeStruct(d_proj.shape, BF16), jax.ShapeDtypeStruct((8, LANES), F32)],
        input_output_aliases={6: 0},
        compiler_params=pltpu.CompilerParams(vmem_limit_bytes=VMEM_LIMIT),
        cost_estimate=pl.CostEstimate(flops=1_000_000_000, bytes_accessed=1_500_000, transcendentals=70_000),
    )(d_act, proj, aux, conv_w, conv_b, d_dt, d_proj)


def make_aux(seg, rows, taps):
    blocks = seg.shape[0]
    columns = [seg.astype(F32)]
    for k in range(1, taps):
        before = jnp.pad(seg, ((0, 0), (k, 0)), constant_values=-1)[:, :rows]
        columns.append((before == seg).astype(F32))
    for k in range(1, taps):
        after = jnp.pad(seg, ((0, 0), (0, k)), constant_values=-1)[:, k:]
        columns.append((after == seg).astype(F32))
    columns += [jnp.zeros_like(columns[0])] * (8 - len(columns))
    return jnp.stack(columns, axis=-1).reshape(blocks * rows, 8)


def assemble_kernel(shard_rows, line, both, *refs):
    place_ref, sources, out, sems = refs[0], refs[1:-2], refs[-2], refs[-1]
    mine, side = place_ref[0], place_ref[1]

    def copies(run):
        count = 0
        for hop in range(-(line - 1), line):
            for other in range(2):
                source = sources[hop + line - 1] if both else sources[(hop + line - 1) * 2 + other]
                owner = mine + hop
                chunk = 2 * owner + (1 - side if other else side)
                chunk = jnp.clip(chunk, 0, 2 * line - 1)
                start = pl.multiple_of(chunk * shard_rows, 16)
                copy = pltpu.make_async_copy(
                    source.at[other] if both else source, out.at[pl.ds(start, shard_rows)], sems.at[count]
                )
                pl.when((owner >= 0) & (owner < line))(functools.partial(run, copy))
                count += 1

    copies(lambda copy: copy.start())
    copies(lambda copy: copy.wait())


def assemble(place, sources, shard_rows, line, both):
    width = sources[0].shape[-1]
    return pl.pallas_call(
        functools.partial(assemble_kernel, shard_rows, line, both),
        in_specs=[pl.BlockSpec(memory_space=pltpu.SMEM)] + [pl.BlockSpec(memory_space=pl.ANY)] * len(sources),
        out_specs=pl.BlockSpec(memory_space=pltpu.VMEM),
        out_shape=jax.ShapeDtypeStruct((2 * line * shard_rows, width), BF16),
        scratch_shapes=[pltpu.SemaphoreType.DMA((2 * (2 * line - 1),))],
        compiler_params=pltpu.CompilerParams(vmem_limit_bytes=VMEM_LIMIT),
        cost_estimate=pl.CostEstimate(
            flops=0, bytes_accessed=4 * line * shard_rows * width * 2, transcendentals=0
        ),
    )(place, *sources)


class Links:
    def __init__(self, mesh_shape):
        self.line = mesh_shape["fsdp"] // 2
        self.at = lax.axis_index("fsdp")
        self.place, self.side = self.at // 2, self.at % 2
        self.row, self.core = lax.axis_index("dp"), lax.axis_index("section")

    def swap_core(self, x):
        return lax.ppermute(x, "section", [(0, 1), (1, 0)])

    def swap_row(self, x):
        return lax.ppermute(x, "dp", [(0, 1), (1, 0)])

    def swap_side(self, x, places=None):
        places = range(self.line) if places is None else places
        return lax.ppermute(x, "fsdp", [(2 * p + s, 2 * p + 1 - s) for p in places for s in range(2)])

    def along(self, x, places, by):
        return lax.ppermute(x, "fsdp", [(2 * p + s, 2 * (p + by) + s) for p in places for s in range(2)])

    def mine_of_core(self, first, second):
        return jnp.where(self.core == 0, first, second)

    def in_row_order(self, own, other, axis):
        return jnp.where(
            self.row == 0, jnp.concatenate([own, other], axis), jnp.concatenate([other, own], axis)
        )

    def in_core_order(self, own, other, axis):
        return jnp.where(
            self.core == 0, jnp.concatenate([own, other], axis), jnp.concatenate([other, own], axis)
        )

    def cut(self, x, axis, which, parts=2):
        size = x.shape[axis] // parts
        return lax.dynamic_slice_in_dim(x, which * size, size, axis)

    def reached(self, hop):
        return [p for p in range(self.line) if 0 <= p + hop < self.line]

    def gather(self, piece, after=None):
        line = self.line
        if after is not None:
            piece, _ = lax.optimization_barrier((piece, after))
        got = {0: (piece, self.swap_side(piece))}
        up = down = piece
        marks = []
        for hop in range(1, line):
            up = self.along(up, [p for p in range(line - 1) if p >= hop - 1], 1)
            down = self.along(down, [p for p in range(1, line) if p <= line - hop], -1)
            marks.append(up)
            if 2 * hop >= line:
                either = jnp.where(self.place >= hop, up, down)
                crossed = self.swap_side(either, sorted(self.reached(-hop) + self.reached(hop)))
                got[-hop], got[hop] = (either, crossed), (either, crossed)
            else:
                got[-hop] = (up, self.swap_side(up, self.reached(-hop)))
                got[hop] = (down, self.swap_side(down, self.reached(hop)))
        sources = [got[hop][k] for hop in range(-(line - 1), line) for k in range(2)]
        where = jnp.stack([self.place, self.side])
        return assemble(where, sources, piece.shape[0], line, False), marks

    def gather_pairs(self, piece, after=None):
        line = self.line
        if after is not None:
            piece, _ = lax.optimization_barrier((piece, after))
        pair = jnp.stack([piece, self.swap_side(piece)])
        got = {0: pair}
        up = down = pair
        for hop in range(1, line):
            up = self.along(up, [p for p in range(line - 1) if p >= hop - 1], 1)
            down = self.along(down, [p for p in range(1, line) if p <= line - hop], -1)
            got[-hop], got[hop] = up, down
        sources = [got[hop] for hop in range(-(line - 1), line)]
        where = jnp.stack([self.place, self.side])
        return assemble(where, sources, piece.shape[0], line, True)

    def scatter(self, parts, after=None):
        line = self.line
        if after is not None:
            parts, _ = lax.optimization_barrier((parts, after))

        def part(place, other):
            index = 2 * place + (1 - self.side if other else self.side)
            return lax.dynamic_index_in_dim(parts, index, 0, keepdims=False)

        def joined(place, places):
            place = jnp.clip(place, 0, line - 1)
            return part(place, False).astype(F32) + self.swap_side(part(place, True), places).astype(F32)

        up = down = 0.0
        for hop in range(line - 1, 0, -1):
            if 2 * hop >= line:
                place = jnp.where(self.place >= hop, self.place - hop, self.place + hop)
                own_up = own_down = joined(place, sorted(self.reached(-hop) + self.reached(hop)))
            else:
                own_down = joined(self.place - hop, self.reached(-hop))
                own_up = joined(self.place + hop, self.reached(hop))
            down = self.along((own_down + down).astype(BF16), self.reached(-hop), -1).astype(F32)
            up = self.along((own_up + up).astype(BF16), self.reached(hop), 1).astype(F32)
        return joined(self.place, range(line)) + up + down

    def scatter_pairs(self, parts, after=None):
        line = self.line
        if after is not None:
            parts, _ = lax.optimization_barrier((parts, after))

        def pair(place):
            place = jnp.clip(place, 0, line - 1)
            return lax.dynamic_slice_in_dim(parts, 2 * place, 2, 0).astype(F32)

        up = down = 0.0
        for hop in range(line - 1, 0, -1):
            down = self.along((pair(self.place - hop) + down).astype(BF16), self.reached(-hop), -1).astype(F32)
            up = self.along((pair(self.place + hop) + up).astype(BF16), self.reached(hop), 1).astype(F32)
        total = pair(self.place) + up + down
        own = lax.dynamic_index_in_dim(total, self.side, 0, keepdims=False)
        sent = lax.dynamic_index_in_dim(total, 1 - self.side, 0, keepdims=False)
        return own + self.swap_side(sent.astype(BF16)).astype(F32)

    def sum_fsdp(self, x):
        x = x + self.swap_side(x)
        size = self.line
        if size & (size - 1):
            return lax.psum(x, "fsdp") / 2
        by = 1
        while by < size:
            pairs = [(2 * p + s, 2 * (p ^ by) + s) for p in range(size) for s in range(2)]
            x = x + lax.ppermute(x, "fsdp", pairs)
            by *= 2
        return x


def body(mesh_shape, inputs, seq_lengths, norm_gain, in_w, conv_w, conv_b, dt_bias, a_log, skip, out_gain, out_w, cotangent):
    links = Links(mesh_shape)
    core, row = links.core, links.row
    shards = mesh_shape["fsdp"]
    width = inputs.shape[1]
    half_width = width // 2
    own_tokens = inputs.shape[0]
    tokens = 2 * own_tokens
    rows = own_tokens // seq_lengths.shape[0]
    inner_all = out_gain.shape[1]
    heads_all = a_log.shape[1]
    head_dim = inner_all // heads_all
    taps, channels = conv_w.shape[1:]
    state_all = channels - inner_all
    state = state_all // 2
    heads = heads_all // 4
    inner = inner_all // 4
    shard_rows = in_w.shape[1]
    direct = (heads_all // shards) % 2 == 0 and heads_all % shards == 0
    groups = shards // 2 if direct else 1
    each = heads // groups
    span = each * head_dim

    def of_row(x, axis):
        return lax.index_in_dim(x, 0, axis, False), lax.index_in_dim(x, 1, axis, False)

    def pick_row(x, axis):
        first, second = of_row(x, axis)
        return jnp.where(row == 0, first, second)

    def wide_part(x, part):
        lead = x.shape[:-1]
        x = x.reshape(lead + (2, groups, 2, span))
        x = lax.index_in_dim(x, part, len(lead), False)
        return pick_row(x, len(lead) + 1).reshape(lead + (inner,))

    def head_part(x, part):
        lead = x.shape[:-1]
        x = x.reshape(lead + (2, groups, 2, each))
        x = lax.index_in_dim(x, part, len(lead), False)
        return pick_row(x, len(lead) + 1).reshape(lead + (heads,))

    def state_part(x, part):
        lead = x.shape[:-1]
        x = x.reshape(lead + (2, 2, state_all // 4))
        x = lax.index_in_dim(x, part, len(lead), False)
        return pick_row(x, len(lead))

    def columns_of(w, part):
        spare = jnp.zeros(w.shape[:-1] + (LANES - heads - state_all // 4,), w.dtype)
        return jnp.concatenate(
            [
                wide_part(w[:, :inner_all], part),
                wide_part(w[:, inner_all : 2 * inner_all], part),
                head_part(w[:, inner_all + channels :], part),
                spare,
                state_part(w[:, 2 * inner_all : inner_all + channels], part),
            ],
            axis=1,
        )

    def both_layers(own_part, other_part):
        came = links.swap_core(other_part)
        return links.mine_of_core(own_part, came), links.mine_of_core(came, own_part)

    in_first, in_second = columns_of(in_w[0], 0), columns_of(in_w[0], 1)
    in_pieces = both_layers(links.mine_of_core(in_first, in_second), links.mine_of_core(in_second, in_first))

    if direct:
        out_rows = pick_row(out_w[0].reshape(2, out_w.shape[1] // 2, width), 0)
    else:
        out_rows = out_w[0]
    out_first, out_second = out_rows[:, :half_width], out_rows[:, half_width:]
    out_pieces = both_layers(
        links.mine_of_core(out_first, out_second), links.mine_of_core(out_second, out_first)
    )

    def wide_row(x):
        return jnp.pad(x, ((0, 0), (0, channels - x.shape[1])))

    packed = jnp.concatenate(
        [conv_w[0], conv_b, wide_row(out_gain), wide_row(norm_gain), wide_row(dt_bias), wide_row(a_log), wide_row(skip)],
        axis=0,
    )
    packed_other = links.swap_core(packed)
    own_core_inner = lambda x: links.mine_of_core(wide_part(x, 0), wide_part(x, 1))
    own_core_heads = lambda x: links.mine_of_core(head_part(x, 0), head_part(x, 1))
    own_core_state = lambda x: links.mine_of_core(state_part(x, 0), state_part(x, 1))
    pad_lanes = lambda x: jnp.pad(x, ((0, 0), (0, LANES - x.shape[1])))

    def layer_params(pack):
        cw, cb = pack[:taps], pack[taps : taps + 1]
        og, ng = pack[taps + 1 : taps + 2, :inner_all], pack[taps + 2 : taps + 3, :width]
        dt, al, sk = (pack[taps + 3 + k : taps + 4 + k, :heads_all] for k in range(3))
        conv_full = jnp.concatenate([own_core_inner(cw[:, :inner_all]), cw[:, inner_all:]], axis=1)
        bias_full = jnp.concatenate([own_core_inner(cb[:, :inner_all]), cb[:, inner_all:]], axis=1)
        al = own_core_heads(al)
        lanes = (
            conv_full,
            bias_full,
            pad_lanes(own_core_heads(dt)),
            pad_lanes(-jnp.exp(al)),
            jnp.repeat(own_core_heads(sk), head_dim, axis=1),
        )
        front = lambda x: jnp.pad(x, ((0, 0), (LANES - x.shape[1], 0)))
        return {
            "lanes": lanes,
            "out_gain": own_core_inner(og),
            "norm_gain": ng,
            "state_w": front(own_core_state(cw[:, inner_all:])),
            "state_b": front(own_core_state(cb[:, inner_all:])),
        }

    params = (
        layer_params(links.mine_of_core(packed, packed_other)),
        layer_params(links.mine_of_core(packed_other, packed)),
    )

    all_tokens = links.in_row_order(inputs, links.swap_row(inputs), 0)
    all_lengths = links.in_row_order(seq_lengths, links.swap_row(seq_lengths), 0)
    ends = jnp.cumsum(all_lengths, axis=1)
    positions = jnp.arange(rows, dtype=jnp.int32)
    segments = jnp.sum((positions[None, :, None] >= ends[:, None, :]).astype(jnp.int32), axis=2)
    aux = make_aux(segments, rows, taps)
    seg_rows = segments.astype(F32)[:, None, :]
    blocks = tokens // rows
    per_call = 2 if blocks % 2 == 0 else 1

    def out_whole(pieces):
        kept = links.cut(pieces, 0, core)
        came = links.swap_core(links.cut(pieces, 0, 1 - core))
        return links.in_core_order(kept, came, 1)

    def gather_out(piece, pairs, after):
        if direct:
            full = links.gather_pairs(piece, after) if pairs else links.gather(piece, after)[0]
        else:
            full = lax.all_gather(piece, "fsdp", axis=0, tiled=True)
            full = pick_row(full.reshape(2, 2, inner, half_width), 1).reshape(2 * inner, half_width)
        return out_whole(full)

    in_weight, out_weight = [None, None], [None, None]
    in_weight[0], marks = links.gather(in_pieces[0])
    out_weight[0] = gather_out(out_pieces[0], False, marks[0])
    in_weight[1], marks = links.gather(in_pieces[1], marks[-1])
    out_weight[1] = gather_out(out_pieces[1], True, marks[-1])

    def to_rows(x):
        return x.reshape(-1, LANES)

    def total_of(x):
        x = to_rows(x)
        x = x + links.swap_core(x)
        x = x + links.swap_row(x)
        return x.reshape(-1)

    def norm_of(u):
        return lax.rsqrt(jnp.mean(u * u, axis=-1, keepdims=True) + 1e-05)

    def ahead(layer, u):
        own = params[layer]
        u = u.astype(F32)
        scaled = (u * norm_of(u) * own["norm_gain"]).astype(BF16)
        proj = dot(scaled, in_weight[layer])
        part = proj[:, 2 * inner + LANES - state_all // 4 :]
        part = links.in_row_order(part, links.swap_row(part), 1)
        bc = links.in_core_order(part, links.swap_core(part), 1)
        done = None
        for at in range(0, blocks, per_call):
            done = ahead_call(heads, rows, at, per_call, proj, bc, aux, seg_rows, own["lanes"], done)
        outs, gated, squares = done
        inverse = lax.rsqrt(total_of(squares[:, 0]) / inner_all + 1e-05)[:, None]
        normed = (gated * inverse * own["out_gain"]).astype(BF16)
        return {"scaled": scaled, "proj": proj, "bc": bc, "outs": outs, "gated": gated, "inverse": inverse, "normed": normed}

    def over_cores(x):
        kept = links.cut(x, 1, core)
        return kept + links.swap_core(links.cut(x, 1, 1 - core))

    def over_rows(x):
        x = x.astype(BF16)
        return x.astype(F32) + links.swap_row(x).astype(F32)

    def over_rows_own(x):
        kept = links.cut(x, 0, row)
        return kept + links.swap_row(links.cut(x, 0, 1 - row).astype(BF16)).astype(F32)

    def own_rows(x):
        return links.cut(x, 0, row)

    saved = [None, None]
    saved[0] = ahead(0, all_tokens)
    branch = over_rows(over_cores(dot(saved[0]["normed"], out_weight[0])))
    first = (links.cut(all_tokens, 1, core).astype(F32) + branch).astype(BF16)
    first = links.in_core_order(first, links.swap_core(first), 1)
    saved[1] = ahead(1, first)
    last_partial = dot(saved[1]["normed"], out_weight[1])
    branch = over_rows_own(over_cores(last_partial))
    second = (links.cut(own_rows(first), 1, core).astype(F32) + branch).astype(BF16)
    second = links.in_core_order(second, links.swap_core(second), 1)
    phase_out = jnp.where(core == 0, own_rows(first), second)[None]

    def out_parts(d_out):
        kept = links.cut(d_out, 1, core)
        came = links.swap_core(links.cut(d_out, 1, 1 - core))
        return links.in_core_order(kept, came, 0)

    def scatter_out(d_out, pairs, after=None):
        parts = out_parts(d_out)
        if direct:
            parts = parts.reshape(shards, -1, half_width)
            return links.scatter_pairs(parts, after) if pairs else links.scatter(parts, after)
        parts = parts.reshape(2, 1, inner, half_width)
        empty = jnp.zeros_like(parts)
        parts = links.in_row_order(parts, empty, 1).reshape(4 * inner, half_width)
        mine = lax.psum_scatter(parts, "fsdp", scatter_dimension=0, tiled=True)
        return mine.astype(F32) + links.swap_row(mine).astype(F32)

    def back(layer, grad):
        own, kept = params[layer], saved[layer]
        d_out = dot(kept["normed"], grad, ((0,), (0,))).astype(BF16)
        d_normed = dot(grad, out_weight[layer], ((1,), (1,)))
        meet = total_of(jnp.sum(kept["gated"] * own["out_gain"] * d_normed, axis=1))[:, None]
        inverse = kept["inverse"]
        scale = jnp.concatenate(
            [inverse, inverse * inverse * inverse * meet / inner_all, jnp.zeros((tokens, 6), F32)], axis=1
        )
        done = None
        for at in range(0, blocks, per_call):
            done = back_call(
                heads, rows, at, per_call, kept["proj"], kept["bc"], aux, seg_rows, own["lanes"],
                own["out_gain"], kept["outs"], d_normed, scale, done,
            )
        d_proj, d_dt, d_bc, d_wide, d_narrow = done
        d_bc = over_cores(d_bc)
        d_bc = links.cut(d_bc, 1, row) + links.swap_row(links.cut(d_bc, 1, 1 - row))
        d_bc = jnp.pad(d_bc, ((0, 0), (LANES - d_bc.shape[1], 0)))
        d_proj, d_state = state_back_call(d_bc, kept["proj"], aux, own["state_w"], own["state_b"], d_dt, d_proj)
        d_in = dot(kept["scaled"], d_proj, ((0,), (0,))).astype(BF16).reshape(shards, shard_rows, -1)
        d_scaled = over_cores(dot(d_proj, in_weight[layer], ((1,), (1,))))
        return d_out, d_in, d_scaled, jnp.sum(d_wide, axis=0), jnp.sum(d_narrow, axis=0), d_state

    def norm_back(layer, u, d_scaled):
        u = u.astype(F32)
        inverse = norm_of(u)
        gain = params[layer]["norm_gain"]
        meet = jnp.mean(u * gain * d_scaled, axis=1, keepdims=True)
        return inverse * gain * d_scaled - u * (inverse * inverse * inverse * meet)

    def gain_back(u, d_scaled):
        u = u.astype(F32)
        return jnp.sum(u * norm_of(u) * d_scaled, axis=0, keepdims=True)

    all_cot = links.in_row_order(cotangent, links.swap_row(cotangent), 0)
    d_out, d_in, d_scaled, wide1, narrow1, state1 = back(1, all_cot)
    sums_out1 = scatter_out(d_out, True)
    sums_in1 = links.scatter(d_in)
    d_scaled = over_rows(d_scaled)
    d_scaled = links.in_core_order(d_scaled, links.swap_core(d_scaled), 1)
    grad = (all_cot.astype(F32) + norm_back(1, first, d_scaled)).astype(BF16)
    gain1 = gain_back(own_rows(first), own_rows(d_scaled))

    d_out, d_in, d_scaled, wide0, narrow0, state0 = back(0, grad)
    sums_out0 = scatter_out(d_out, False)
    sums_in0 = links.scatter(d_in)
    d_scaled = over_rows_own(d_scaled)
    d_scaled = links.in_core_order(d_scaled, links.swap_core(d_scaled), 1)
    own_grad = own_rows(grad)
    grad_in = (own_grad.astype(F32) + norm_back(0, inputs, d_scaled)).astype(BF16)
    gain0 = gain_back(inputs, d_scaled)
    input_grad = jnp.where(core == 0, grad_in, own_grad)[None]

    def pack_small(wide, narrow, gain, d_state):
        gain = gain.reshape(-1, inner)
        narrow_rows = jnp.concatenate([narrow[:2], d_state[: taps + 1]], axis=0)
        narrow_rows = jnp.pad(narrow_rows.reshape(1, -1), ((0, 0), (0, 2 * inner - narrow_rows.size)))
        return jnp.concatenate([wide[: taps + 3], gain, narrow_rows.reshape(2, inner)], axis=0)

    gain_rows = width // inner
    small = jnp.concatenate([pack_small(wide0, narrow0, gain0, state0), pack_small(wide1, narrow1, gain1, state1)], axis=0)
    small = links.sum_fsdp(small)
    per = small.shape[0] // 2
    small_other = links.swap_row(small)
    mine = links.mine_of_core(small[:per], small[per:])
    mine_other = links.mine_of_core(small_other[:per], small_other[per:])
    theirs = links.mine_of_core(small[per:], small[:per])
    theirs_other = links.mine_of_core(small_other[per:], small_other[:per])
    came = links.swap_core(jnp.stack([theirs, theirs_other]))
    by_row = lambda a, b: jnp.where(row == 0, jnp.stack([a, b]), jnp.stack([b, a]))
    own_parts, came_parts = by_row(mine, mine_other), by_row(came[0], came[1])
    quarters = jnp.where(core == 0, jnp.stack([own_parts, came_parts]), jnp.stack([came_parts, own_parts]))

    def spread_wide(x):
        lead = x.shape[2:-1]
        x = x.reshape((2, 2) + lead + (groups, span))
        x = jnp.moveaxis(x, (0, 1), (len(lead), len(lead) + 2))
        return x.reshape(lead + (inner_all,))

    def spread_heads(x):
        x = x.reshape((2, 2, groups, each))
        return jnp.moveaxis(x, 1, 2).reshape(1, heads_all)

    wide = quarters[:, :, : taps + 3]
    grad_norm = mine[taps + 3 : taps + 3 + gain_rows] + mine_other[taps + 3 : taps + 3 + gain_rows]
    grad_norm = grad_norm.reshape(1, width)
    narrow = quarters[:, :, taps + 3 + gain_rows :].reshape(2, 2, -1)
    narrow = narrow[:, :, : (taps + 3) * LANES].reshape(2, 2, taps + 3, LANES)
    states = narrow[:, :, 2:, LANES - state_all // 4 :]
    states = jnp.moveaxis(states, 2, 0).reshape(taps + 1, state_all)
    wide_full = spread_wide(wide)
    grad_conv_w = jnp.concatenate([wide_full[:taps], states[:taps]], axis=1)[None]
    grad_conv_b = jnp.concatenate([wide_full[taps : taps + 1], states[taps:]], axis=1)
    grad_skip = wide_full[taps + 1].reshape(1, heads_all, head_dim).sum(axis=-1)
    grad_out_gain = wide_full[taps + 2 : taps + 3]
    grad_dt = spread_heads(narrow[:, :, 0, :heads])
    grad_a = spread_heads(narrow[:, :, 1, :heads])

    def own_layer(x0, x1):
        low0, low1 = x0.astype(BF16), x1.astype(BF16)
        far0, far1 = links.swap_row(low0), links.swap_row(low1)
        mine, far = links.mine_of_core(low0, low1), links.mine_of_core(far0, far1)
        came = links.swap_core(jnp.stack([links.mine_of_core(low1, low0), links.mine_of_core(far1, far0)]))
        own_rows_, came_rows = by_row(mine, far), by_row(came[0], came[1])
        return jnp.where(core == 0, jnp.stack([own_rows_, came_rows]), jnp.stack([came_rows, own_rows_]))

    whole_in = own_layer(sums_in0, sums_in1).astype(F32)

    def spread_columns(x):
        x = x.reshape(2, 2, shard_rows, groups, span)
        return x.transpose(2, 0, 3, 1, 4).reshape(shard_rows, inner_all)

    tail = whole_in[..., 2 * inner :]
    grad_in_w = jnp.concatenate(
        [
            spread_columns(whole_in[..., :inner]),
            spread_columns(whole_in[..., inner : 2 * inner]),
            tail[..., LANES - state_all // 4 :].transpose(2, 0, 1, 3).reshape(shard_rows, state_all),
            tail[..., :heads].reshape(2, 2, shard_rows, groups, each).transpose(2, 0, 3, 1, 4).reshape(shard_rows, heads_all),
        ],
        axis=1,
    )[None]
    if direct:
        whole_out = own_layer(sums_out0, sums_out1).astype(F32)
        grad_out_w = whole_out.transpose(1, 2, 0, 3).reshape(1, out_w.shape[1], width)
    else:
        came = links.swap_core(links.mine_of_core(sums_out1, sums_out0).astype(BF16)).astype(F32)
        grad_out_w = links.in_core_order(links.mine_of_core(sums_out0, sums_out1), came, 1)[None]

    return (
        phase_out, input_grad, grad_norm, grad_in_w, grad_conv_w, grad_conv_b,
        grad_dt, grad_a, grad_skip, grad_out_gain, grad_out_w,
    )


def solution(mesh):
    return jax.shard_map(
        functools.partial(body, dict(mesh.shape)),
        mesh=mesh,
        in_specs=(
            P(("fsdp", "dp"), None),
            P(("fsdp", "dp"), None),
            P("section", None),
            P("section", "fsdp", None),
            P("section", None, None),
            P("section", None),
            P("section", None),
            P("section", None),
            P("section", None),
            P("section", None),
            P("section", "fsdp", None),
            P(("fsdp", "dp"), None),
        ),
        out_specs=(
            P("section", ("fsdp", "dp"), None),
            P("section", ("fsdp", "dp"), None),
            P("section", None),
            P("section", "fsdp", None),
            P("section", None, None),
            P("section", None),
            P("section", None),
            P("section", None),
            P("section", None),
            P("section", None),
            P("section", "fsdp", None),
        ),
        check_vma=False,
    )
```

```python
import functools

import jax
import jax.numpy as jnp
from jax import lax
from jax.experimental import pallas as pl
from jax.experimental.pallas import tpu as pltpu
from jax.sharding import PartitionSpec as P

F32 = jnp.float32
BF16 = jnp.bfloat16
LANES = 128
HALF = 64
VMEM_LIMIT = 40 * 1024 * 1024
VMEM_ALL = 60 * 1024 * 1024


def dot(a, b, dims=((1,), (0,)), precision=None):
    return lax.dot_general(a, b, (dims, ((), ())), precision=precision, preferred_element_type=F32)


def dot_exact(a, b, dims=((1,), (0,))):
    return dot(a, b, dims, lax.Precision.HIGHEST)


def silu_parts(x):
    gate = 1.0 / (1.0 + jnp.exp(-x))
    return gate, x * gate


def softplus(x):
    return jnp.maximum(x, 0.0) + jnp.log1p(jnp.exp(-jnp.abs(x)))


def conv_mixed(conv_in, aux, conv_w, conv_b):
    taps = conv_w.shape[0]
    mixed = conv_b + conv_w[taps - 1 : taps] * conv_in
    shifted = []
    for back in range(1, taps):
        moved = pltpu.roll(conv_in, back, 0) * aux[:, back : back + 1]
        shifted.append(moved)
        mixed = mixed + conv_w[taps - 1 - back : taps - back] * moved
    return mixed, shifted


def conv_back(d_mixed, conv_in, shifted, aux, conv_w):
    taps = conv_w.shape[0]
    rows = d_mixed.shape[0]
    d_in = conv_w[taps - 1 : taps] * d_mixed
    d_w = [None] * taps
    d_w[taps - 1] = jnp.sum(d_mixed * conv_in, axis=0, keepdims=True)
    for back in range(1, taps):
        ahead = pltpu.roll(d_mixed, rows - back, 0) * aux[:, taps - 1 + back : taps + back]
        d_in = d_in + conv_w[taps - 1 - back : taps - back] * ahead
        d_w[taps - 1 - back] = jnp.sum(d_mixed * shifted[back - 1], axis=0, keepdims=True)
    return d_in, d_w, jnp.sum(d_mixed, axis=0, keepdims=True)


def decays(last, dt_bias, neg_rate, aux, seg_row):
    rows = last.shape[0]
    step = softplus(last + dt_bias)
    row = lax.broadcasted_iota(jnp.int32, (rows, rows), 0)
    col = lax.broadcasted_iota(jnp.int32, (rows, rows), 1)
    lower = row >= col
    log_decay = dot_exact(lower.astype(F32), neg_rate * step)
    allowed = lower & (aux[:, 0:1] == seg_row)
    return step, log_decay, allowed, lower


def pair_masks(rows):
    lane = lax.broadcasted_iota(jnp.int32, (rows, LANES), 1)
    return (lane < HALF).astype(F32), (lane >= HALF).astype(F32)


def unpack(packed, taps, heads):
    inner = heads * HALF
    conv_w, conv_b = packed[:taps, :], packed[taps : taps + 1, :]
    out_gain, skip = packed[taps + 1 : taps + 2, :inner], packed[taps + 2 : taps + 3, :inner]
    dt_bias, neg_rate = packed[taps + 3 : taps + 4, :LANES], packed[taps + 3 : taps + 4, LANES : 2 * LANES]
    return conv_w, conv_b, dt_bias, neg_rate, skip, out_gain


def ahead_kernel(heads, taps, proj, last, bc, aux, seg_row, packed, outs_ref, gated_ref, square_ref):
    rows = proj.shape[0]
    conv_w, conv_b, dt_bias, neg_rate, skip, _ = unpack(packed, taps, heads)
    inner = heads * HALF
    aux_v = aux[...]
    values_mixed, _ = conv_mixed(proj[:, inner : 2 * inner], aux_v, conv_w[:, :inner], conv_b[:, :inner])
    _, values = silu_parts(values_mixed)
    state_mixed, _ = conv_mixed(bc[...], aux_v, conv_w[:, inner:], conv_b[:, inner:])
    _, state = silu_parts(state_mixed)
    in_state, out_state = state[:, :LANES].astype(BF16), state[:, LANES:].astype(BF16)
    step, log_decay, allowed, _ = decays(
        last[...], dt_bias, neg_rate, aux_v, seg_row[0]
    )
    step_t, log_t = step.T, log_decay.T
    inter = dot(out_state, in_state, ((1,), (1,)))
    first, second = pair_masks(rows)
    squares = jnp.zeros((rows, 1), F32)
    for pair in range(heads // 2):
        weights = []
        for h in (2 * pair, 2 * pair + 1):
            gap = log_decay[:, h : h + 1] - log_t[h : h + 1]
            decay = jnp.exp(jnp.where(allowed, gap, -1e30))
            weights.append((inter * decay * step_t[h : h + 1]).astype(BF16))
        at = slice(pair * LANES, (pair + 1) * LANES)
        own = values[:, at]
        low = own.astype(BF16).astype(F32)
        both = jnp.concatenate([low * first, low * second], axis=0).astype(BF16)
        carried = dot(jnp.concatenate(weights, axis=1), both)
        outs = carried + skip[:, at] * own
        _, gate = silu_parts(proj[:, at])
        gated = outs * gate
        outs_ref[:, at] = outs
        gated_ref[:, at] = gated
        squares = squares + jnp.sum(gated * gated, axis=1, keepdims=True)
    square_ref[...] = jnp.broadcast_to(squares, square_ref.shape)


def back_kernel(
    heads, taps, proj, last_ref, bc, aux, seg_row, packed, outs, d_normed, inverse_ref, shrink_ref, *results
):
    d_main_ref, d_dt_ref, d_state_ref, d_wide_ref, d_narrow_ref = results
    rows = proj.shape[0]
    conv_w, conv_b, dt_bias, neg_rate, skip, out_gain = unpack(packed, taps, heads)
    inner = heads * HALF
    aux_v = aux[...]
    values_in = proj[:, inner : 2 * inner]
    values_mixed, values_shifted = conv_mixed(values_in, aux_v, conv_w[:, :inner], conv_b[:, :inner])
    values_gate, values = silu_parts(values_mixed)
    state_mixed, _ = conv_mixed(bc[...], aux_v, conv_w[:, inner:], conv_b[:, inner:])
    _, state = silu_parts(state_mixed)
    in_state, out_state = state[:, :LANES].astype(BF16), state[:, LANES:].astype(BF16)
    last = last_ref[...]
    step, log_decay, allowed, lower = decays(last, dt_bias, neg_rate, aux_v, seg_row[0])
    step_t, log_t = step.T, log_decay.T
    inter = dot(out_state, in_state, ((1,), (1,)))
    first, second = pair_masks(rows)
    lane = lax.broadcasted_iota(jnp.int32, (rows, LANES), 1)
    sub = lax.broadcasted_iota(jnp.int32, (LANES, rows), 0)
    inverse, shrink = inverse_ref[...], shrink_ref[...]
    d_inter = jnp.zeros((rows, rows), F32)
    row_sums = jnp.zeros((rows, LANES), F32)
    col_sums = jnp.zeros((LANES, rows), F32)
    d_skip, d_gain, d_values = [], [], []
    for pair in range(heads // 2):
        at = slice(pair * LANES, (pair + 1) * LANES)
        own = values[:, at]
        low = own.astype(BF16)
        gate_in = proj[:, at]
        sig, gate = silu_parts(gate_in)
        outs_at = outs[:, at]
        gated = outs_at * gate
        dn = d_normed[:, at]
        d_gain.append(jnp.sum(gated * inverse * dn, axis=0, keepdims=True))
        d_gated = inverse * (out_gain[:, at] * dn) - gated * shrink
        d_outs = d_gated * gate
        d_main_ref[:, at] = (d_gated * outs_at * (sig * (1.0 + gate_in * (1.0 - sig)))).astype(BF16)
        d_skip.append(jnp.sum(d_outs * own, axis=0, keepdims=True))
        d_both = jnp.concatenate([d_outs * first, d_outs * second], axis=0).astype(BF16)
        d_weights = dot(d_both, low, ((1,), (1,)))
        weights = []
        for k, h in enumerate((2 * pair, 2 * pair + 1)):
            gap = log_decay[:, h : h + 1] - log_t[h : h + 1]
            decay = jnp.exp(jnp.where(allowed, gap, -1e30))
            step_row = step_t[h : h + 1]
            weights.append((inter * decay * step_row).astype(BF16))
            part = d_weights[k * rows : (k + 1) * rows] * decay
            d_inter = d_inter + part * step_row
            part = part * inter
            col = jnp.sum(part, axis=0, keepdims=True)
            col_sums = jnp.where(sub == h, col, col_sums)
            row_sum = jnp.sum(part * step_row, axis=1, keepdims=True)
            row_sums = jnp.where(lane == h, row_sum, row_sums)
        d_low = dot(jnp.concatenate(weights, axis=0), d_both, ((0,), (0,)))
        d_values.append(skip[:, at] * d_outs + d_low)
    d_values = jnp.concatenate(d_values, axis=1)
    d_mixed = d_values * (values_gate * (1.0 + values_mixed * (1.0 - values_gate)))
    d_in, d_w, d_b = conv_back(d_mixed, values_in, values_shifted, aux_v, conv_w[:, :inner])
    d_main_ref[:, inner : 2 * inner] = d_in.astype(BF16)
    low_inter = d_inter.astype(BF16)
    d_state_ref[:, :LANES] = dot(low_inter, out_state, ((0,), (0,)))
    d_state_ref[:, LANES:] = dot(low_inter, in_state)
    direct = col_sums.T
    d_log = row_sums - direct * step
    d_pace = dot_exact(lower.astype(F32), d_log, ((0,), (0,)))
    d_step = direct + d_pace * neg_rate
    d_last = jnp.where(lane < heads, d_step * (1.0 / (1.0 + jnp.exp(-(last + dt_bias)))), 0.0)
    d_dt_ref[...] = d_last
    wide = d_w + [d_b, jnp.concatenate(d_skip, axis=1), jnp.concatenate(d_gain, axis=1)]
    wide.append(jnp.zeros((d_wide_ref.shape[1] - len(wide), inner), F32))
    d_wide_ref[0] = jnp.concatenate(wide, axis=0)
    d_rate = jnp.sum(d_pace * neg_rate * step, axis=0, keepdims=True)
    narrow = [
        jnp.sum(d_last, axis=0, keepdims=True),
        jnp.where(lane[:1] < heads, d_rate, 0.0),
        jnp.zeros((d_narrow_ref.shape[1] - 2, LANES), F32),
    ]
    d_narrow_ref[0] = jnp.concatenate(narrow, axis=0)


def state_back_kernel(taps, d_act, last, aux, packed, d_dt, d_proj_ref, d_sums_ref):
    aux_v = aux[...]
    last_v = last[...]
    conv_w, conv_b = packed[8 : 8 + taps, :LANES], packed[8 + taps : 9 + taps, :LANES]
    mixed, shifted = conv_mixed(last_v, aux_v, conv_w, conv_b)
    sig, _ = silu_parts(mixed)
    d_mixed = d_act[...] * (sig * (1.0 + mixed * (1.0 - sig)))
    d_in, d_w, d_b = conv_back(d_mixed, last_v, shifted, aux_v, conv_w)
    lane = lax.broadcasted_iota(jnp.int32, last_v.shape, 1)
    d_proj_ref[...] = jnp.where(lane < HALF, d_dt[...], d_in).astype(BF16)
    sums = d_w + [d_b]
    sums.append(jnp.zeros((d_sums_ref.shape[0] - len(sums), LANES), F32))
    d_sums_ref[...] = jnp.concatenate(sums, axis=0)


def rows_spec(rows, width):
    return pl.BlockSpec((rows, width), lambda i: (i, 0))


def whole_spec(shape):
    return pl.BlockSpec(shape, lambda i: (0,) * len(shape))


def ahead_call(heads, taps, rows, proj, last, bc, aux, seg_rows, packed):
    total = proj.shape[0]
    inner = heads * HALF
    count = total // rows
    return pl.pallas_call(
        functools.partial(ahead_kernel, heads, taps),
        grid=(count,),
        in_specs=[
            rows_spec(rows, proj.shape[1]),
            rows_spec(rows, LANES),
            rows_spec(rows, bc.shape[1]),
            rows_spec(rows, aux.shape[1]),
            pl.BlockSpec((1, 1, rows), lambda i: (i, 0, 0)),
            whole_spec(packed.shape),
        ],
        out_specs=[rows_spec(rows, inner), rows_spec(rows, inner), rows_spec(rows, LANES)],
        out_shape=[
            jax.ShapeDtypeStruct((total, inner), F32),
            jax.ShapeDtypeStruct((total, inner), F32),
            jax.ShapeDtypeStruct((total, LANES), F32),
        ],
        compiler_params=pltpu.CompilerParams(vmem_limit_bytes=VMEM_LIMIT),
        cost_estimate=pl.CostEstimate(
            flops=count * 1_000_000_000, bytes_accessed=count * 2_000_000, transcendentals=count * 400_000
        ),
    )(proj, last, bc, aux, seg_rows, packed)


def back_call(heads, taps, rows, proj, last, bc, aux, seg_rows, packed, outs, d_normed, inverse, shrink):
    total = proj.shape[0]
    inner = heads * HALF
    count = total // rows
    return pl.pallas_call(
        functools.partial(back_kernel, heads, taps),
        grid=(count,),
        in_specs=[
            rows_spec(rows, proj.shape[1]),
            rows_spec(rows, LANES),
            rows_spec(rows, bc.shape[1]),
            rows_spec(rows, aux.shape[1]),
            pl.BlockSpec((1, 1, rows), lambda i: (i, 0, 0)),
            whole_spec(packed.shape),
            rows_spec(rows, inner),
            rows_spec(rows, inner),
            rows_spec(rows, 1),
            rows_spec(rows, 1),
        ],
        out_specs=[
            rows_spec(rows, 2 * inner),
            rows_spec(rows, LANES),
            rows_spec(rows, bc.shape[1]),
            pl.BlockSpec((1, 8, inner), lambda i: (i, 0, 0)),
            pl.BlockSpec((1, 8, LANES), lambda i: (i, 0, 0)),
        ],
        out_shape=[
            jax.ShapeDtypeStruct((total, 2 * inner), BF16),
            jax.ShapeDtypeStruct((total, LANES), F32),
            jax.ShapeDtypeStruct((total, bc.shape[1]), F32),
            jax.ShapeDtypeStruct((count, 8, inner), F32),
            jax.ShapeDtypeStruct((count, 8, LANES), F32),
        ],
        compiler_params=pltpu.CompilerParams(vmem_limit_bytes=VMEM_LIMIT),
        cost_estimate=pl.CostEstimate(
            flops=count * 2_000_000_000, bytes_accessed=count * 3_000_000, transcendentals=count * 600_000
        ),
    )(proj, last, bc, aux, seg_rows, packed, outs, d_normed, inverse, shrink)


def state_back_call(taps, d_act, last, aux, packed, d_dt):
    args = (d_act, last, aux, packed, d_dt)
    return pl.pallas_call(
        functools.partial(state_back_kernel, taps),
        grid=(1,),
        in_specs=[whole_spec(x.shape) for x in args],
        out_specs=[whole_spec(last.shape), whole_spec((8, LANES))],
        out_shape=[jax.ShapeDtypeStruct(last.shape, BF16), jax.ShapeDtypeStruct((8, LANES), F32)],
        compiler_params=pltpu.CompilerParams(vmem_limit_bytes=VMEM_LIMIT),
        cost_estimate=pl.CostEstimate(flops=100_000_000, bytes_accessed=1_500_000, transcendentals=70_000),
    )(*args)


def make_aux(seg, rows, taps):
    blocks = seg.shape[0]
    columns = [seg.astype(F32)]
    for k in range(1, taps):
        before = jnp.pad(seg, ((0, 0), (k, 0)), constant_values=-1)[:, :rows]
        columns.append((before == seg).astype(F32))
    for k in range(1, taps):
        after = jnp.pad(seg, ((0, 0), (0, k)), constant_values=-1)[:, k:]
        columns.append((after == seg).astype(F32))
    columns += [jnp.zeros_like(columns[0])] * (8 - len(columns))
    return jnp.stack(columns, axis=-1).reshape(blocks * rows, 8)


def ring_owner(at, line):
    at = lax.rem(at + 2 * line, 2 * line)
    return jnp.where(at < line, 2 * at, 4 * line - 2 * at - 1)


def assemble_kernel(cuts, starts, *refs):
    outs, sems = refs[-1 - len(cuts) : -1], refs[-1]
    sources = refs[: -1 - len(cuts)]

    def copies(run):
        for k, source in enumerate(sources):
            start = pl.multiple_of(starts[k], 16)
            for n, (low, high) in enumerate(cuts):
                run(
                    pltpu.make_async_copy(
                        source.at[:, low:high],
                        outs[n].at[pl.ds(start, source.shape[0])],
                        sems.at[k * len(cuts) + n],
                    )
                )

    copies(lambda copy: copy.start())
    copies(lambda copy: copy.wait())


def assemble(starts, sources, cuts):
    total = sum(x.shape[0] for x in sources)
    return pl.pallas_call(
        functools.partial(assemble_kernel, cuts),
        in_specs=[pl.BlockSpec(memory_space=pltpu.SMEM)] + [pl.BlockSpec(memory_space=pl.ANY)] * len(sources),
        out_specs=[pl.BlockSpec(memory_space=pltpu.VMEM)] * len(cuts),
        out_shape=[jax.ShapeDtypeStruct((total, high - low), BF16) for low, high in cuts],
        scratch_shapes=[pltpu.SemaphoreType.DMA((len(sources) * len(cuts),))],
        compiler_params=pltpu.CompilerParams(vmem_limit_bytes=VMEM_ALL),
        cost_estimate=pl.CostEstimate(
            flops=0, bytes_accessed=4 * total * sources[0].shape[1], transcendentals=0
        ),
    )(jnp.stack(starts).astype(jnp.int32), *sources)


def quarter_kernel(sizes, where, in_w, out_w, own_ref, other_ref):
    inner_all, state_all, groups, each, heads_all = sizes
    span = each * HALF
    inner = inner_all // 4
    row, core = where[2], where[3]
    tail = in_w[:, 2 * inner_all :]
    spare, depth = LANES - state_all // 4, tail.shape[1]
    for part, ref in ((core, own_ref), (1 - core, other_ref)):
        for base in range(2):
            for group in range(groups):
                pieces = []
                for c in range(2):
                    at = base * inner_all + c * inner_all // 2 + group * 2 * span
                    both = in_w[:, at : at + 2 * span]
                    pieces.append(jnp.where(row == 0, both[:, :span], both[:, span:]))
                ref[:, base * inner + group * span : base * inner + (group + 1) * span] = jnp.where(
                    part == 0, pieces[0], pieces[1]
                )
        source = lax.broadcasted_iota(jnp.int32, (depth, LANES), 0)
        lane = lax.broadcasted_iota(jnp.int32, (depth, LANES), 1)
        group = sum((lane >= g * each).astype(jnp.int32) for g in range(1, groups))
        head = state_all + part * (heads_all // 2) + (2 * group + row) * each + lane - group * each
        state = part * (state_all // 2) + row * (state_all // 4) + lane - spare
        wanted = jnp.where(lane < groups * each, head, jnp.where(lane >= spare, state, -1))
        ref[:, 2 * inner : 2 * inner + LANES] = dot(tail, (source == wanted).astype(BF16)).astype(BF16)
        if out_w is not None:
            half_rows, half = out_w.shape[0] // 2, out_w.shape[1] // 2
            mine = jnp.where(row == 0, out_w[:half_rows, :], out_w[half_rows:, :])
            ref[:, 2 * inner + LANES :] = jnp.where(part == 0, mine[:, :half], mine[:, half:])


def quarters_of(where, in_w, out_w, sizes):
    inner = sizes[0] // 4
    width = 2 * inner + LANES + (0 if out_w is None else out_w.shape[1] // 2)
    spec = pl.BlockSpec(memory_space=pltpu.VMEM)
    kernel = functools.partial(quarter_kernel, sizes)
    args = [where, in_w, out_w]
    if out_w is None:
        args = args[:2]
        inner_kernel = kernel
        kernel = lambda a, b, c, d: inner_kernel(a, b, None, c, d)
    return pl.pallas_call(
        kernel,
        in_specs=[pl.BlockSpec(memory_space=pltpu.SMEM)] + [spec] * (len(args) - 1),
        out_specs=[spec, spec],
        out_shape=[jax.ShapeDtypeStruct((in_w.shape[0], width), BF16)] * 2,
        compiler_params=pltpu.CompilerParams(vmem_limit_bytes=VMEM_LIMIT),
        cost_estimate=pl.CostEstimate(flops=0, bytes_accessed=10_000_000, transcendentals=0),
    )(*args)


def join_kernel(sizes, where, *refs):
    inner_all, state_all, groups, each, heads_all = sizes
    span = each * HALF
    inner = inner_all // 4
    row, core = where[2], where[3]
    has_out = len(refs) > 5
    in_ref = refs[-2] if has_out else refs[-1]

    def quarter(sources, c, r, low, high):
        mine, far, came, came_far = sources
        own = jnp.where(row == r, mine[:, low:high], far[:, low:high])
        theirs = jnp.where(row == r, came[:, low:high], came_far[:, low:high])
        return jnp.where(core == c, own, theirs)

    tails = 0.0
    spare, depth = LANES - state_all // 4, state_all + heads_all
    lane = lax.broadcasted_iota(jnp.int32, (LANES, depth), 0)
    target = lax.broadcasted_iota(jnp.int32, (LANES, depth), 1)
    group = sum((lane >= g * each).astype(jnp.int32) for g in range(1, groups))
    for c in range(2):
        for base in range(2):
            for g in range(groups):
                low = base * inner + g * span
                both = [quarter(refs[:4], c, r, low, low + span).astype(F32) for r in range(2)]
                at = base * inner_all + c * inner_all // 2 + g * 2 * span
                in_ref[0, :, at : at + 2 * span] = jnp.concatenate(both, axis=1)
        for r in range(2):
            head = state_all + c * (heads_all // 2) + (2 * group + r) * each + lane - group * each
            state = c * (state_all // 2) + r * (state_all // 4) + lane - spare
            wanted = jnp.where(lane < groups * each, head, jnp.where(lane >= spare, state, -1))
            chosen = (target == wanted).astype(BF16)
            tails = tails + dot(quarter(refs[:4], c, r, 2 * inner, 2 * inner + LANES), chosen)
            if has_out:
                half_rows, half = refs[4].shape
                low = quarter(refs[4:8], c, r, 0, half).astype(F32)
                refs[-1][0, r * half_rows : (r + 1) * half_rows, c * half : (c + 1) * half] = low
    in_ref[0, :, 2 * inner_all :] = tails


def join(where, quarters, sizes):
    rows = quarters[0].shape[0]
    inner_all, state_all, groups, each, heads_all = sizes
    shapes = [jax.ShapeDtypeStruct((1, rows, 2 * inner_all + state_all + heads_all), F32)]
    if len(quarters) > 4:
        shapes.append(jax.ShapeDtypeStruct((1, 2 * quarters[4].shape[0], 2 * quarters[4].shape[1]), F32))
    spec = pl.BlockSpec(memory_space=pltpu.VMEM)
    return pl.pallas_call(
        functools.partial(join_kernel, sizes),
        in_specs=[pl.BlockSpec(memory_space=pltpu.SMEM)] + [spec] * len(quarters),
        out_specs=[spec] * len(shapes),
        out_shape=shapes,
        compiler_params=pltpu.CompilerParams(vmem_limit_bytes=VMEM_LIMIT),
        cost_estimate=pl.CostEstimate(flops=0, bytes_accessed=12_000_000, transcendentals=0),
    )(where, *quarters)


class Links:
    def __init__(self, mesh_shape):
        self.line = mesh_shape["fsdp"] // 2
        at = self.fsdp = lax.axis_index("fsdp")
        self.at = jnp.where(at % 2 == 0, at // 2, 2 * self.line - 1 - at // 2)
        ring = [2 * p for p in range(self.line)] + [2 * p + 1 for p in reversed(range(self.line))]
        self.ahead = [(ring[k - 1], ring[k]) for k in range(len(ring))]
        self.behind = [(after, before) for before, after in self.ahead]
        self.row, self.core = lax.axis_index("dp"), lax.axis_index("section")

    def swap_core(self, x):
        return lax.ppermute(x, "section", [(0, 1), (1, 0)])

    def swap_row(self, x):
        return lax.ppermute(x, "dp", [(0, 1), (1, 0)])

    def swap_side(self, x):
        return lax.ppermute(x, "fsdp", [(2 * p + s, 2 * p + 1 - s) for p in range(self.line) for s in range(2)])

    def mine_of_core(self, first, second):
        return jnp.where(self.core == 0, first, second)

    def in_row_order(self, own, other, axis):
        return jnp.where(
            self.row == 0, jnp.concatenate([own, other], axis), jnp.concatenate([other, own], axis)
        )

    def in_core_order(self, own, other, axis):
        return jnp.where(
            self.core == 0, jnp.concatenate([own, other], axis), jnp.concatenate([other, own], axis)
        )

    def cut(self, x, axis, which, parts=2):
        size = x.shape[axis] // parts
        return lax.dynamic_slice_in_dim(x, which * size, size, axis)

    def upper(self, shard_rows):
        return (shard_rows + 31) // 32 * 16

    def gather(self, piece):
        shard_rows = piece.shape[0]
        upper = self.upper(shard_rows)
        up, down = piece[:upper], piece[upper:]
        sources, starts = [piece], [ring_owner(self.at, self.line) * shard_rows]
        for hop in range(1, 2 * self.line):
            up, down = yield [lax.ppermute(up, "fsdp", self.ahead), lax.ppermute(down, "fsdp", self.behind)]
            sources += [up, down]
            starts.append(ring_owner(self.at - hop, self.line) * shard_rows)
            starts.append(ring_owner(self.at + hop, self.line) * shard_rows + upper)
        return starts, sources

    def shift(self, x, by):
        line = self.line
        return lax.ppermute(x, "fsdp", [(2 * p + s, 2 * ((p + by) % line) + s) for p in range(line) for s in range(2)])

    def gather_side(self, piece):
        line, shard_rows = self.line, piece.shape[0]
        place, side = self.fsdp // 2, self.fsdp % 2
        order = sorted(range(1, line), key=lambda by: min(by, line - by))
        sources, starts = [], []
        held = piece
        for turn in range(line):
            by = 0 if turn == 0 else order[turn - 1]
            parts = [self.swap_side(held)]
            if turn < line - 1:
                parts.append(self.shift(piece, order[turn]))
            crossed, *moved = yield parts
            owner = 2 * lax.rem(place - by + line, line)
            sources += [held, crossed]
            starts += [(owner + side) * shard_rows, (owner + 1 - side) * shard_rows]
            held = moved[0] if moved else None
        return starts, sources

    def scatter_side(self, parts):
        line = self.line
        place, side = self.fsdp // 2, self.fsdp % 2
        order = sorted(range(1, line), key=lambda by: -min(by, line - by)) + [0]

        def term(by, other):
            owner = 2 * lax.rem(place + by, line) + (1 - side if other else side)
            return lax.dynamic_index_in_dim(parts, owner, 0, keepdims=False)

        total, summed = 0.0, None
        for turn in range(line):
            moves = [self.swap_side(term(order[turn], True))]
            if turn > 0:
                moves.append(self.shift(summed, order[turn - 1]))
            crossed, *moved = yield moves
            summed = term(order[turn], False).astype(F32) + crossed.astype(F32)
            if turn < line - 1:
                summed = summed.astype(BF16)
            if moved:
                total = total + moved[0].astype(F32)
        return (total + summed).astype(BF16)

    def scatter(self, shard_rows, term):
        upper = self.upper(shard_rows)
        up = down = None
        for hop in range(1, 2 * self.line):
            own_up = term(ring_owner(self.at - hop, self.line), 0, upper)
            own_down = term(ring_owner(self.at + hop, self.line), upper, shard_rows)
            if hop > 1:
                own_up = (own_up.astype(F32) + up.astype(F32)).astype(BF16)
                own_down = (own_down.astype(F32) + down.astype(F32)).astype(BF16)
            up, down = yield [lax.ppermute(own_up, "fsdp", self.ahead), lax.ppermute(own_down, "fsdp", self.behind)]
        owner = ring_owner(self.at, self.line)
        up = up.astype(F32) + term(owner, 0, upper).astype(F32)
        down = down.astype(F32) + term(owner, upper, shard_rows).astype(F32)
        return jnp.concatenate([up.astype(BF16), down.astype(BF16)], axis=0)

    def sum_line(self, x):
        size = self.line
        if size & (size - 1):
            return lax.psum(x, "fsdp") / 2
        by = 1
        while by < size:
            pairs = [(2 * p + s, 2 * (p ^ by) + s) for p in range(size) for s in range(2)]
            x = x + lax.ppermute(x, "fsdp", pairs)
            by *= 2
        return x


RING = {('gb', 0): True, ('gb', 1): False, ('out', 1): False, ('in', 1): True, ('out', 0): False, ('in', 0): True}


class Schedule:
    def __init__(self, work):
        self.work, self.sent, self.sides = work, None, []

    def launch(self, moves, finish):
        self.sides.append([moves, None, finish])

    def round(self, parts):
        extra = []
        if self.work is not None:
            try:
                extra = list(self.work.send(self.sent))
            except StopIteration:
                self.work = None
        groups = [list(parts), extra]
        going = []
        for side in self.sides:
            try:
                groups.append(list(side[0].send(side[1])))
                going.append(side)
            except StopIteration as stop:
                side[2](stop.value)
        self.sides = going
        joined = list(lax.optimization_barrier(tuple(x for group in groups for x in group)))
        split = []
        for group in groups:
            split.append(joined[: len(group)])
            joined = joined[len(group) :]
        self.sent = split[1]
        for side, values in zip(going, split[2:]):
            side[1] = values
        return split[0]

    def run(self, moves):
        sent = None
        while True:
            try:
                parts = moves.send(sent)
            except StopIteration as stop:
                return stop.value
            sent = self.round(parts)


def body(mesh_shape, inputs, seq_lengths, norm_gain, in_w, conv_w, conv_b, dt_bias, a_log, skip, out_gain, out_w, cotangent):
    links = Links(mesh_shape)
    core, row = links.core, links.row
    shards = mesh_shape["fsdp"]
    width = inputs.shape[1]
    half_width = width // 2
    own_tokens = inputs.shape[0]
    tokens = 2 * own_tokens
    rows = own_tokens // seq_lengths.shape[0]
    inner_all = out_gain.shape[1]
    heads_all = a_log.shape[1]
    head_dim = inner_all // heads_all
    taps, channels = conv_w.shape[1:]
    state_all = channels - inner_all
    state_own = state_all // 4
    heads = heads_all // 4
    inner = inner_all // 4
    split = 2 * inner + LANES
    shard_rows = in_w.shape[1]
    direct = heads_all % shards == 0 and (heads_all // shards) % 2 == 0
    groups = shards // 2 if direct else 1
    each = heads // groups
    span = each * head_dim
    sizes = (inner_all, state_all, groups, each, heads_all)

    def pick_row(x, axis):
        return jnp.where(row == 0, lax.index_in_dim(x, 0, axis, False), lax.index_in_dim(x, 1, axis, False))

    def pick(x, axis):
        return links.mine_of_core(lax.index_in_dim(x, 0, axis, False), lax.index_in_dim(x, 1, axis, False))

    def wide_part(x):
        x = pick(x.reshape(x.shape[0], 2, groups, 2, span), 1)
        return pick_row(x, 2).reshape(x.shape[0], inner)

    def head_part(x):
        x = pick(x.reshape(x.shape[0], 2, groups, 2, each), 1)
        return pick_row(x, 2).reshape(x.shape[0], heads)

    def state_part(x):
        x = pick(x.reshape(x.shape[0], 2, 2, state_own), 1)
        return pick_row(x, 1)

    def wide_row(x):
        return jnp.pad(x, ((0, 0), (0, channels - x.shape[1])))

    zero = jnp.int32(0)
    where = jnp.stack([zero, zero, row, core]).astype(jnp.int32)
    own_part, other_part = quarters_of(where, in_w[0], out_w[0] if direct else None, sizes)
    came_part = links.swap_core(other_part)
    both = (links.mine_of_core(own_part, came_part), links.mine_of_core(came_part, own_part))
    if not direct:
        out_first, out_second = out_w[0][:, :half_width], out_w[0][:, half_width:]
        kept = links.mine_of_core(out_first, out_second)
        came = links.swap_core(links.mine_of_core(out_second, out_first))
        out_pieces = (links.mine_of_core(kept, came), links.mine_of_core(came, kept))
    pieces = list(both)

    packed = jnp.concatenate(
        [conv_w[0], conv_b, wide_row(out_gain), wide_row(norm_gain), wide_row(dt_bias), wide_row(a_log), wide_row(skip)],
        axis=0,
    )
    packed_other = links.swap_core(packed)
    all_lengths = links.in_row_order(seq_lengths, links.swap_row(seq_lengths), 0)
    sent_tokens, pieces[0], all_lengths, packed_other = lax.optimization_barrier(
        (inputs, pieces[0], all_lengths, packed_other)
    )

    def layer_params(pack):
        cw, cb = pack[:taps], pack[taps : taps + 1]
        og, ng = pack[taps + 1 : taps + 2, :inner_all], pack[taps + 2 : taps + 3, :width]
        dt, al, sk = (pack[taps + 3 + k : taps + 4 + k, :heads_all] for k in range(3))
        lanes = inner + state_all
        fill = lambda x: jnp.pad(x, ((0, 0), (0, lanes - x.shape[1])))
        conv = jnp.concatenate([cw, cb], axis=0)
        narrow = jnp.concatenate([head_part(dt), -jnp.exp(head_part(al))], axis=0)
        narrow = jnp.pad(narrow, ((0, 0), (0, LANES - heads))).reshape(1, 2 * LANES)
        own_state = jnp.pad(state_part(conv[:, inner_all:]), ((0, 0), (LANES - state_own, 0)))
        rows_ = [
            jnp.concatenate([wide_part(conv[:, :inner_all]), conv[:, inner_all:]], axis=1),
            fill(wide_part(og)),
            fill(jnp.repeat(head_part(sk), head_dim, axis=1)),
            fill(narrow),
            fill(own_state),
        ]
        return fill(jnp.concatenate([jnp.concatenate(rows_, axis=0), jnp.zeros((16 - 2 * taps - 5, lanes), F32)], axis=0)), ng

    blocks = tokens // rows
    big = {}

    def to_rows(x):
        return x.reshape(-1, LANES)

    def norm_of(u):
        return lax.rsqrt(jnp.mean(u * u, axis=-1, keepdims=True) + 1e-05)

    def over_cores(x):
        return links.cut(x, 1, core) + links.swap_core(links.cut(x, 1, 1 - core))

    def own_rows(x):
        return links.cut(x, 0, row)

    def norm_back(u, gain, d_scaled):
        u = u.astype(F32)
        inverse = norm_of(u)
        meet = jnp.mean(u * gain * d_scaled, axis=1, keepdims=True)
        return inverse * gain * d_scaled - u * (inverse * inverse * inverse * meet)

    def gain_back(u, d_scaled):
        u = u.astype(F32)
        return jnp.sum(u * norm_of(u) * d_scaled, axis=0, keepdims=True)

    def scaled_of(u, gain):
        u = u.astype(F32)
        return (u * norm_of(u) * gain).astype(BF16)

    def out_whole(pieces):
        kept = links.cut(pieces, 0, core)
        came = links.swap_core(links.cut(pieces, 0, 1 - core))
        return links.in_core_order(kept, came, 1)

    def ahead(layer, scaled):
        wide_w, last_w = big["in", layer]
        last = dot(scaled, last_w)
        came = links.swap_row(last[:, LANES - state_own :])
        proj = dot(scaled, wide_w)
        proj, last, came = yield [proj, last, came]
        part = links.in_row_order(last[:, LANES - state_own :], came, 1)
        bc = links.in_core_order(part, links.swap_core(part), 1)
        outs, gated, squares = ahead_call(heads, taps, rows, proj, last, bc, aux, seg_rows, big["pack", layer])
        bc, outs, gated, squares = yield [bc, outs, gated, squares]
        squares = to_rows(squares[:, 0])
        squares = squares + links.swap_core(squares)
        squares = squares + links.swap_row(squares)
        (squares,) = yield [squares]
        inverse = lax.rsqrt(squares.reshape(tokens, 1) / inner_all + 1e-05)
        gain = big["pack", layer][taps + 1 : taps + 2, :inner]
        normed = (gated * inverse * gain).astype(BF16)
        normed_all = links.in_core_order(normed, links.swap_core(normed), 1)
        return {"scaled": scaled, "proj": proj, "last": last, "bc": bc, "outs": outs, "gated": gated, "inverse": inverse, "normed": normed_all}

    def back_first(layer, kept, grad, meet=None):
        d_normed = dot(grad, big["out_whole", layer], ((1,), (1,)))
        gain = big["pack", layer][taps + 1 : taps + 2, :inner]
        if meet is None:
            meet = to_rows(jnp.sum(kept["gated"] * gain * d_normed, axis=1))
            d_normed, meet = yield [d_normed, meet]
            meet = meet + links.swap_core(meet)
            meet = (links.swap_row(meet) + meet) * to_rows(kept["inverse"][:, 0])
            (meet,) = yield [meet]
        else:
            meet = meet + links.swap_core(meet)
            d_normed, meet = yield [d_normed, meet]
        inverse = kept["inverse"]
        shrink = inverse * inverse * meet.reshape(tokens, 1) / inner_all
        d_main, d_dt, d_bc, d_wide, d_narrow = back_call(
            heads, taps, rows, kept["proj"], kept["last"], kept["bc"], aux, seg_rows, big["pack", layer],
            kept["outs"], d_normed, inverse, shrink,
        )
        d_main, d_dt, d_bc, d_wide, d_narrow = yield [d_main, d_dt, d_bc, d_wide, d_narrow]
        wide_w, last_w = big["in", layer]
        d_bc = over_cores(d_bc)
        d_bc = links.cut(d_bc, 1, row) + links.swap_row(links.cut(d_bc, 1, 1 - row))
        d_in = dot(kept["scaled"], d_main, ((0,), (0,))).astype(BF16)
        d_scaled = dot(d_main, wide_w, ((1,), (1,)))
        d_bc, d_in, d_scaled = yield [d_bc, d_in, d_scaled]
        d_bc = jnp.pad(d_bc, ((0, 0), (LANES - d_bc.shape[1], 0)))
        d_last, d_state = state_back_call(taps, d_bc, kept["last"], aux, big["pack", layer], d_dt)
        d_in_last = dot(kept["scaled"], d_last, ((0,), (0,))).astype(BF16)
        d_scaled = d_scaled + dot(d_last, last_w, ((1,), (1,)))
        d_scaled, d_in, d_in_last = yield [d_scaled, d_in, d_in_last]
        done["in", layer] = d_in, d_in_last
        return d_scaled, (jnp.sum(d_wide, axis=0), jnp.sum(d_narrow, axis=0), d_state)

    def out_grad(kept, grad):
        return dot(kept["normed"], links.cut(grad, 1, core), ((0,), (0,))).astype(BF16)

    def four(low0, low1, far0, far1, theirs):
        return [
            links.mine_of_core(low0, low1),
            links.mine_of_core(far0, far1),
            theirs,
            links.swap_core(links.mine_of_core(far1, far0)),
        ]

    aux = seg_rows = None
    done = {}

    def send_out(layer, d_out):
        done["out", layer] = d_out
        if direct and not RING["out", layer]:


            def finish(total):
                done["sum", ("out", layer)] = total

            schedule.launch(links.scatter_side(d_out.reshape(shards, shard_rows, half_width)), finish)

    def work():
        nonlocal aux, seg_rows
        pack0, gain0 = layer_params(links.mine_of_core(packed, packed_other))
        pack1, gain1 = layer_params(links.mine_of_core(packed_other, packed))
        ends = jnp.cumsum(all_lengths, axis=1)
        positions = jnp.arange(rows, dtype=jnp.int32)
        segments = jnp.sum((positions[None, :, None] >= ends[:, None, :]).astype(jnp.int32), axis=2)
        aux, seg_rows = make_aux(segments, rows, taps), segments.astype(F32)[:, None, :]
        came_tokens = links.swap_row(sent_tokens)
        pack0, pack1, gain0, gain1, aux, seg_rows = yield [pack0, pack1, gain0, gain1, aux, seg_rows]
        big["pack", 0], big["pack", 1] = pack0, pack1
        (came_tokens,) = yield [came_tokens]
        tokens_all = links.in_row_order(inputs, came_tokens, 0)
        scaled = scaled_of(tokens_all, gain0)
        sent_cot, _ = lax.optimization_barrier((cotangent, came_tokens))
        came_cot = links.swap_row(sent_cot)
        tokens_all, scaled = yield [tokens_all, scaled]
        yield [scaled]
        cot_all = links.in_row_order(cotangent, came_cot, 0)
        (cot_all,) = yield [cot_all]
        while ("in", 0) not in big:
            yield [scaled]
        kept0 = yield from ahead(0, scaled)
        while ("out", 0) not in big:
            yield [scaled]
        branch = dot(kept0["normed"], big["out", 0]).astype(BF16)
        kept0["normed"], kept0["inverse"], branch = yield [kept0["normed"], kept0["inverse"], branch]
        came = links.swap_row(branch)
        big["out_whole", 0] = out_whole(big["out", 0])
        branch, big["out_whole", 0] = yield [branch, big["out_whole", 0]]
        (came,) = yield [came]
        while ("in", 1) not in big:
            yield [came]
        branch = branch.astype(F32) + came.astype(F32)
        first = (links.cut(tokens_all, 1, core).astype(F32) + branch).astype(BF16)
        first = links.in_core_order(first, links.swap_core(first), 1)
        scaled = scaled_of(first, gain1)
        kept1 = yield from ahead(1, scaled)
        d_out = out_grad(kept1, cot_all)
        kept1["normed"], kept1["inverse"], d_out = yield [kept1["normed"], kept1["inverse"], d_out]
        send_out(1, d_out)
        while ("out", 1) not in big:
            yield [first]
        big["out_whole", 1] = out_whole(big["out", 1])
        d_scaled, small1 = yield from back_first(1, kept1, cot_all)
        d_scaled = over_cores(d_scaled).astype(BF16)
        (d_scaled,) = yield [d_scaled]
        came = links.swap_row(d_scaled)
        yield [d_scaled]
        (came,) = yield [came]
        d_scaled = d_scaled.astype(F32) + came.astype(F32)
        d_scaled = links.in_core_order(d_scaled, links.swap_core(d_scaled), 1)
        grad = (cot_all.astype(F32) + norm_back(first, gain1, d_scaled)).astype(BF16)
        gain_sum1 = gain_back(own_rows(first), own_rows(d_scaled))
        d_out = out_grad(kept0, grad)
        grad, d_out = yield [grad, d_out]
        send_out(0, d_out)
        meet = to_rows(jnp.sum(branch * links.cut(grad, 1, core).astype(F32), axis=1))
        d_scaled, small0 = yield from back_first(0, kept0, grad, meet)
        d_scaled = over_cores(d_scaled)
        (d_scaled,) = yield [d_scaled]
        came = links.swap_row(links.cut(d_scaled, 0, 1 - row).astype(BF16))
        (came,) = yield [came]
        d_scaled = own_rows(d_scaled) + came.astype(F32)
        d_scaled = links.in_core_order(d_scaled, links.swap_core(d_scaled), 1)
        own_grad = own_rows(grad)
        grad_in = (own_grad.astype(F32) + norm_back(inputs, gain0, d_scaled)).astype(BF16)
        gain_sum0 = gain_back(inputs, d_scaled)
        grad_in, gain_sum0 = yield [grad_in, gain_sum0]
        done["input_grad"] = jnp.where(core == 0, grad_in, own_grad)[None]
        while ("sum", ("in", 1)) not in done:
            yield [gain_sum0]
        far_in1 = links.swap_row(done["sum", ("in", 1)])
        small = jnp.concatenate([pack_small(*small0, gain_sum0), pack_small(*small1, gain_sum1)], axis=0)
        small = small + links.swap_side(small)
        if direct:
            while ("sum", ("out", 0)) not in done:
                yield [small]
            out0, out1 = done["sum", ("out", 0)], done["sum", ("out", 1)]
            far0, far1 = links.swap_row(out0), links.swap_row(out1)
            small, far0, far1 = yield [small, far0, far1]
            theirs = links.swap_core(links.mine_of_core(out1, out0))
            done["out_quarters"] = four(out0, out1, far0, far1, theirs)
        small = links.sum_line(small)
        (small,) = yield [small]
        small_other = links.swap_row(small)
        partial = dot(kept1["normed"], big["out", 1])
        small, small_other, partial = yield [small, small_other, partial]
        came = links.swap_row(links.cut(partial, 0, 1 - row).astype(BF16))
        done["small"] = spread_small(small, small_other)
        came, done["far", "in"], *done["small"] = yield [came, far_in1] + list(done["small"])
        second = own_rows(partial) + came.astype(F32) + links.cut(own_rows(first), 1, core).astype(F32)
        second = second.astype(BF16)
        second = links.in_core_order(second, links.swap_core(second), 1)
        done["phase_out"] = jnp.where(core == 0, own_rows(first), second)[None]
        (done["phase_out"],) = yield [done["phase_out"]]

    gain_rows = width // inner

    def pack_small(wide_, narrow, d_state, gain):
        gain = gain.reshape(-1, inner)
        narrow_rows = jnp.concatenate([narrow[:2], d_state[: taps + 1]], axis=0)
        narrow_rows = jnp.pad(narrow_rows.reshape(1, -1), ((0, 0), (0, 2 * inner - narrow_rows.size)))
        return jnp.concatenate([wide_[: taps + 3], gain, narrow_rows.reshape(2, inner)], axis=0)

    def by_row(a, b):
        return jnp.where(row == 0, jnp.stack([a, b]), jnp.stack([b, a]))

    def spread_small(small, small_other):
        per = small.shape[0] // 2
        mine = links.mine_of_core(small[:per], small[per:])
        mine_other = links.mine_of_core(small_other[:per], small_other[per:])
        theirs = links.mine_of_core(small[per:], small[:per])
        theirs_other = links.mine_of_core(small_other[per:], small_other[:per])
        came = links.swap_core(jnp.stack([theirs, theirs_other]))
        own_parts, came_parts = by_row(mine, mine_other), by_row(came[0], came[1])
        quarters = jnp.where(core == 0, jnp.stack([own_parts, came_parts]), jnp.stack([came_parts, own_parts]))

        def spread_wide(x):
            lead = x.shape[2:-1]
            x = x.reshape((2, 2) + lead + (groups, span))
            x = jnp.moveaxis(x, (0, 1), (len(lead), len(lead) + 2))
            return x.reshape(lead + (inner_all,))

        def spread_heads(x):
            x = x.reshape((2, 2, groups, each))
            return jnp.moveaxis(x, 1, 2).reshape(1, heads_all)

        grad_norm = mine[taps + 3 : taps + 3 + gain_rows] + mine_other[taps + 3 : taps + 3 + gain_rows]
        narrow = quarters[:, :, taps + 3 + gain_rows :].reshape(2, 2, -1)
        narrow = narrow[:, :, : (taps + 3) * LANES].reshape(2, 2, taps + 3, LANES)
        states = jnp.moveaxis(narrow[:, :, 2:, LANES - state_own :], 2, 0).reshape(taps + 1, state_all)
        wide_full = spread_wide(quarters[:, :, : taps + 3])
        return [
            grad_norm.reshape(1, width),
            jnp.concatenate([wide_full[:taps], states[:taps]], axis=1)[None],
            jnp.concatenate([wide_full[taps : taps + 1], states[taps:]], axis=1),
            spread_heads(narrow[:, :, 0, :heads]),
            spread_heads(narrow[:, :, 1, :heads]),
            wide_full[taps + 1].reshape(1, heads_all, head_dim).sum(axis=-1),
            wide_full[taps + 2 : taps + 3],
        ]

    schedule = Schedule(work())

    def gather(layer):
        cuts = [(0, 2 * inner), (2 * inner, split)]
        piece, side_piece = pieces[layer], None
        if direct and RING["gb", layer]:
            cuts.append((split, split + half_width))
        elif direct:
            piece, side_piece = piece[:, :split], piece[:, split:]
        if side_piece is not None:

            def finish(found):
                (big["out", layer],) = assemble(*found, [(0, half_width)])

            schedule.launch(links.gather_side(side_piece), finish)
        full = assemble(*schedule.run(links.gather(piece)), cuts)
        big["in", layer] = full[:2]
        if len(cuts) > 2:
            big["out", layer] = full[2]
        elif not direct:
            big["out", layer] = out_gathered(layer)

    def scatter(kind, layer):
        name = (kind, layer)
        while name not in done:
            schedule.round([])
        if kind == "out" and direct and not RING[name]:
            return
        if kind == "out" and not direct:
            parts = done[name].reshape(2, 1, inner, half_width)
            parts = links.in_row_order(parts, jnp.zeros_like(parts), 1).reshape(4 * inner, half_width)
            mine = lax.psum_scatter(parts, "fsdp", scatter_dimension=0, tiled=True)
            total = mine.astype(F32) + links.swap_row(mine).astype(F32)
            done["sum", name] = total.astype(BF16)
        elif RING[name]:
            parts = [x.reshape(shards, shard_rows, -1) for x in (done[name] if kind == "in" else [done[name]])]

            def term(owner, low, high):
                taken = [lax.dynamic_slice(x, (owner, low, 0), (1, high - low, x.shape[2]))[0] for x in parts]
                return taken[0] if len(taken) == 1 else jnp.concatenate(taken, axis=1)

            done["sum", name] = schedule.run(links.scatter(shard_rows, term))
        else:
            parts = jnp.concatenate(done[name], axis=1) if kind == "in" else done[name]
            done["sum", name] = lax.psum_scatter(parts, "fsdp", scatter_dimension=0, tiled=True)

    def out_gathered(layer):
        full = lax.all_gather(out_pieces[layer], "fsdp", axis=0, tiled=True)
        return pick_row(full.reshape(2, 2, inner, half_width), 1).reshape(2 * inner, half_width)

    gather(0)
    gather(1)
    scatter("out", 1)
    scatter("in", 1)
    scatter("out", 0)
    scatter("in", 0)
    while schedule.work is not None:
        schedule.round([])

    low0, low1, far1 = done["sum", ("in", 0)], done["sum", ("in", 1)], done["far", "in"]
    out0, out1 = done["sum", ("out", 0)], done["sum", ("out", 1)]
    theirs = links.swap_core(links.mine_of_core(low1, low0))
    quarters = four(low0, low1, links.swap_row(low0), far1, theirs)
    if direct:
        grad_in_w, grad_out_w = join(where, quarters + done["out_quarters"], sizes)
    else:
        (grad_in_w,) = join(where, quarters, sizes)
        theirs = links.swap_core(links.mine_of_core(out1, out0))
        grad_out_w = links.in_core_order(links.mine_of_core(out0, out1), theirs, 1).astype(F32)[None]
    grad_norm, grad_conv_w, grad_conv_b, grad_dt, grad_a, grad_skip, grad_out_gain = done["small"]
    return (
        done["phase_out"], done["input_grad"], grad_norm, grad_in_w, grad_conv_w, grad_conv_b,
        grad_dt, grad_a, grad_skip, grad_out_gain, grad_out_w,
    )


def solution(mesh):
    return jax.shard_map(
        functools.partial(body, dict(mesh.shape)),
        mesh=mesh,
        in_specs=(
            P(("fsdp", "dp"), None),
            P(("fsdp", "dp"), None),
            P("section", None),
            P("section", "fsdp", None),
            P("section", None, None),
            P("section", None),
            P("section", None),
            P("section", None),
            P("section", None),
            P("section", None),
            P("section", "fsdp", None),
            P(("fsdp", "dp"), None),
        ),
        out_specs=(
            P("section", ("fsdp", "dp"), None),
            P("section", ("fsdp", "dp"), None),
            P("section", None),
            P("section", "fsdp", None),
            P("section", None, None),
            P("section", None),
            P("section", None),
            P("section", None),
            P("section", None),
            P("section", None),
            P("section", "fsdp", None),
        ),
        check_vma=False,
    )
```

```python
import functools

import jax
import jax.numpy as jnp
from jax import lax
from jax.experimental import pallas as pl
from jax.experimental.pallas import tpu as pltpu
from jax.sharding import PartitionSpec as P

F32 = jnp.float32
BF16 = jnp.bfloat16
LANES = 128
HALF = 64
VMEM_LIMIT = 40 * 1024 * 1024
VMEM_ALL = 60 * 1024 * 1024
VMEM_ADD = 16 * 1024 * 1024


def dot(a, b, dims=((1,), (0,)), precision=None):
    return lax.dot_general(a, b, (dims, ((), ())), precision=precision, preferred_element_type=F32)


def dot_exact(a, b, dims=((1,), (0,))):
    return dot(a, b, dims, lax.Precision.HIGHEST)


def silu_parts(x):
    gate = 1.0 / (1.0 + jnp.exp(-x))
    return gate, x * gate


def softplus(x):
    return jnp.maximum(x, 0.0) + jnp.log1p(jnp.exp(-jnp.abs(x)))


def conv_mixed(conv_in, aux, conv_w, conv_b):
    taps = conv_w.shape[0]
    mixed = conv_b + conv_w[taps - 1 : taps] * conv_in
    shifted = []
    for back in range(1, taps):
        moved = pltpu.roll(conv_in, back, 0) * aux[:, back : back + 1]
        shifted.append(moved)
        mixed = mixed + conv_w[taps - 1 - back : taps - back] * moved
    return mixed, shifted


def conv_back(d_mixed, conv_in, shifted, aux, conv_w):
    taps = conv_w.shape[0]
    rows = d_mixed.shape[0]
    d_in = conv_w[taps - 1 : taps] * d_mixed
    d_w = [None] * taps
    d_w[taps - 1] = jnp.sum(d_mixed * conv_in, axis=0, keepdims=True)
    for back in range(1, taps):
        ahead = pltpu.roll(d_mixed, rows - back, 0) * aux[:, taps - 1 + back : taps + back]
        d_in = d_in + conv_w[taps - 1 - back : taps - back] * ahead
        d_w[taps - 1 - back] = jnp.sum(d_mixed * shifted[back - 1], axis=0, keepdims=True)
    return d_in, d_w, jnp.sum(d_mixed, axis=0, keepdims=True)


def decays(last, dt_bias, neg_rate, aux, seg_row):
    rows = last.shape[0]
    step = softplus(last + dt_bias)
    row = lax.broadcasted_iota(jnp.int32, (rows, rows), 0)
    col = lax.broadcasted_iota(jnp.int32, (rows, rows), 1)
    lower = row >= col
    log_decay = dot_exact(lower.astype(F32), neg_rate * step)
    allowed = lower & (aux[:, 0:1] == seg_row)
    return step, log_decay, allowed, lower


def pair_masks(rows):
    lane = lax.broadcasted_iota(jnp.int32, (rows, LANES), 1)
    return (lane < HALF).astype(F32), (lane >= HALF).astype(F32)


def unpack(packed, taps, heads):
    inner = heads * HALF
    conv_w, conv_b = packed[:taps, :], packed[taps : taps + 1, :]
    out_gain, skip = packed[taps + 1 : taps + 2, :inner], packed[taps + 2 : taps + 3, :inner]
    dt_bias, neg_rate = packed[taps + 3 : taps + 4, :LANES], packed[taps + 3 : taps + 4, LANES : 2 * LANES]
    return conv_w, conv_b, dt_bias, neg_rate, skip, out_gain


def ahead_kernel(heads, taps, proj, last, bc, aux, seg_row, packed, outs_ref, gated_ref, square_ref):
    rows = proj.shape[0]
    conv_w, conv_b, dt_bias, neg_rate, skip, _ = unpack(packed, taps, heads)
    inner = heads * HALF
    aux_v = aux[...]
    values_mixed, _ = conv_mixed(proj[:, inner : 2 * inner], aux_v, conv_w[:, :inner], conv_b[:, :inner])
    _, values = silu_parts(values_mixed)
    state_mixed, _ = conv_mixed(bc[...], aux_v, conv_w[:, inner:], conv_b[:, inner:])
    _, state = silu_parts(state_mixed)
    in_state, out_state = state[:, :LANES].astype(BF16), state[:, LANES:].astype(BF16)
    step, log_decay, allowed, _ = decays(
        last[...], dt_bias, neg_rate, aux_v, seg_row[0]
    )
    step_t, log_t = step.T, log_decay.T
    inter = dot(out_state, in_state, ((1,), (1,)))
    first, second = pair_masks(rows)
    squares = jnp.zeros((rows, 1), F32)
    for pair in range(heads // 2):
        weights = []
        for h in (2 * pair, 2 * pair + 1):
            gap = log_decay[:, h : h + 1] - log_t[h : h + 1]
            decay = jnp.exp(jnp.where(allowed, gap, -1e30))
            weights.append((inter * decay * step_t[h : h + 1]).astype(BF16))
        at = slice(pair * LANES, (pair + 1) * LANES)
        own = values[:, at]
        low = own.astype(BF16).astype(F32)
        both = jnp.concatenate([low * first, low * second], axis=0).astype(BF16)
        carried = dot(jnp.concatenate(weights, axis=1), both)
        outs = carried + skip[:, at] * own
        _, gate = silu_parts(proj[:, at])
        gated = outs * gate
        outs_ref[:, at] = outs
        gated_ref[:, at] = gated
        squares = squares + jnp.sum(gated * gated, axis=1, keepdims=True)
    square_ref[...] = jnp.broadcast_to(squares, square_ref.shape)


def back_kernel(
    heads, taps, proj, last_ref, bc, aux, seg_row, packed, outs, d_normed, scale, *results
):
    d_main_ref, d_dt_ref, d_state_ref, d_wide_ref, d_narrow_ref = results
    rows = proj.shape[0]
    conv_w, conv_b, dt_bias, neg_rate, skip, out_gain = unpack(packed, taps, heads)
    inner = heads * HALF
    aux_v = aux[...]
    values_in = proj[:, inner : 2 * inner]
    values_mixed, values_shifted = conv_mixed(values_in, aux_v, conv_w[:, :inner], conv_b[:, :inner])
    values_gate, values = silu_parts(values_mixed)
    state_mixed, _ = conv_mixed(bc[...], aux_v, conv_w[:, inner:], conv_b[:, inner:])
    _, state = silu_parts(state_mixed)
    in_state, out_state = state[:, :LANES].astype(BF16), state[:, LANES:].astype(BF16)
    last = last_ref[...]
    step, log_decay, allowed, lower = decays(last, dt_bias, neg_rate, aux_v, seg_row[0])
    step_t, log_t = step.T, log_decay.T
    inter = dot(out_state, in_state, ((1,), (1,)))
    first, second = pair_masks(rows)
    lane = lax.broadcasted_iota(jnp.int32, (rows, LANES), 1)
    sub = lax.broadcasted_iota(jnp.int32, (LANES, rows), 0)
    inverse, shrink = scale[:, 0:1], scale[:, 1:2]
    d_inter = jnp.zeros((rows, rows), F32)
    row_sums = jnp.zeros((rows, LANES), F32)
    col_sums = jnp.zeros((LANES, rows), F32)
    d_skip, d_gain, d_values = [], [], []
    for pair in range(heads // 2):
        at = slice(pair * LANES, (pair + 1) * LANES)
        own = values[:, at]
        low = own.astype(BF16)
        gate_in = proj[:, at]
        sig, gate = silu_parts(gate_in)
        outs_at = outs[:, at]
        gated = outs_at * gate
        dn = d_normed[:, at]
        d_gain.append(jnp.sum(gated * inverse * dn, axis=0, keepdims=True))
        d_gated = inverse * (out_gain[:, at] * dn) - gated * shrink
        d_outs = d_gated * gate
        d_main_ref[:, at] = (d_gated * outs_at * (sig * (1.0 + gate_in * (1.0 - sig)))).astype(BF16)
        d_skip.append(jnp.sum(d_outs * own, axis=0, keepdims=True))
        d_both = jnp.concatenate([d_outs * first, d_outs * second], axis=0).astype(BF16)
        d_weights = dot(d_both, low, ((1,), (1,)))
        weights = []
        for k, h in enumerate((2 * pair, 2 * pair + 1)):
            gap = log_decay[:, h : h + 1] - log_t[h : h + 1]
            decay = jnp.exp(jnp.where(allowed, gap, -1e30))
            step_row = step_t[h : h + 1]
            weights.append((inter * decay * step_row).astype(BF16))
            part = d_weights[k * rows : (k + 1) * rows] * decay
            d_inter = d_inter + part * step_row
            part = part * inter
            col = jnp.sum(part, axis=0, keepdims=True)
            col_sums = jnp.where(sub == h, col, col_sums)
            row_sum = jnp.sum(part * step_row, axis=1, keepdims=True)
            row_sums = jnp.where(lane == h, row_sum, row_sums)
        d_low = dot(jnp.concatenate(weights, axis=0), d_both, ((0,), (0,)))
        d_values.append(skip[:, at] * d_outs + d_low)
    d_values = jnp.concatenate(d_values, axis=1)
    d_mixed = d_values * (values_gate * (1.0 + values_mixed * (1.0 - values_gate)))
    d_in, d_w, d_b = conv_back(d_mixed, values_in, values_shifted, aux_v, conv_w[:, :inner])
    d_main_ref[:, inner : 2 * inner] = d_in.astype(BF16)
    low_inter = d_inter.astype(BF16)
    d_state_ref[:, :LANES] = dot(low_inter, out_state, ((0,), (0,)))
    d_state_ref[:, LANES:] = dot(low_inter, in_state)
    direct = col_sums.T
    d_log = row_sums - direct * step
    d_pace = dot_exact(lower.astype(F32), d_log, ((0,), (0,)))
    d_step = direct + d_pace * neg_rate
    d_last = jnp.where(lane < heads, d_step * (1.0 / (1.0 + jnp.exp(-(last + dt_bias)))), 0.0)
    d_dt_ref[...] = d_last
    wide = d_w + [d_b, jnp.concatenate(d_skip, axis=1), jnp.concatenate(d_gain, axis=1)]
    wide.append(jnp.zeros((d_wide_ref.shape[1] - len(wide), inner), F32))
    d_wide_ref[0] = jnp.concatenate(wide, axis=0)
    d_rate = jnp.sum(d_pace * neg_rate * step, axis=0, keepdims=True)
    narrow = [
        jnp.sum(d_last, axis=0, keepdims=True),
        jnp.where(lane[:1] < heads, d_rate, 0.0),
        jnp.zeros((d_narrow_ref.shape[1] - 2, LANES), F32),
    ]
    d_narrow_ref[0] = jnp.concatenate(narrow, axis=0)


def state_back_kernel(taps, d_act, last, aux, packed, d_dt, d_proj_ref, d_sums_ref):
    aux_v = aux[...]
    last_v = last[...]
    conv_w, conv_b = packed[8 : 8 + taps, :LANES], packed[8 + taps : 9 + taps, :LANES]
    mixed, shifted = conv_mixed(last_v, aux_v, conv_w, conv_b)
    sig, _ = silu_parts(mixed)
    d_mixed = d_act[...] * (sig * (1.0 + mixed * (1.0 - sig)))
    d_in, d_w, d_b = conv_back(d_mixed, last_v, shifted, aux_v, conv_w)
    lane = lax.broadcasted_iota(jnp.int32, last_v.shape, 1)
    d_proj_ref[...] = jnp.where(lane < HALF, d_dt[...], d_in).astype(BF16)
    sums = d_w + [d_b]
    sums.append(jnp.zeros((d_sums_ref.shape[0] - len(sums), LANES), F32))
    d_sums_ref[...] = jnp.concatenate(sums, axis=0)


def rows_spec(rows, width):
    return pl.BlockSpec((rows, width), lambda i: (i, 0))


def whole_spec(shape):
    return pl.BlockSpec(shape, lambda i: (0,) * len(shape))


def ahead_call(heads, taps, rows, proj, last, bc, aux, seg_rows, packed):
    total = proj.shape[0]
    inner = heads * HALF
    count = total // rows
    return pl.pallas_call(
        functools.partial(ahead_kernel, heads, taps),
        grid=(count,),
        in_specs=[
            rows_spec(rows, proj.shape[1]),
            rows_spec(rows, LANES),
            rows_spec(rows, bc.shape[1]),
            rows_spec(rows, aux.shape[1]),
            pl.BlockSpec((1, 1, rows), lambda i: (i, 0, 0)),
            whole_spec(packed.shape),
        ],
        out_specs=[rows_spec(rows, inner), rows_spec(rows, inner), rows_spec(rows, LANES)],
        out_shape=[
            jax.ShapeDtypeStruct((total, inner), F32),
            jax.ShapeDtypeStruct((total, inner), F32),
            jax.ShapeDtypeStruct((total, LANES), F32),
        ],
        compiler_params=pltpu.CompilerParams(vmem_limit_bytes=VMEM_LIMIT),
        cost_estimate=pl.CostEstimate(
            flops=count * 1_000_000_000, bytes_accessed=count * 2_000_000, transcendentals=count * 400_000
        ),
    )(proj, last, bc, aux, seg_rows, packed)


def back_call(heads, taps, rows, proj, last, bc, aux, seg_rows, packed, outs, d_normed, scale):
    total = proj.shape[0]
    inner = heads * HALF
    count = total // rows
    return pl.pallas_call(
        functools.partial(back_kernel, heads, taps),
        grid=(count,),
        in_specs=[
            rows_spec(rows, proj.shape[1]),
            rows_spec(rows, LANES),
            rows_spec(rows, bc.shape[1]),
            rows_spec(rows, aux.shape[1]),
            pl.BlockSpec((1, 1, rows), lambda i: (i, 0, 0)),
            whole_spec(packed.shape),
            rows_spec(rows, inner),
            rows_spec(rows, inner),
            rows_spec(rows, 2),
        ],
        out_specs=[
            rows_spec(rows, 2 * inner),
            rows_spec(rows, LANES),
            rows_spec(rows, bc.shape[1]),
            pl.BlockSpec((1, 8, inner), lambda i: (i, 0, 0)),
            pl.BlockSpec((1, 8, LANES), lambda i: (i, 0, 0)),
        ],
        out_shape=[
            jax.ShapeDtypeStruct((total, 2 * inner), BF16),
            jax.ShapeDtypeStruct((total, LANES), F32),
            jax.ShapeDtypeStruct((total, bc.shape[1]), F32),
            jax.ShapeDtypeStruct((count, 8, inner), F32),
            jax.ShapeDtypeStruct((count, 8, LANES), F32),
        ],
        compiler_params=pltpu.CompilerParams(vmem_limit_bytes=VMEM_LIMIT),
        cost_estimate=pl.CostEstimate(
            flops=count * 2_000_000_000, bytes_accessed=count * 3_000_000, transcendentals=count * 600_000
        ),
    )(proj, last, bc, aux, seg_rows, packed, outs, d_normed, scale)


def state_back_call(taps, d_act, last, aux, packed, d_dt):
    args = (d_act, last, aux, packed, d_dt)
    return pl.pallas_call(
        functools.partial(state_back_kernel, taps),
        grid=(1,),
        in_specs=[whole_spec(x.shape) for x in args],
        out_specs=[whole_spec(last.shape), whole_spec((8, LANES))],
        out_shape=[jax.ShapeDtypeStruct(last.shape, BF16), jax.ShapeDtypeStruct((8, LANES), F32)],
        compiler_params=pltpu.CompilerParams(vmem_limit_bytes=VMEM_LIMIT),
        cost_estimate=pl.CostEstimate(flops=100_000_000, bytes_accessed=1_500_000, transcendentals=70_000),
    )(*args)


def make_aux(seg, rows, taps):
    blocks = seg.shape[0]
    columns = [seg.astype(F32)]
    for k in range(1, taps):
        before = jnp.pad(seg, ((0, 0), (k, 0)), constant_values=-1)[:, :rows]
        columns.append((before == seg).astype(F32))
    for k in range(1, taps):
        after = jnp.pad(seg, ((0, 0), (0, k)), constant_values=-1)[:, k:]
        columns.append((after == seg).astype(F32))
    columns += [jnp.zeros_like(columns[0])] * (8 - len(columns))
    return jnp.stack(columns, axis=-1).reshape(blocks * rows, 8)


def ring_owner(at, line):
    at = lax.rem(at + 2 * line, 2 * line)
    return jnp.where(at < line, 2 * at, 4 * line - 2 * at - 1)


def ring_add_kernel(count, upper, has_sums, owners, *refs):
    ups, downs = refs[:count], refs[count : 2 * count]
    sums = refs[2 * count : 2 * count + 2] if has_sums else None
    outs = refs[2 * count + 2 * has_sums :]
    low = 0
    for up, down in zip(ups, downs):
        high = low + up.shape[2]
        for way, part in enumerate((up, down)):
            value = part[0]
            if has_sums:
                value = (value.astype(F32) + sums[way][:, low:high].astype(F32)).astype(BF16)
            if len(outs) == 2:
                outs[way][:, low:high] = value
            elif way == 0:
                outs[0][:upper, low:high] = value
            else:
                outs[0][upper:, low:high] = value
        low = high


def ring_add(parts, owners, upper, sums, final):
    shard_rows = parts[0].shape[1]
    lower = shard_rows - upper
    width = sum(x.shape[2] for x in parts)
    count = len(parts)
    specs = []
    for k, x in enumerate(parts):
        specs.append(pl.BlockSpec((1, upper, x.shape[2]), functools.partial(lambda k, i, own: (own[2 * k], 0, 0), k)))
    for k, x in enumerate(parts):
        at = upper // lower
        specs.append(
            pl.BlockSpec((1, lower, x.shape[2]), functools.partial(lambda k, at, i, own: (own[2 * k + 1], at, 0), k, at))
        )
    whole = lambda rows: pl.BlockSpec((rows, width), lambda i, own: (0, 0))
    if sums is not None:
        specs += [whole(upper), whole(lower)]
    outs = [shard_rows] if final else [upper, lower]
    return pl.pallas_call(
        functools.partial(ring_add_kernel, count, upper, sums is not None),
        grid_spec=pltpu.PrefetchScalarGridSpec(
            num_scalar_prefetch=1, grid=(1,), in_specs=specs, out_specs=[whole(r) for r in outs]
        ),
        out_shape=[jax.ShapeDtypeStruct((r, width), BF16) for r in outs],
        compiler_params=pltpu.CompilerParams(vmem_limit_bytes=VMEM_ADD),
        cost_estimate=pl.CostEstimate(flops=0, bytes_accessed=1_000_000, transcendentals=0),
    )(jnp.stack(owners).astype(jnp.int32), *parts, *parts, *(sums or ()))


def outer_kernel(a, b, out):
    out[...] = dot(a[...], b[...], ((0,), (0,))).astype(BF16)


def outer(a, b, block):
    rows, height = a.shape
    return pl.pallas_call(
        outer_kernel,
        grid=(height // block,),
        in_specs=[pl.BlockSpec((rows, block), lambda i: (0, i)), whole_spec(b.shape)],
        out_specs=pl.BlockSpec((block, b.shape[1]), lambda i: (i, 0)),
        out_shape=jax.ShapeDtypeStruct((height, b.shape[1]), BF16),
        compiler_params=pltpu.CompilerParams(vmem_limit_bytes=VMEM_LIMIT),
        cost_estimate=pl.CostEstimate(flops=0, bytes_accessed=1_000_000, transcendentals=0),
    )(a, b)


def assemble_kernel(cuts, turned, starts, *refs):
    outs, sems = refs[-1 - len(cuts) : -1], refs[-1]
    sources = refs[: -1 - len(cuts)]

    def copies(run):
        for k, source in enumerate(sources):
            for n, (low, high) in enumerate(cuts):
                start = pl.multiple_of(starts[k + len(sources) * (n == turned)], 16)
                run(
                    pltpu.make_async_copy(
                        source.at[:, low:high],
                        outs[n].at[pl.ds(start, source.shape[0])],
                        sems.at[k * len(cuts) + n],
                    )
                )

    copies(lambda copy: copy.start())
    copies(lambda copy: copy.wait())


def assemble(starts, sources, cuts, turned=None, turn=0):
    total = sum(x.shape[0] for x in sources)
    starts = starts + [lax.rem(start + total - turn, total) for start in starts]
    return pl.pallas_call(
        functools.partial(assemble_kernel, cuts, turned),
        in_specs=[pl.BlockSpec(memory_space=pltpu.SMEM)] + [pl.BlockSpec(memory_space=pl.ANY)] * len(sources),
        out_specs=[pl.BlockSpec(memory_space=pltpu.VMEM)] * len(cuts),
        out_shape=[jax.ShapeDtypeStruct((total, high - low), BF16) for low, high in cuts],
        scratch_shapes=[pltpu.SemaphoreType.DMA((len(sources) * len(cuts),))],
        compiler_params=pltpu.CompilerParams(vmem_limit_bytes=VMEM_ALL),
        cost_estimate=pl.CostEstimate(
            flops=0, bytes_accessed=4 * total * sources[0].shape[1], transcendentals=0
        ),
    )(jnp.stack(starts).astype(jnp.int32), *sources)


def quarter_kernel(sizes, where, in_w, out_w, own_ref, other_ref):
    inner_all, state_all, groups, each, heads_all = sizes
    span = each * HALF
    inner = inner_all // 4
    row, core = where[2], where[3]
    tail = in_w[:, 2 * inner_all :]
    spare, depth = LANES - state_all // 4, tail.shape[1]
    for part, ref in ((core, own_ref), (1 - core, other_ref)):
        for base in range(2):
            for group in range(groups):
                pieces = []
                for c in range(2):
                    at = base * inner_all + c * inner_all // 2 + group * 2 * span
                    both = in_w[:, at : at + 2 * span]
                    pieces.append(jnp.where(row == 0, both[:, :span], both[:, span:]))
                ref[:, base * inner + group * span : base * inner + (group + 1) * span] = jnp.where(
                    part == 0, pieces[0], pieces[1]
                )
        source = lax.broadcasted_iota(jnp.int32, (depth, LANES), 0)
        lane = lax.broadcasted_iota(jnp.int32, (depth, LANES), 1)
        group = sum((lane >= g * each).astype(jnp.int32) for g in range(1, groups))
        head = state_all + part * (heads_all // 2) + (2 * group + row) * each + lane - group * each
        state = part * (state_all // 2) + row * (state_all // 4) + lane - spare
        wanted = jnp.where(lane < groups * each, head, jnp.where(lane >= spare, state, -1))
        ref[:, 2 * inner : 2 * inner + LANES] = dot(tail, (source == wanted).astype(BF16)).astype(BF16)
        if out_w is not None:
            half_rows, half = out_w.shape[0] // 2, out_w.shape[1] // 2
            mine = jnp.where(row == 0, out_w[:half_rows, :], out_w[half_rows:, :])
            ref[:, 2 * inner + LANES :] = jnp.where(part == 0, mine[:, :half], mine[:, half:])


def quarters_of(where, in_w, out_w, sizes):
    inner = sizes[0] // 4
    width = 2 * inner + LANES + (0 if out_w is None else out_w.shape[1] // 2)
    spec = pl.BlockSpec(memory_space=pltpu.VMEM)
    kernel = functools.partial(quarter_kernel, sizes)
    args = [where, in_w, out_w]
    if out_w is None:
        args = args[:2]
        inner_kernel = kernel
        kernel = lambda a, b, c, d: inner_kernel(a, b, None, c, d)
    return pl.pallas_call(
        kernel,
        in_specs=[pl.BlockSpec(memory_space=pltpu.SMEM)] + [spec] * (len(args) - 1),
        out_specs=[spec, spec],
        out_shape=[jax.ShapeDtypeStruct((in_w.shape[0], width), BF16)] * 2,
        compiler_params=pltpu.CompilerParams(vmem_limit_bytes=VMEM_LIMIT),
        cost_estimate=pl.CostEstimate(flops=0, bytes_accessed=10_000_000, transcendentals=0),
    )(*args)


def join_kernel(sizes, where, *refs):
    inner_all, state_all, groups, each, heads_all = sizes
    span = each * HALF
    inner = inner_all // 4
    row, core = where[2], where[3]
    has_out = len(refs) > 5
    in_ref = refs[4]
    split = 2 * inner + LANES

    def quarter(sources, c, r, low, high):
        mine, far, came, came_far = sources
        own = jnp.where(row == r, mine[:, low:high], far[:, low:high])
        theirs = jnp.where(row == r, came[:, low:high], came_far[:, low:high])
        return jnp.where(core == c, own, theirs)

    tails = 0.0
    spare, depth = LANES - state_all // 4, state_all + heads_all
    lane = lax.broadcasted_iota(jnp.int32, (LANES, depth), 0)
    target = lax.broadcasted_iota(jnp.int32, (LANES, depth), 1)
    group = sum((lane >= g * each).astype(jnp.int32) for g in range(1, groups))
    for c in range(2):
        for base in range(2):
            for g in range(groups):
                low = base * inner + g * span
                both = [quarter(refs[:4], c, r, low, low + span).astype(F32) for r in range(2)]
                at = base * inner_all + c * inner_all // 2 + g * 2 * span
                in_ref[0, :, at : at + 2 * span] = jnp.concatenate(both, axis=1)
        for r in range(2):
            head = state_all + c * (heads_all // 2) + (2 * group + r) * each + lane - group * each
            state = c * (state_all // 2) + r * (state_all // 4) + lane - spare
            wanted = jnp.where(lane < groups * each, head, jnp.where(lane >= spare, state, -1))
            chosen = (target == wanted).astype(BF16)
            tails = tails + dot(quarter(refs[:4], c, r, 2 * inner, 2 * inner + LANES), chosen)
            if has_out:
                half_rows, half = refs[0].shape[0], refs[0].shape[1] - split
                low = quarter(refs[:4], c, r, split, split + half).astype(F32)
                refs[5][0, r * half_rows : (r + 1) * half_rows, c * half : (c + 1) * half] = low
    in_ref[0, :, 2 * inner_all :] = tails


def join(where, quarters, sizes):
    rows, width = quarters[0].shape
    inner_all, state_all, groups, each, heads_all = sizes
    split = inner_all // 2 + LANES
    shapes = [jax.ShapeDtypeStruct((1, rows, 2 * inner_all + state_all + heads_all), F32)]
    if width > split:
        shapes.append(jax.ShapeDtypeStruct((1, 2 * rows, 2 * (width - split)), F32))
    spec = pl.BlockSpec(memory_space=pltpu.VMEM)
    return pl.pallas_call(
        functools.partial(join_kernel, sizes),
        in_specs=[pl.BlockSpec(memory_space=pltpu.SMEM)] + [spec] * len(quarters),
        out_specs=[spec] * len(shapes),
        out_shape=shapes,
        compiler_params=pltpu.CompilerParams(vmem_limit_bytes=VMEM_LIMIT),
        cost_estimate=pl.CostEstimate(flops=0, bytes_accessed=12_000_000, transcendentals=0),
    )(where, *quarters)


class Links:
    def __init__(self, mesh_shape):
        self.line = mesh_shape["fsdp"] // 2
        at = self.fsdp = lax.axis_index("fsdp")
        self.at = jnp.where(at % 2 == 0, at // 2, 2 * self.line - 1 - at // 2)
        ring = [2 * p for p in range(self.line)] + [2 * p + 1 for p in reversed(range(self.line))]
        self.ahead = [(ring[k - 1], ring[k]) for k in range(len(ring))]
        self.behind = [(after, before) for before, after in self.ahead]
        self.row, self.core = lax.axis_index("dp"), lax.axis_index("section")

    def swap_core(self, x):
        return lax.ppermute(x, "section", [(0, 1), (1, 0)])

    def swap_row(self, x):
        return lax.ppermute(x, "dp", [(0, 1), (1, 0)])

    def swap_side(self, x):
        return lax.ppermute(x, "fsdp", [(2 * p + s, 2 * p + 1 - s) for p in range(self.line) for s in range(2)])

    def mine_of_core(self, first, second):
        return jnp.where(self.core == 0, first, second)

    def in_row_order(self, own, other, axis):
        return jnp.where(
            self.row == 0, jnp.concatenate([own, other], axis), jnp.concatenate([other, own], axis)
        )

    def in_core_order(self, own, other, axis):
        return jnp.where(
            self.core == 0, jnp.concatenate([own, other], axis), jnp.concatenate([other, own], axis)
        )

    def cut(self, x, axis, which, parts=2):
        size = x.shape[axis] // parts
        return lax.dynamic_slice_in_dim(x, which * size, size, axis)

    def upper(self, shard_rows):
        return (shard_rows + 31) // 32 * 16

    def gather(self, piece):
        shard_rows = piece.shape[0]
        upper = self.upper(shard_rows)
        up, down = piece[:upper], piece[upper:]
        sources, starts = [piece], [ring_owner(self.at, self.line) * shard_rows]
        for hop in range(1, 2 * self.line):
            up, down = yield [lax.ppermute(up, "fsdp", self.ahead), lax.ppermute(down, "fsdp", self.behind)]
            sources += [up, down]
            starts.append(ring_owner(self.at - hop, self.line) * shard_rows)
            starts.append(ring_owner(self.at + hop, self.line) * shard_rows + upper)
        return starts, sources

    def scatter(self, shard_rows, parts):
        upper = self.upper(shard_rows)
        sums = None
        for hop in range(1, 2 * self.line):
            owners = []
            for _, f in parts:
                owners += [f(ring_owner(self.at - hop, self.line)), f(ring_owner(self.at + hop, self.line))]
            up, down = ring_add([x for x, _ in parts], owners, upper, sums, False)
            sums = yield [lax.ppermute(up, "fsdp", self.ahead), lax.ppermute(down, "fsdp", self.behind)]
        owners = [f(ring_owner(self.at, self.line)) for _, f in parts for _ in range(2)]
        return ring_add([x for x, _ in parts], owners, upper, sums, True)[0]

    def sum_line(self, x):
        size = self.line
        if size & (size - 1):
            return lax.psum(x, "fsdp") / 2
        by = 1
        while by < size:
            pairs = [(2 * p + s, 2 * (p ^ by) + s) for p in range(size) for s in range(2)]
            x = x + lax.ppermute(x, "fsdp", pairs)
            by *= 2
            if by < size:
                (x,) = yield [x]
        return x


class Schedule:
    def __init__(self, work):
        self.work, self.sent = work, None

    def round(self, parts):
        extra = []
        if self.work is not None:
            try:
                extra = list(self.work.send(self.sent))
            except StopIteration:
                self.work = None
        joined = lax.optimization_barrier(tuple(parts) + tuple(extra))
        self.sent = list(joined[len(parts) :])
        return list(joined[: len(parts)])

    def run(self, moves):
        sent = None
        while True:
            try:
                parts = moves.send(sent)
            except StopIteration as stop:
                return stop.value
            sent = self.round(parts)


def body(mesh_shape, inputs, seq_lengths, norm_gain, in_w, conv_w, conv_b, dt_bias, a_log, skip, out_gain, out_w, cotangent):
    links = Links(mesh_shape)
    core, row = links.core, links.row
    shards = mesh_shape["fsdp"]
    width = inputs.shape[1]
    half_width = width // 2
    own_tokens = inputs.shape[0]
    tokens = 2 * own_tokens
    rows = own_tokens // seq_lengths.shape[0]
    inner_all = out_gain.shape[1]
    heads_all = a_log.shape[1]
    head_dim = inner_all // heads_all
    taps, channels = conv_w.shape[1:]
    state_all = channels - inner_all
    state_own = state_all // 4
    heads = heads_all // 4
    inner = inner_all // 4
    split = 2 * inner + LANES
    shard_rows = in_w.shape[1]
    direct = heads_all % shards == 0 and (heads_all // shards) % 2 == 0
    groups = shards // 2 if direct else 1
    each = heads // groups
    span = each * head_dim
    sizes = (inner_all, state_all, groups, each, heads_all)

    def pick_row(x, axis):
        return jnp.where(row == 0, lax.index_in_dim(x, 0, axis, False), lax.index_in_dim(x, 1, axis, False))

    def pick(x, axis):
        return links.mine_of_core(lax.index_in_dim(x, 0, axis, False), lax.index_in_dim(x, 1, axis, False))

    def wide_part(x):
        x = pick(x.reshape(x.shape[0], 2, groups, 2, span), 1)
        return pick_row(x, 2).reshape(x.shape[0], inner)

    def head_part(x):
        x = pick(x.reshape(x.shape[0], 2, groups, 2, each), 1)
        return pick_row(x, 2).reshape(x.shape[0], heads)

    def state_part(x):
        x = pick(x.reshape(x.shape[0], 2, 2, state_own), 1)
        return pick_row(x, 1)

    def wide_row(x):
        return jnp.pad(x, ((0, 0), (0, channels - x.shape[1])))

    zero = jnp.int32(0)
    where = jnp.stack([zero, zero, row, core]).astype(jnp.int32)
    own_part, other_part = quarters_of(where, in_w[0], out_w[0] if direct else None, sizes)
    came_part = links.swap_core(other_part)
    both = (links.mine_of_core(own_part, came_part), links.mine_of_core(came_part, own_part))
    if not direct:
        out_first, out_second = out_w[0][:, :half_width], out_w[0][:, half_width:]
        kept = links.mine_of_core(out_first, out_second)
        came = links.swap_core(links.mine_of_core(out_second, out_first))
        out_pieces = (links.mine_of_core(kept, came), links.mine_of_core(came, kept))
    pieces = list(both)

    packed = jnp.concatenate(
        [conv_w[0], conv_b, wide_row(out_gain), wide_row(norm_gain), wide_row(dt_bias), wide_row(a_log), wide_row(skip)],
        axis=0,
    )
    packed_other = links.swap_core(packed)
    all_lengths = links.in_row_order(seq_lengths, links.swap_row(seq_lengths), 0)
    sent_tokens, pieces[0], all_lengths, packed_other = lax.optimization_barrier(
        (inputs, pieces[0], all_lengths, packed_other)
    )

    def layer_params(pack):
        cw, cb = pack[:taps], pack[taps : taps + 1]
        og, ng = pack[taps + 1 : taps + 2, :inner_all], pack[taps + 2 : taps + 3, :width]
        dt, al, sk = (pack[taps + 3 + k : taps + 4 + k, :heads_all] for k in range(3))
        lanes = inner + state_all
        fill = lambda x: jnp.pad(x, ((0, 0), (0, lanes - x.shape[1])))
        conv = jnp.concatenate([cw, cb], axis=0)
        narrow = jnp.concatenate([head_part(dt), -jnp.exp(head_part(al))], axis=0)
        narrow = jnp.pad(narrow, ((0, 0), (0, LANES - heads))).reshape(1, 2 * LANES)
        own_state = jnp.pad(state_part(conv[:, inner_all:]), ((0, 0), (LANES - state_own, 0)))
        rows_ = [
            jnp.concatenate([wide_part(conv[:, :inner_all]), conv[:, inner_all:]], axis=1),
            fill(wide_part(og)),
            fill(jnp.repeat(head_part(sk), head_dim, axis=1)),
            fill(narrow),
            fill(own_state),
        ]
        return fill(jnp.concatenate([jnp.concatenate(rows_, axis=0), jnp.zeros((16 - 2 * taps - 5, lanes), F32)], axis=0)), ng

    blocks = tokens // rows
    big = {}

    def to_rows(x):
        return x.reshape(-1, LANES)

    def norm_of(u):
        return lax.rsqrt(jnp.mean(u * u, axis=-1, keepdims=True) + 1e-05)

    def over_cores(x):
        return links.cut(x, 1, core) + links.swap_core(links.cut(x, 1, 1 - core))

    def own_rows(x):
        return links.cut(x, 0, row)

    def norm_back(u, gain, d_scaled):
        u = u.astype(F32)
        inverse = norm_of(u)
        meet = jnp.mean(u * gain * d_scaled, axis=1, keepdims=True)
        return inverse * gain * d_scaled - u * (inverse * inverse * inverse * meet)

    def gain_back(u, d_scaled):
        u = u.astype(F32)
        return jnp.sum(u * norm_of(u) * d_scaled, axis=0, keepdims=True)

    def scaled_of(u, gain):
        u = u.astype(F32)
        return (u * norm_of(u) * gain).astype(BF16)

    def out_whole(pieces):
        half = pieces.shape[0] // 2
        kept, sent = (pieces[:half], pieces[half:]) if direct else (links.cut(pieces, 0, core), links.cut(pieces, 0, 1 - core))
        return links.in_core_order(kept, links.swap_core(sent), 1)

    def project(layer, scaled):
        wide_w, last_w = big["in", layer]
        last = dot(scaled, last_w)
        came = links.swap_row(last[:, LANES - state_own :])
        proj = dot(scaled, wide_w)
        proj, last, came = yield [proj, last, came]
        part = links.in_row_order(last[:, LANES - state_own :], came, 1)
        bc = links.in_core_order(part, links.swap_core(part), 1)
        return proj, last, bc

    def mix(layer, proj, last, bc):
        outs, gated, squares = ahead_call(heads, taps, rows, proj, last, bc, aux, seg_rows, big["pack", layer])
        return outs, gated, to_rows(squares[:, 0])

    def over_all(x):
        x = x + links.swap_core(x)
        return x + links.swap_row(x)

    def inverse_of(squares):
        return lax.rsqrt(squares / inner_all + 1e-05)

    def as_columns(*rows_):
        return jnp.stack([x.reshape(tokens) for x in rows_]).T

    def normed_of(layer, gated, inverse):
        gain = big["pack", layer][taps + 1 : taps + 2, :inner]
        normed = (gated * inverse.reshape(tokens, 1) * gain).astype(BF16)
        other = links.swap_core(normed)
        return jnp.concatenate([normed, other], axis=1) if direct else links.in_core_order(normed, other, 1)

    def back_mix(layer, kept, d_normed, meet):
        scale = as_columns(kept["inverse"], kept["inverse"] * meet / inner_all)
        return back_call(
            heads, taps, rows, kept["proj"], kept["last"], kept["bc"], aux, seg_rows, big["pack", layer],
            kept["outs"], d_normed, scale,
        )

    def back_project(layer, kept, d_main, d_dt, d_bc):
        wide_w, last_w = big["in", layer]
        d_bc = over_cores(d_bc)
        d_scaled = dot(d_main, wide_w, ((1,), (1,)))
        d_bc, d_scaled = yield [d_bc, d_scaled]
        d_bc = links.cut(d_bc, 1, row) + links.swap_row(links.cut(d_bc, 1, 1 - row))
        d_in = outer(kept["scaled"], d_main, width // 3)
        d_bc, d_in = yield [d_bc, d_in]
        d_bc = jnp.pad(d_bc, ((0, 0), (LANES - d_bc.shape[1], 0)))
        d_last, d_state = state_back_call(taps, d_bc, kept["last"], aux, big["pack", layer], d_dt)
        d_in_last = dot(kept["scaled"], d_last, ((0,), (0,))).astype(BF16)
        d_scaled = d_scaled + dot(d_last, last_w, ((1,), (1,)))
        return d_scaled, d_in, d_in_last, d_state

    def out_grad(normed, grad_half):
        return dot(normed, grad_half, ((0,), (0,))).astype(BF16)

    aux = seg_rows = None
    done = {}

    def send_out(layer, d_out):
        done["out", layer] = d_out

    def work():
        nonlocal aux, seg_rows
        pack0, gain0 = layer_params(links.mine_of_core(packed, packed_other))
        pack1, gain1 = layer_params(links.mine_of_core(packed_other, packed))
        ends = jnp.cumsum(all_lengths, axis=1)
        positions = jnp.arange(rows, dtype=jnp.int32)
        segments = jnp.sum((positions[None, :, None] >= ends[:, None, :]).astype(jnp.int32), axis=2)
        aux, seg_rows = make_aux(segments, rows, taps), segments.astype(F32)[:, None, :]
        came_tokens = links.swap_row(sent_tokens)
        pack0, pack1, gain0, gain1, aux, seg_rows = yield [pack0, pack1, gain0, gain1, aux, seg_rows]
        big["pack", 0], big["pack", 1] = pack0, pack1
        (came_tokens,) = yield [came_tokens]
        tokens_all = links.in_row_order(inputs, came_tokens, 0)
        scaled = scaled_of(tokens_all, gain0)
        sent_cot, _ = lax.optimization_barrier((cotangent, came_tokens))
        came_cot = links.swap_row(sent_cot)
        tokens_all, scaled = yield [tokens_all, scaled]
        yield [scaled]
        cot_all = links.in_row_order(cotangent, came_cot, 0)
        cot_half = links.cut(cot_all, 1, core)
        cot_all, cot_half = yield [cot_all, cot_half]
        while ("in", 0) not in big:
            yield [scaled]
        wide_w, last_w = big["in", 0]
        if direct:
            wide_w, last_w, big["out", 0] = yield [wide_w, last_w, big["out", 0]]
        else:
            wide_w, last_w = yield [wide_w, last_w]
        big["in", 0] = wide_w, last_w
        proj, last, bc = yield from project(0, scaled)
        outs, gated, squares = mix(0, proj, last, bc)
        bc, outs, gated, squares = yield [bc, outs, gated, squares]
        (squares,) = yield [over_all(squares)]
        inverse = inverse_of(squares)
        normed = normed_of(0, gated, inverse)
        while ("out", 0) not in big:
            yield [normed]
        branch = dot(normed, big["out", 0]).astype(BF16)
        came = links.swap_row(branch)
        normed, inverse, branch = yield [normed, inverse, branch]
        kept0 = {"scaled": scaled, "proj": proj, "last": last, "bc": bc, "outs": outs, "inverse": inverse}
        big["out_whole", 0] = out_whole(big["out", 0])
        came, big["out_whole", 0] = yield [came, big["out_whole", 0]]
        normed0 = normed
        while ("in", 1) not in big or ("out", 1) not in big:
            yield [came]
        branch = branch.astype(F32) + came.astype(F32)
        first = (links.cut(tokens_all, 1, core).astype(F32) + branch).astype(BF16)
        first = links.in_core_order(first, links.swap_core(first), 1)
        scaled = scaled_of(first, gain1)
        big["out_whole", 1] = out_whole(big["out", 1])
        proj, last, bc = yield from project(1, scaled)
        d_normed = dot(cot_all, big["out_whole", 1], ((1,), (1,)))
        outs, gated, squares = mix(1, proj, last, bc)
        gain = big["pack", 1][taps + 1 : taps + 2, :inner]
        meet = to_rows(jnp.sum(gated * gain * d_normed, axis=1))
        both_sums = over_all(jnp.concatenate([squares, meet], axis=0))
        bc, outs, gated, d_normed, both_sums = yield [bc, outs, gated, d_normed, both_sums]
        squares, meet = both_sums[: squares.shape[0]], both_sums[squares.shape[0] :]
        inverse = inverse_of(squares)
        kept1 = {"scaled": scaled, "proj": proj, "last": last, "bc": bc, "outs": outs, "inverse": inverse}
        found = back_mix(1, kept1, d_normed, inverse * inverse * meet)
        d_main, d_dt, d_bc, d_wide1, d_narrow1 = yield list(found)
        normed1 = normed_of(1, gated, inverse)
        d_out = out_grad(normed1, cot_half)
        d_scaled, d_in, d_in_last, d_state1 = yield from back_project(1, kept1, d_main, d_dt, d_bc)
        d_scaled, d_in, d_in_last, d_out = yield [d_scaled, d_in, d_in_last, d_out]
        done["in", 1] = d_in, d_in_last
        send_out(1, d_out)
        small1 = jnp.sum(d_wide1, axis=0), jnp.sum(d_narrow1, axis=0), d_state1
        d_scaled = over_cores(d_scaled).astype(BF16)
        came = links.swap_row(d_scaled)
        (d_scaled,) = yield [d_scaled]
        (came,) = yield [came]
        d_scaled = d_scaled.astype(F32) + came.astype(F32)
        d_scaled = links.in_core_order(d_scaled, links.swap_core(d_scaled), 1)
        grad = (cot_all.astype(F32) + norm_back(first, gain1, d_scaled)).astype(BF16)
        gain_sum1 = gain_back(own_rows(first), own_rows(d_scaled))
        grad, gain_sum1 = yield [grad, gain_sum1]
        grad_half = links.cut(grad, 1, core)
        meet = to_rows(jnp.sum(branch * grad_half.astype(F32), axis=1))
        meet = meet + links.swap_core(meet)
        d_normed = dot(grad, big["out_whole", 0], ((1,), (1,)))
        d_normed, meet, grad_half = yield [d_normed, meet, grad_half]
        found = back_mix(0, kept0, d_normed, kept0["inverse"] * meet)
        d_main, d_dt, d_bc, d_wide0, d_narrow0 = yield list(found)
        d_out = out_grad(normed0, grad_half)
        d_scaled, d_in, d_in_last, d_state0 = yield from back_project(0, kept0, d_main, d_dt, d_bc)
        d_scaled, d_in, d_in_last, d_out = yield [d_scaled, d_in, d_in_last, d_out]
        done["in", 0] = d_in, d_in_last
        send_out(0, d_out)
        small0 = jnp.sum(d_wide0, axis=0), jnp.sum(d_narrow0, axis=0), d_state0
        while ("sum", 1) not in done:
            yield [d_scaled]
        far_upper = links.swap_row(done["sum", 1][: shard_rows // 2])
        d_scaled = over_cores(d_scaled)
        d_scaled, far_upper = yield [d_scaled, far_upper]
        came = links.swap_row(links.cut(d_scaled, 0, 1 - row).astype(BF16))
        partial = dot(normed1, big["out", 1])
        came, partial = yield [came, partial]
        far_lower = links.swap_row(done["sum", 1][shard_rows // 2 :])
        d_scaled = own_rows(d_scaled) + came.astype(F32)
        d_scaled = links.in_core_order(d_scaled, links.swap_core(d_scaled), 1)
        own_grad = own_rows(grad)
        grad_in = (own_grad.astype(F32) + norm_back(inputs, gain0, d_scaled)).astype(BF16)
        gain_sum0 = gain_back(inputs, d_scaled)
        done["input_grad"] = jnp.where(core == 0, grad_in, own_grad)[None]
        done["input_grad"], gain_sum0, far_lower = yield [done["input_grad"], gain_sum0, far_lower]
        done["far", 1] = jnp.concatenate([far_upper, far_lower], axis=0)
        came = links.swap_row(links.cut(partial, 0, 1 - row).astype(BF16))
        small = jnp.concatenate([pack_small(*small0, gain_sum0), pack_small(*small1, gain_sum1)], axis=0)
        small = small + links.swap_side(small)
        came, small = yield [came, small]
        second = own_rows(partial) + came.astype(F32) + links.cut(own_rows(first), 1, core).astype(F32)
        second = second.astype(BF16)
        second = links.in_core_order(second, links.swap_core(second), 1)
        done["phase_out"] = jnp.where(core == 0, own_rows(first), second)[None]
        small = yield from links.sum_line(small)
        done["phase_out"], small = yield [done["phase_out"], small]
        small_other = links.swap_row(small)
        done["small"] = spread_small(small, small_other)
        done["small"] = yield list(done["small"])

    gain_rows = width // inner

    def pack_small(wide_, narrow, d_state, gain):
        gain = gain.reshape(-1, inner)
        narrow_rows = jnp.concatenate([narrow[:2], d_state[: taps + 1]], axis=0)
        narrow_rows = jnp.pad(narrow_rows.reshape(1, -1), ((0, 0), (0, 2 * inner - narrow_rows.size)))
        return jnp.concatenate([wide_[: taps + 3], gain, narrow_rows.reshape(2, inner)], axis=0)

    def by_row(a, b):
        return jnp.where(row == 0, jnp.stack([a, b]), jnp.stack([b, a]))

    def spread_small(small, small_other):
        per = small.shape[0] // 2
        mine = links.mine_of_core(small[:per], small[per:])
        mine_other = links.mine_of_core(small_other[:per], small_other[per:])
        theirs = links.mine_of_core(small[per:], small[:per])
        theirs_other = links.mine_of_core(small_other[per:], small_other[:per])
        came = links.swap_core(jnp.stack([theirs, theirs_other]))
        own_parts, came_parts = by_row(mine, mine_other), by_row(came[0], came[1])
        quarters = jnp.where(core == 0, jnp.stack([own_parts, came_parts]), jnp.stack([came_parts, own_parts]))

        def spread_wide(x):
            lead = x.shape[2:-1]
            x = x.reshape((2, 2) + lead + (groups, span))
            x = jnp.moveaxis(x, (0, 1), (len(lead), len(lead) + 2))
            return x.reshape(lead + (inner_all,))

        def spread_heads(x):
            x = x.reshape((2, 2, groups, each))
            return jnp.moveaxis(x, 1, 2).reshape(1, heads_all)

        grad_norm = mine[taps + 3 : taps + 3 + gain_rows] + mine_other[taps + 3 : taps + 3 + gain_rows]
        narrow = quarters[:, :, taps + 3 + gain_rows :].reshape(2, 2, -1)
        narrow = narrow[:, :, : (taps + 3) * LANES].reshape(2, 2, taps + 3, LANES)
        states = jnp.moveaxis(narrow[:, :, 2:, LANES - state_own :], 2, 0).reshape(taps + 1, state_all)
        wide_full = spread_wide(quarters[:, :, : taps + 3])
        return [
            grad_norm.reshape(1, width),
            jnp.concatenate([wide_full[:taps], states[:taps]], axis=1)[None],
            jnp.concatenate([wide_full[taps : taps + 1], states[taps:]], axis=1),
            spread_heads(narrow[:, :, 0, :heads]),
            spread_heads(narrow[:, :, 1, :heads]),
            wide_full[taps + 1].reshape(1, heads_all, head_dim).sum(axis=-1),
            wide_full[taps + 2 : taps + 3],
        ]

    schedule = Schedule(work())

    def gather(layer):
        cuts = [(0, 2 * inner), (2 * inner, split)] + ([(split, split + half_width)] if direct else [])
        full = assemble(*schedule.run(links.gather(pieces[layer])), cuts, 2, core * (shards // 2 * shard_rows))
        if direct:
            big["out", layer] = full[2]
        else:
            big["out", layer] = out_gathered(layer)
        big["in", layer] = full[:2]

    def scatter(layer):
        while ("in", layer) not in done:
            schedule.round([])
        parts = list(done["in", layer])
        if direct:
            parts.append(done["out", layer])
        else:
            sums = done["out", layer].reshape(2, 1, inner, half_width)
            sums = links.in_row_order(sums, jnp.zeros_like(sums), 1).reshape(4 * inner, half_width)
            sums = lax.psum_scatter(sums, "fsdp", scatter_dimension=0, tiled=True)
            done["out_sum", layer] = (sums.astype(F32) + links.swap_row(sums).astype(F32)).astype(BF16)
        by_core = (lambda f: jnp.where(core == 0, f, (f + shards // 2) % shards)) if direct else (lambda f: f)
        laid = [lambda f: f, lambda f: f, by_core]
        parts = [(x.reshape(shards, shard_rows, -1), f) for x, f in zip(parts, laid)]
        done["sum", layer] = schedule.run(links.scatter(shard_rows, parts))

    def out_gathered(layer):
        full = lax.all_gather(out_pieces[layer], "fsdp", axis=0, tiled=True)
        return pick_row(full.reshape(2, 2, inner, half_width), 1).reshape(2 * inner, half_width)

    gather(0)
    gather(1)
    scatter(1)
    scatter(0)
    while schedule.work is not None:
        schedule.round([])

    low0, low1, far1 = done["sum", 0], done["sum", 1], done["far", 1]
    theirs = links.swap_core(links.mine_of_core(low1, low0))
    far0 = links.swap_row(low0)
    quarters = [links.mine_of_core(low0, low1), links.mine_of_core(far0, far1)]
    quarters += [theirs, links.swap_core(links.mine_of_core(far1, far0))]
    if direct:
        grad_in_w, grad_out_w = join(where, quarters, sizes)
    else:
        (grad_in_w,) = join(where, quarters, sizes)
        out0, out1 = done["out_sum", 0], done["out_sum", 1]
        theirs = links.swap_core(links.mine_of_core(out1, out0))
        grad_out_w = links.in_core_order(links.mine_of_core(out0, out1), theirs, 1).astype(F32)[None]
    grad_norm, grad_conv_w, grad_conv_b, grad_dt, grad_a, grad_skip, grad_out_gain = done["small"]
    return (
        done["phase_out"], done["input_grad"], grad_norm, grad_in_w, grad_conv_w, grad_conv_b,
        grad_dt, grad_a, grad_skip, grad_out_gain, grad_out_w,
    )


def solution(mesh):
    return jax.shard_map(
        functools.partial(body, dict(mesh.shape)),
        mesh=mesh,
        in_specs=(
            P(("fsdp", "dp"), None),
            P(("fsdp", "dp"), None),
            P("section", None),
            P("section", "fsdp", None),
            P("section", None, None),
            P("section", None),
            P("section", None),
            P("section", None),
            P("section", None),
            P("section", None),
            P("section", "fsdp", None),
            P(("fsdp", "dp"), None),
        ),
        out_specs=(
            P("section", ("fsdp", "dp"), None),
            P("section", ("fsdp", "dp"), None),
            P("section", None),
            P("section", "fsdp", None),
            P("section", None, None),
            P("section", None),
            P("section", None),
            P("section", None),
            P("section", None),
            P("section", None),
            P("section", "fsdp", None),
        ),
        check_vma=False,
    )
```

```python
import functools

import jax
import jax.numpy as jnp
from jax import lax
from jax.experimental import pallas as pl
from jax.experimental.pallas import tpu as pltpu
from jax.sharding import PartitionSpec as P

F32 = jnp.float32
BF16 = jnp.bfloat16
LANES = 128
HALF = 64
VMEM_LIMIT = 40 * 1024 * 1024
VMEM_ALL = 60 * 1024 * 1024
VMEM_ADD = 16 * 1024 * 1024
ROOM = 12


def dot(a, b, dims=((1,), (0,)), precision=None):
    return lax.dot_general(a, b, (dims, ((), ())), precision=precision, preferred_element_type=F32)


def dot_exact(a, b, dims=((1,), (0,))):
    return dot(a, b, dims, lax.Precision.HIGHEST)


def silu_parts(x):
    gate = 1.0 / (1.0 + jnp.exp(-x))
    return gate, x * gate


def softplus(x):
    return jnp.maximum(x, 0.0) + jnp.log1p(jnp.exp(-jnp.abs(x)))


def conv_mixed(conv_in, aux, conv_w, conv_b):
    taps = conv_w.shape[0]
    mixed = conv_b + conv_w[taps - 1 : taps] * conv_in
    shifted = []
    for back in range(1, taps):
        moved = pltpu.roll(conv_in, back, 0) * aux[:, back : back + 1]
        shifted.append(moved)
        mixed = mixed + conv_w[taps - 1 - back : taps - back] * moved
    return mixed, shifted


def conv_back(d_mixed, conv_in, shifted, aux, conv_w):
    taps = conv_w.shape[0]
    rows = d_mixed.shape[0]
    d_in = conv_w[taps - 1 : taps] * d_mixed
    d_w = [None] * taps
    d_w[taps - 1] = jnp.sum(d_mixed * conv_in, axis=0, keepdims=True)
    for back in range(1, taps):
        ahead = pltpu.roll(d_mixed, rows - back, 0) * aux[:, taps - 1 + back : taps + back]
        d_in = d_in + conv_w[taps - 1 - back : taps - back] * ahead
        d_w[taps - 1 - back] = jnp.sum(d_mixed * shifted[back - 1], axis=0, keepdims=True)
    return d_in, d_w, jnp.sum(d_mixed, axis=0, keepdims=True)


def decays(last, dt_bias, neg_rate, aux, seg_row):
    rows = last.shape[0]
    step = softplus(last + dt_bias)
    row = lax.broadcasted_iota(jnp.int32, (rows, rows), 0)
    col = lax.broadcasted_iota(jnp.int32, (rows, rows), 1)
    lower = row >= col
    log_decay = dot_exact(lower.astype(F32), neg_rate * step)
    allowed = lower & (aux[:, 0:1] == seg_row)
    return step, log_decay, allowed, lower


def pair_masks(rows):
    lane = lax.broadcasted_iota(jnp.int32, (rows, LANES), 1)
    return (lane < HALF).astype(F32), (lane >= HALF).astype(F32)


def unpack(packed, taps, heads):
    inner = heads * HALF
    conv_w, conv_b = packed[:taps, :], packed[taps : taps + 1, :]
    out_gain, skip = packed[taps + 1 : taps + 2, :inner], packed[taps + 2 : taps + 3, :inner]
    dt_bias, neg_rate = packed[taps + 3 : taps + 4, :LANES], packed[taps + 3 : taps + 4, LANES : 2 * LANES]
    return conv_w, conv_b, dt_bias, neg_rate, skip, out_gain


def ahead_kernel(heads, taps, proj, last, bc, aux, seg_row, packed, outs_ref, gated_ref, square_ref):
    rows = proj.shape[0]
    conv_w, conv_b, dt_bias, neg_rate, skip, _ = unpack(packed, taps, heads)
    inner = heads * HALF
    aux_v = aux[...]
    values_mixed, _ = conv_mixed(proj[:, inner : 2 * inner], aux_v, conv_w[:, :inner], conv_b[:, :inner])
    _, values = silu_parts(values_mixed)
    state_mixed, _ = conv_mixed(bc[...], aux_v, conv_w[:, inner:], conv_b[:, inner:])
    _, state = silu_parts(state_mixed)
    in_state, out_state = state[:, :LANES].astype(BF16), state[:, LANES:].astype(BF16)
    step, log_decay, allowed, _ = decays(
        last[...], dt_bias, neg_rate, aux_v, seg_row[0]
    )
    step_t, log_t = step.T, log_decay.T
    inter = dot(out_state, in_state, ((1,), (1,)))
    first, second = pair_masks(rows)
    squares = jnp.zeros((rows, 1), F32)
    for pair in range(heads // 2):
        weights = []
        for h in (2 * pair, 2 * pair + 1):
            gap = log_decay[:, h : h + 1] - log_t[h : h + 1]
            decay = jnp.exp(jnp.where(allowed, gap, -1e30))
            weights.append((inter * decay * step_t[h : h + 1]).astype(BF16))
        at = slice(pair * LANES, (pair + 1) * LANES)
        own = values[:, at]
        low = own.astype(BF16).astype(F32)
        both = jnp.concatenate([low * first, low * second], axis=0).astype(BF16)
        carried = dot(jnp.concatenate(weights, axis=1), both)
        outs = carried + skip[:, at] * own
        _, gate = silu_parts(proj[:, at])
        gated = outs * gate
        outs_ref[:, at] = outs
        gated_ref[:, at] = gated
        squares = squares + jnp.sum(gated * gated, axis=1, keepdims=True)
    square_ref[...] = jnp.broadcast_to(squares, square_ref.shape)


def back_kernel(
    heads, taps, proj, last_ref, bc, aux, seg_row, packed, outs, d_normed, scale, *results
):
    d_main_ref, d_dt_ref, d_state_ref, d_wide_ref, d_narrow_ref = results
    rows = proj.shape[0]
    conv_w, conv_b, dt_bias, neg_rate, skip, out_gain = unpack(packed, taps, heads)
    inner = heads * HALF
    aux_v = aux[...]
    values_in = proj[:, inner : 2 * inner]
    values_mixed, values_shifted = conv_mixed(values_in, aux_v, conv_w[:, :inner], conv_b[:, :inner])
    values_gate, values = silu_parts(values_mixed)
    state_mixed, _ = conv_mixed(bc[...], aux_v, conv_w[:, inner:], conv_b[:, inner:])
    _, state = silu_parts(state_mixed)
    in_state, out_state = state[:, :LANES].astype(BF16), state[:, LANES:].astype(BF16)
    last = last_ref[...]
    step, log_decay, allowed, lower = decays(last, dt_bias, neg_rate, aux_v, seg_row[0])
    step_t, log_t = step.T, log_decay.T
    inter = dot(out_state, in_state, ((1,), (1,)))
    first, second = pair_masks(rows)
    lane = lax.broadcasted_iota(jnp.int32, (rows, LANES), 1)
    sub = lax.broadcasted_iota(jnp.int32, (LANES, rows), 0)
    inverse, shrink = scale[:, 0:1], scale[:, 1:2]
    d_inter = jnp.zeros((rows, rows), F32)
    row_sums = jnp.zeros((rows, LANES), F32)
    col_sums = jnp.zeros((LANES, rows), F32)
    d_skip, d_gain, d_values = [], [], []
    for pair in range(heads // 2):
        at = slice(pair * LANES, (pair + 1) * LANES)
        own = values[:, at]
        low = own.astype(BF16)
        gate_in = proj[:, at]
        sig, gate = silu_parts(gate_in)
        outs_at = outs[:, at]
        gated = outs_at * gate
        dn = d_normed[:, at]
        d_gain.append(jnp.sum(gated * inverse * dn, axis=0, keepdims=True))
        d_gated = inverse * (out_gain[:, at] * dn) - gated * shrink
        d_outs = d_gated * gate
        d_main_ref[:, at] = (d_gated * outs_at * (sig * (1.0 + gate_in * (1.0 - sig)))).astype(BF16)
        d_skip.append(jnp.sum(d_outs * own, axis=0, keepdims=True))
        d_both = jnp.concatenate([d_outs * first, d_outs * second], axis=0).astype(BF16)
        d_weights = dot(d_both, low, ((1,), (1,)))
        weights = []
        for k, h in enumerate((2 * pair, 2 * pair + 1)):
            gap = log_decay[:, h : h + 1] - log_t[h : h + 1]
            decay = jnp.exp(jnp.where(allowed, gap, -1e30))
            step_row = step_t[h : h + 1]
            weights.append((inter * decay * step_row).astype(BF16))
            part = d_weights[k * rows : (k + 1) * rows] * decay
            d_inter = d_inter + part * step_row
            part = part * inter
            col = jnp.sum(part, axis=0, keepdims=True)
            col_sums = jnp.where(sub == h, col, col_sums)
            row_sum = jnp.sum(part * step_row, axis=1, keepdims=True)
            row_sums = jnp.where(lane == h, row_sum, row_sums)
        d_low = dot(jnp.concatenate(weights, axis=0), d_both, ((0,), (0,)))
        d_values.append(skip[:, at] * d_outs + d_low)
    d_values = jnp.concatenate(d_values, axis=1)
    d_mixed = d_values * (values_gate * (1.0 + values_mixed * (1.0 - values_gate)))
    d_in, d_w, d_b = conv_back(d_mixed, values_in, values_shifted, aux_v, conv_w[:, :inner])
    d_main_ref[:, inner : 2 * inner] = d_in.astype(BF16)
    low_inter = d_inter.astype(BF16)
    d_state_ref[:, :LANES] = dot(low_inter, out_state, ((0,), (0,)))
    d_state_ref[:, LANES:] = dot(low_inter, in_state)
    direct = col_sums.T
    d_log = row_sums - direct * step
    d_pace = dot_exact(lower.astype(F32), d_log, ((0,), (0,)))
    d_step = direct + d_pace * neg_rate
    d_last = jnp.where(lane < heads, d_step * (1.0 / (1.0 + jnp.exp(-(last + dt_bias)))), 0.0)
    d_dt_ref[...] = d_last
    wide = d_w + [d_b, jnp.concatenate(d_skip, axis=1), jnp.concatenate(d_gain, axis=1)]
    wide.append(jnp.zeros((d_wide_ref.shape[1] - len(wide), inner), F32))
    d_wide_ref[0] = jnp.concatenate(wide, axis=0)
    d_rate = jnp.sum(d_pace * neg_rate * step, axis=0, keepdims=True)
    narrow = [
        jnp.sum(d_last, axis=0, keepdims=True),
        jnp.where(lane[:1] < heads, d_rate, 0.0),
        jnp.zeros((d_narrow_ref.shape[1] - 2, LANES), F32),
    ]
    d_narrow_ref[0] = jnp.concatenate(narrow, axis=0)


def state_back_kernel(taps, d_act, last, aux, packed, d_dt, d_proj_ref, d_sums_ref):
    aux_v = aux[...]
    last_v = last[...]
    conv_w, conv_b = packed[8 : 8 + taps, :LANES], packed[8 + taps : 9 + taps, :LANES]
    mixed, shifted = conv_mixed(last_v, aux_v, conv_w, conv_b)
    sig, _ = silu_parts(mixed)
    d_mixed = d_act[...] * (sig * (1.0 + mixed * (1.0 - sig)))
    d_in, d_w, d_b = conv_back(d_mixed, last_v, shifted, aux_v, conv_w)
    lane = lax.broadcasted_iota(jnp.int32, last_v.shape, 1)
    d_proj_ref[...] = jnp.where(lane < HALF, d_dt[...], d_in).astype(BF16)
    sums = d_w + [d_b]
    sums.append(jnp.zeros((d_sums_ref.shape[0] - len(sums), LANES), F32))
    d_sums_ref[...] = jnp.concatenate(sums, axis=0)


def rows_spec(rows, width):
    return pl.BlockSpec((rows, width), lambda i: (i, 0))


def whole_spec(shape):
    return pl.BlockSpec(shape, lambda i: (0,) * len(shape))


def ahead_call(heads, taps, rows, proj, last, bc, aux, seg_rows, packed):
    total = proj.shape[0]
    inner = heads * HALF
    count = total // rows
    return pl.pallas_call(
        functools.partial(ahead_kernel, heads, taps),
        grid=(count,),
        in_specs=[
            rows_spec(rows, proj.shape[1]),
            rows_spec(rows, LANES),
            rows_spec(rows, bc.shape[1]),
            rows_spec(rows, aux.shape[1]),
            pl.BlockSpec((1, 1, rows), lambda i: (i, 0, 0)),
            whole_spec(packed.shape),
        ],
        out_specs=[rows_spec(rows, inner), rows_spec(rows, inner), rows_spec(rows, LANES)],
        out_shape=[
            jax.ShapeDtypeStruct((total, inner), F32),
            jax.ShapeDtypeStruct((total, inner), F32),
            jax.ShapeDtypeStruct((total, LANES), F32),
        ],
        compiler_params=pltpu.CompilerParams(vmem_limit_bytes=VMEM_LIMIT),
        cost_estimate=pl.CostEstimate(
            flops=count * 1_000_000_000, bytes_accessed=count * 2_000_000, transcendentals=count * 400_000
        ),
    )(proj, last, bc, aux, seg_rows, packed)


def back_call(heads, taps, rows, proj, last, bc, aux, seg_rows, packed, outs, d_normed, scale):
    total = proj.shape[0]
    inner = heads * HALF
    count = total // rows
    return pl.pallas_call(
        functools.partial(back_kernel, heads, taps),
        grid=(count,),
        in_specs=[
            rows_spec(rows, proj.shape[1]),
            rows_spec(rows, LANES),
            rows_spec(rows, bc.shape[1]),
            rows_spec(rows, aux.shape[1]),
            pl.BlockSpec((1, 1, rows), lambda i: (i, 0, 0)),
            whole_spec(packed.shape),
            rows_spec(rows, inner),
            rows_spec(rows, inner),
            rows_spec(rows, 2),
        ],
        out_specs=[
            rows_spec(rows, 2 * inner),
            rows_spec(rows, LANES),
            rows_spec(rows, bc.shape[1]),
            pl.BlockSpec((1, 8, inner), lambda i: (i, 0, 0)),
            pl.BlockSpec((1, 8, LANES), lambda i: (i, 0, 0)),
        ],
        out_shape=[
            jax.ShapeDtypeStruct((total, 2 * inner), BF16),
            jax.ShapeDtypeStruct((total, LANES), F32),
            jax.ShapeDtypeStruct((total, bc.shape[1]), F32),
            jax.ShapeDtypeStruct((count, 8, inner), F32),
            jax.ShapeDtypeStruct((count, 8, LANES), F32),
        ],
        compiler_params=pltpu.CompilerParams(vmem_limit_bytes=VMEM_LIMIT),
        cost_estimate=pl.CostEstimate(
            flops=count * 2_000_000_000, bytes_accessed=count * 3_000_000, transcendentals=count * 600_000
        ),
    )(proj, last, bc, aux, seg_rows, packed, outs, d_normed, scale)


def state_back_call(taps, d_act, last, aux, packed, d_dt):
    args = (d_act, last, aux, packed, d_dt)
    return pl.pallas_call(
        functools.partial(state_back_kernel, taps),
        grid=(1,),
        in_specs=[whole_spec(x.shape) for x in args],
        out_specs=[whole_spec(last.shape), whole_spec((8, LANES))],
        out_shape=[jax.ShapeDtypeStruct(last.shape, BF16), jax.ShapeDtypeStruct((8, LANES), F32)],
        compiler_params=pltpu.CompilerParams(vmem_limit_bytes=VMEM_LIMIT),
        cost_estimate=pl.CostEstimate(flops=100_000_000, bytes_accessed=1_500_000, transcendentals=70_000),
    )(*args)


def make_aux(seg, rows, taps):
    blocks = seg.shape[0]
    columns = [seg.astype(F32)]
    for k in range(1, taps):
        before = jnp.pad(seg, ((0, 0), (k, 0)), constant_values=-1)[:, :rows]
        columns.append((before == seg).astype(F32))
    for k in range(1, taps):
        after = jnp.pad(seg, ((0, 0), (0, k)), constant_values=-1)[:, k:]
        columns.append((after == seg).astype(F32))
    columns += [jnp.zeros_like(columns[0])] * (8 - len(columns))
    return jnp.stack(columns, axis=-1).reshape(blocks * rows, 8)


def ring_owner(at, line):
    at = lax.rem(at + 2 * line, 2 * line)
    return jnp.where(at < line, 2 * at, 4 * line - 2 * at - 1)


def ring_add_kernel(count, upper, has_sums, owners, *refs):
    ups, downs = refs[:count], refs[count : 2 * count]
    sums = refs[2 * count : 2 * count + 2] if has_sums else None
    outs = refs[2 * count + 2 * has_sums :]
    low = 0
    for up, down in zip(ups, downs):
        high = low + up.shape[2]
        for way, part in enumerate((up, down)):
            value = part[0]
            if has_sums:
                value = (value.astype(F32) + sums[way][:, low:high].astype(F32)).astype(BF16)
            if len(outs) == 2:
                outs[way][:, low:high] = value
            elif way == 0:
                outs[0][:upper, low:high] = value
            else:
                outs[0][upper:, low:high] = value
        low = high


def ring_add(parts, owners, upper, sums, final):
    shard_rows = parts[0].shape[1]
    lower = shard_rows - upper
    width = sum(x.shape[2] for x in parts)
    count = len(parts)
    specs = []
    for k, x in enumerate(parts):
        specs.append(pl.BlockSpec((1, upper, x.shape[2]), functools.partial(lambda k, i, own: (own[2 * k], 0, 0), k)))
    for k, x in enumerate(parts):
        at = upper // lower
        specs.append(
            pl.BlockSpec((1, lower, x.shape[2]), functools.partial(lambda k, at, i, own: (own[2 * k + 1], at, 0), k, at))
        )
    whole = lambda rows: pl.BlockSpec((rows, width), lambda i, own: (0, 0))
    if sums is not None:
        specs += [whole(upper), whole(lower)]
    outs = [shard_rows] if final else [upper, lower]
    return pl.pallas_call(
        functools.partial(ring_add_kernel, count, upper, sums is not None),
        grid_spec=pltpu.PrefetchScalarGridSpec(
            num_scalar_prefetch=1, grid=(1,), in_specs=specs, out_specs=[whole(r) for r in outs]
        ),
        out_shape=[jax.ShapeDtypeStruct((r, width), BF16) for r in outs],
        compiler_params=pltpu.CompilerParams(vmem_limit_bytes=VMEM_ADD),
        cost_estimate=pl.CostEstimate(flops=0, bytes_accessed=1_000_000, transcendentals=0),
    )(jnp.stack(owners).astype(jnp.int32), *parts, *parts, *(sums or ()))


def outer_kernel(a, b, out):
    out[...] = dot(a[...], b[...], ((0,), (0,))).astype(BF16)


def outer(a, b, block, room):
    rows, height = a.shape
    return pl.pallas_call(
        outer_kernel,
        grid=(height // block,),
        in_specs=[pl.BlockSpec((rows, block), lambda i: (0, i)), whole_spec(b.shape)],
        out_specs=pl.BlockSpec((block, b.shape[1]), lambda i: (i, 0)),
        out_shape=jax.ShapeDtypeStruct((room * height, b.shape[1]), BF16),
        compiler_params=pltpu.CompilerParams(vmem_limit_bytes=VMEM_LIMIT),
        cost_estimate=pl.CostEstimate(flops=0, bytes_accessed=1_000_000, transcendentals=0),
    )(a, b)


def assemble_kernel(cuts, turned, starts, *refs):
    outs, sems = refs[-1 - len(cuts) : -1], refs[-1]
    sources = refs[: -1 - len(cuts)]

    def copies(run):
        for k, source in enumerate(sources):
            for n, (low, high) in enumerate(cuts):
                start = pl.multiple_of(starts[k + len(sources) * (n == turned)], 16)
                run(
                    pltpu.make_async_copy(
                        source.at[:, low:high],
                        outs[n].at[pl.ds(start, source.shape[0])],
                        sems.at[k * len(cuts) + n],
                    )
                )

    copies(lambda copy: copy.start())
    copies(lambda copy: copy.wait())


def assemble(starts, sources, cuts, turned=None, turn=0):
    total = sum(x.shape[0] for x in sources)
    starts = starts + [lax.rem(start + total - turn, total) for start in starts]
    return pl.pallas_call(
        functools.partial(assemble_kernel, cuts, turned),
        in_specs=[pl.BlockSpec(memory_space=pltpu.SMEM)] + [pl.BlockSpec(memory_space=pl.ANY)] * len(sources),
        out_specs=[pl.BlockSpec(memory_space=pltpu.VMEM)] * len(cuts),
        out_shape=[jax.ShapeDtypeStruct((total, high - low), BF16) for low, high in cuts],
        scratch_shapes=[pltpu.SemaphoreType.DMA((len(sources) * len(cuts),))],
        compiler_params=pltpu.CompilerParams(vmem_limit_bytes=VMEM_ALL),
        cost_estimate=pl.CostEstimate(
            flops=0, bytes_accessed=4 * total * sources[0].shape[1], transcendentals=0
        ),
    )(jnp.stack(starts).astype(jnp.int32), *sources)


def quarter_kernel(sizes, where, in_w, out_w, own_ref, other_ref):
    inner_all, state_all, groups, each, heads_all = sizes
    span = each * HALF
    inner = inner_all // 4
    row, core = where[2], where[3]
    tail = in_w[:, 2 * inner_all :]
    spare, depth = LANES - state_all // 4, tail.shape[1]
    for part, ref in ((core, own_ref), (1 - core, other_ref)):
        for base in range(2):
            for group in range(groups):
                pieces = []
                for c in range(2):
                    at = base * inner_all + c * inner_all // 2 + group * 2 * span
                    both = in_w[:, at : at + 2 * span]
                    pieces.append(jnp.where(row == 0, both[:, :span], both[:, span:]))
                ref[:, base * inner + group * span : base * inner + (group + 1) * span] = jnp.where(
                    part == 0, pieces[0], pieces[1]
                )
        source = lax.broadcasted_iota(jnp.int32, (depth, LANES), 0)
        lane = lax.broadcasted_iota(jnp.int32, (depth, LANES), 1)
        group = sum((lane >= g * each).astype(jnp.int32) for g in range(1, groups))
        head = state_all + part * (heads_all // 2) + (2 * group + row) * each + lane - group * each
        state = part * (state_all // 2) + row * (state_all // 4) + lane - spare
        wanted = jnp.where(lane < groups * each, head, jnp.where(lane >= spare, state, -1))
        ref[:, 2 * inner : 2 * inner + LANES] = dot(tail, (source == wanted).astype(BF16)).astype(BF16)
        if out_w is not None:
            half_rows, half = out_w.shape[0] // 2, out_w.shape[1] // 2
            mine = jnp.where(row == 0, out_w[:half_rows, :], out_w[half_rows:, :])
            ref[:, 2 * inner + LANES :] = jnp.where(part == 0, mine[:, :half], mine[:, half:])


def quarters_of(where, in_w, out_w, sizes):
    inner = sizes[0] // 4
    width = 2 * inner + LANES + (0 if out_w is None else out_w.shape[1] // 2)
    spec = pl.BlockSpec(memory_space=pltpu.VMEM)
    kernel = functools.partial(quarter_kernel, sizes)
    args = [where, in_w, out_w]
    if out_w is None:
        args = args[:2]
        inner_kernel = kernel
        kernel = lambda a, b, c, d: inner_kernel(a, b, None, c, d)
    return pl.pallas_call(
        kernel,
        in_specs=[pl.BlockSpec(memory_space=pltpu.SMEM)] + [spec] * (len(args) - 1),
        out_specs=[spec, spec],
        out_shape=[jax.ShapeDtypeStruct((in_w.shape[0], width), BF16)] * 2,
        compiler_params=pltpu.CompilerParams(vmem_limit_bytes=VMEM_LIMIT),
        cost_estimate=pl.CostEstimate(flops=0, bytes_accessed=10_000_000, transcendentals=0),
    )(*args)


def join_kernel(sizes, where, *refs):
    inner_all, state_all, groups, each, heads_all = sizes
    span = each * HALF
    inner = inner_all // 4
    row, core = where[2], where[3]
    has_out = len(refs) > 5
    in_ref = refs[4]
    split = 2 * inner + LANES

    def quarter(sources, c, r, low, high):
        mine, far, came, came_far = sources
        own = jnp.where(row == r, mine[:, low:high], far[:, low:high])
        theirs = jnp.where(row == r, came[:, low:high], came_far[:, low:high])
        return jnp.where(core == c, own, theirs)

    tails = 0.0
    spare, depth = LANES - state_all // 4, state_all + heads_all
    lane = lax.broadcasted_iota(jnp.int32, (LANES, depth), 0)
    target = lax.broadcasted_iota(jnp.int32, (LANES, depth), 1)
    group = sum((lane >= g * each).astype(jnp.int32) for g in range(1, groups))
    for c in range(2):
        for base in range(2):
            for g in range(groups):
                low = base * inner + g * span
                both = [quarter(refs[:4], c, r, low, low + span).astype(F32) for r in range(2)]
                at = base * inner_all + c * inner_all // 2 + g * 2 * span
                in_ref[0, :, at : at + 2 * span] = jnp.concatenate(both, axis=1)
        for r in range(2):
            head = state_all + c * (heads_all // 2) + (2 * group + r) * each + lane - group * each
            state = c * (state_all // 2) + r * (state_all // 4) + lane - spare
            wanted = jnp.where(lane < groups * each, head, jnp.where(lane >= spare, state, -1))
            chosen = (target == wanted).astype(BF16)
            tails = tails + dot(quarter(refs[:4], c, r, 2 * inner, 2 * inner + LANES), chosen)
            if has_out:
                half_rows, half = refs[0].shape[0], refs[0].shape[1] - split
                low = quarter(refs[:4], c, r, split, split + half).astype(F32)
                refs[5][0, r * half_rows : (r + 1) * half_rows, c * half : (c + 1) * half] = low
    in_ref[0, :, 2 * inner_all :] = tails


def join(where, quarters, sizes):
    rows, width = quarters[0].shape
    inner_all, state_all, groups, each, heads_all = sizes
    split = inner_all // 2 + LANES
    shapes = [jax.ShapeDtypeStruct((1, rows, 2 * inner_all + state_all + heads_all), F32)]
    if width > split:
        shapes.append(jax.ShapeDtypeStruct((1, 2 * rows, 2 * (width - split)), F32))
    spec = pl.BlockSpec(memory_space=pltpu.VMEM)
    return pl.pallas_call(
        functools.partial(join_kernel, sizes),
        in_specs=[pl.BlockSpec(memory_space=pltpu.SMEM)] + [spec] * len(quarters),
        out_specs=[spec] * len(shapes),
        out_shape=shapes,
        compiler_params=pltpu.CompilerParams(vmem_limit_bytes=VMEM_LIMIT),
        cost_estimate=pl.CostEstimate(flops=0, bytes_accessed=12_000_000, transcendentals=0),
    )(where, *quarters)


class Links:
    def __init__(self, mesh_shape):
        self.line = mesh_shape["fsdp"] // 2
        at = self.fsdp = lax.axis_index("fsdp")
        self.at = jnp.where(at % 2 == 0, at // 2, 2 * self.line - 1 - at // 2)
        ring = [2 * p for p in range(self.line)] + [2 * p + 1 for p in reversed(range(self.line))]
        self.ahead = [(ring[k - 1], ring[k]) for k in range(len(ring))]
        self.behind = [(after, before) for before, after in self.ahead]
        self.row, self.core = lax.axis_index("dp"), lax.axis_index("section")

    def swap_core(self, x):
        return lax.ppermute(x, "section", [(0, 1), (1, 0)])

    def swap_row(self, x):
        return lax.ppermute(x, "dp", [(0, 1), (1, 0)])

    def swap_side(self, x):
        return lax.ppermute(x, "fsdp", [(2 * p + s, 2 * p + 1 - s) for p in range(self.line) for s in range(2)])

    def mine_of_core(self, first, second):
        return jnp.where(self.core == 0, first, second)

    def in_row_order(self, own, other, axis):
        return jnp.where(
            self.row == 0, jnp.concatenate([own, other], axis), jnp.concatenate([other, own], axis)
        )

    def in_core_order(self, own, other, axis):
        return jnp.where(
            self.core == 0, jnp.concatenate([own, other], axis), jnp.concatenate([other, own], axis)
        )

    def cut(self, x, axis, which, parts=2):
        size = x.shape[axis] // parts
        return lax.dynamic_slice_in_dim(x, which * size, size, axis)

    def upper(self, shard_rows):
        return (shard_rows + 31) // 32 * 16

    def gather(self, piece, apart):
        shard_rows = piece.shape[0]
        upper = self.upper(shard_rows)
        up, down = piece[:upper], piece[upper:]
        sources, starts = [piece], [ring_owner(self.at, self.line) * shard_rows]
        mark = None
        sent_up, sent_down = lax.ppermute(up, "fsdp", self.ahead), lax.ppermute(down, "fsdp", self.behind)
        for hop in range(1, 2 * self.line):
            last = hop == 2 * self.line - 1
            if apart:
                up, mark = yield [sent_up, sent_up if mark is None else mark]
                sent_up = None if last else lax.ppermute(up, "fsdp", self.ahead)
                down, mark = lax.optimization_barrier((sent_down, mark))
                sent_down = None if last else lax.ppermute(down, "fsdp", self.behind)
            else:
                up, down = yield [sent_up, sent_down]
                if not last:
                    sent_up = lax.ppermute(up, "fsdp", self.ahead)
                    sent_down = lax.ppermute(down, "fsdp", self.behind)
            sources += [up, down]
            starts.append(ring_owner(self.at - hop, self.line) * shard_rows)
            starts.append(ring_owner(self.at + hop, self.line) * shard_rows + upper)
        return starts, sources

    def scatter(self, shard_rows, parts):
        upper = self.upper(shard_rows)
        sums = None
        for hop in range(1, 2 * self.line):
            owners = []
            for _, f in parts:
                owners += [f(ring_owner(self.at - hop, self.line)), f(ring_owner(self.at + hop, self.line))]
            up, down = ring_add([x for x, _ in parts], owners, upper, sums, False)
            sums = yield [lax.ppermute(up, "fsdp", self.ahead), lax.ppermute(down, "fsdp", self.behind)]
        owners = [f(ring_owner(self.at, self.line)) for _, f in parts for _ in range(2)]
        return ring_add([x for x, _ in parts], owners, upper, sums, True)[0]

    def sum_line(self, x):
        size = self.line
        if size & (size - 1):
            return lax.psum(x, "fsdp") / 2
        by = 1
        while by < size:
            pairs = [(2 * p + s, 2 * (p ^ by) + s) for p in range(size) for s in range(2)]
            x = x + lax.ppermute(x, "fsdp", pairs)
            by *= 2
            if by < size:
                (x,) = yield [x]
        return x


class Schedule:
    def __init__(self, work):
        self.work, self.sent = work, None

    def round(self, parts):
        extra = []
        if self.work is not None:
            try:
                extra = list(self.work.send(self.sent))
            except StopIteration:
                self.work = None
        joined = lax.optimization_barrier(tuple(parts) + tuple(extra))
        self.sent = list(joined[len(parts) :])
        return list(joined[: len(parts)])

    def run(self, moves):
        sent = None
        while True:
            try:
                parts = moves.send(sent)
            except StopIteration as stop:
                return stop.value
            sent = self.round(parts)


def body(mesh_shape, inputs, seq_lengths, norm_gain, in_w, conv_w, conv_b, dt_bias, a_log, skip, out_gain, out_w, cotangent):
    links = Links(mesh_shape)
    core, row = links.core, links.row
    shards = mesh_shape["fsdp"]
    width = inputs.shape[1]
    half_width = width // 2
    own_tokens = inputs.shape[0]
    tokens = 2 * own_tokens
    rows = own_tokens // seq_lengths.shape[0]
    inner_all = out_gain.shape[1]
    heads_all = a_log.shape[1]
    head_dim = inner_all // heads_all
    taps, channels = conv_w.shape[1:]
    state_all = channels - inner_all
    state_own = state_all // 4
    heads = heads_all // 4
    inner = inner_all // 4
    split = 2 * inner + LANES
    shard_rows = in_w.shape[1]
    direct = heads_all % shards == 0 and (heads_all // shards) % 2 == 0
    groups = shards // 2 if direct else 1
    each = heads // groups
    span = each * head_dim
    sizes = (inner_all, state_all, groups, each, heads_all)

    def pick_row(x, axis):
        return jnp.where(row == 0, lax.index_in_dim(x, 0, axis, False), lax.index_in_dim(x, 1, axis, False))

    def pick(x, axis):
        return links.mine_of_core(lax.index_in_dim(x, 0, axis, False), lax.index_in_dim(x, 1, axis, False))

    def wide_part(x):
        x = pick(x.reshape(x.shape[0], 2, groups, 2, span), 1)
        return pick_row(x, 2).reshape(x.shape[0], inner)

    def head_part(x):
        x = pick(x.reshape(x.shape[0], 2, groups, 2, each), 1)
        return pick_row(x, 2).reshape(x.shape[0], heads)

    def state_part(x):
        x = pick(x.reshape(x.shape[0], 2, 2, state_own), 1)
        return pick_row(x, 1)

    def wide_row(x):
        return jnp.pad(x, ((0, 0), (0, channels - x.shape[1])))

    zero = jnp.int32(0)
    where = jnp.stack([zero, zero, row, core]).astype(jnp.int32)
    own_part, other_part = quarters_of(where, in_w[0], out_w[0] if direct else None, sizes)
    came_part = links.swap_core(other_part)
    both = (links.mine_of_core(own_part, came_part), links.mine_of_core(came_part, own_part))
    if not direct:
        out_first, out_second = out_w[0][:, :half_width], out_w[0][:, half_width:]
        kept = links.mine_of_core(out_first, out_second)
        came = links.swap_core(links.mine_of_core(out_second, out_first))
        out_pieces = (links.mine_of_core(kept, came), links.mine_of_core(came, kept))
    pieces = list(both)

    packed = jnp.concatenate(
        [conv_w[0], conv_b, wide_row(out_gain), wide_row(norm_gain), wide_row(dt_bias), wide_row(a_log), wide_row(skip)],
        axis=0,
    )
    packed_other = links.swap_core(packed)
    all_lengths = links.in_row_order(seq_lengths, links.swap_row(seq_lengths), 0)
    sent_tokens, pieces[0], all_lengths, packed_other = lax.optimization_barrier(
        (inputs, pieces[0], all_lengths, packed_other)
    )

    def layer_params(pack):
        cw, cb = pack[:taps], pack[taps : taps + 1]
        og, ng = pack[taps + 1 : taps + 2, :inner_all], pack[taps + 2 : taps + 3, :width]
        dt, al, sk = (pack[taps + 3 + k : taps + 4 + k, :heads_all] for k in range(3))
        lanes = inner + state_all
        fill = lambda x: jnp.pad(x, ((0, 0), (0, lanes - x.shape[1])))
        conv = jnp.concatenate([cw, cb], axis=0)
        narrow = jnp.concatenate([head_part(dt), -jnp.exp(head_part(al))], axis=0)
        narrow = jnp.pad(narrow, ((0, 0), (0, LANES - heads))).reshape(1, 2 * LANES)
        own_state = jnp.pad(state_part(conv[:, inner_all:]), ((0, 0), (LANES - state_own, 0)))
        rows_ = [
            jnp.concatenate([wide_part(conv[:, :inner_all]), conv[:, inner_all:]], axis=1),
            fill(wide_part(og)),
            fill(jnp.repeat(head_part(sk), head_dim, axis=1)),
            fill(narrow),
            fill(own_state),
        ]
        return fill(jnp.concatenate([jnp.concatenate(rows_, axis=0), jnp.zeros((16 - 2 * taps - 5, lanes), F32)], axis=0)), ng

    blocks = tokens // rows
    big = {}

    def to_rows(x):
        return x.reshape(-1, LANES)

    def norm_of(u):
        return lax.rsqrt(jnp.mean(u * u, axis=-1, keepdims=True) + 1e-05)

    def over_cores(x):
        return links.cut(x, 1, core) + links.swap_core(links.cut(x, 1, 1 - core))

    def own_rows(x):
        return links.cut(x, 0, row)

    def norm_back(u, gain, d_scaled):
        u = u.astype(F32)
        inverse = norm_of(u)
        meet = jnp.mean(u * gain * d_scaled, axis=1, keepdims=True)
        return inverse * gain * d_scaled - u * (inverse * inverse * inverse * meet)

    def gain_back(u, d_scaled):
        u = u.astype(F32)
        return jnp.sum(u * norm_of(u) * d_scaled, axis=0, keepdims=True)

    def scaled_of(u, gain):
        u = u.astype(F32)
        return (u * norm_of(u) * gain).astype(BF16)

    def out_whole(pieces):
        half = pieces.shape[0] // 2
        kept, sent = (pieces[:half], pieces[half:]) if direct else (links.cut(pieces, 0, core), links.cut(pieces, 0, 1 - core))
        return links.in_core_order(kept, links.swap_core(sent), 1)

    def project(layer, scaled):
        wide_w, last_w = big["in", layer]
        last = dot(scaled, last_w)
        came = links.swap_row(last[:, LANES - state_own :])
        proj = dot(scaled, wide_w)
        proj, last, came = yield [proj, last, came]
        part = links.in_row_order(last[:, LANES - state_own :], came, 1)
        bc = links.in_core_order(part, links.swap_core(part), 1)
        return proj, last, bc

    def mix(layer, proj, last, bc):
        outs, gated, squares = ahead_call(heads, taps, rows, proj, last, bc, aux, seg_rows, big["pack", layer])
        return outs, gated, to_rows(squares[:, 0])

    def over_all(x):
        x = x + links.swap_core(x)
        return x + links.swap_row(x)

    def inverse_of(squares):
        return lax.rsqrt(squares / inner_all + 1e-05)

    def as_columns(*rows_):
        return jnp.stack([x.reshape(tokens) for x in rows_]).T

    def normed_of(layer, gated, inverse):
        gain = big["pack", layer][taps + 1 : taps + 2, :inner]
        normed = (gated * inverse.reshape(tokens, 1) * gain).astype(BF16)
        other = links.swap_core(normed)
        return jnp.concatenate([normed, other], axis=1) if direct else links.in_core_order(normed, other, 1)

    def back_mix(layer, kept, d_normed, meet):
        scale = as_columns(kept["inverse"], kept["inverse"] * meet / inner_all)
        return back_call(
            heads, taps, rows, kept["proj"], kept["last"], kept["bc"], aux, seg_rows, big["pack", layer],
            kept["outs"], d_normed, scale,
        )

    def back_project(layer, kept, d_main, d_dt, d_bc):
        wide_w, last_w = big["in", layer]
        d_bc = over_cores(d_bc)
        d_scaled = dot(d_main, wide_w, ((1,), (1,)))
        d_bc, d_scaled = yield [d_bc, d_scaled]
        d_bc = links.cut(d_bc, 1, row) + links.swap_row(links.cut(d_bc, 1, 1 - row))
        d_in = outer(kept["scaled"], d_main, width // 3, ROOM)
        d_bc, d_in = yield [d_bc, d_in]
        d_bc = jnp.pad(d_bc, ((0, 0), (LANES - d_bc.shape[1], 0)))
        d_last, d_state = state_back_call(taps, d_bc, kept["last"], aux, big["pack", layer], d_dt)
        d_in_last = dot(kept["scaled"], d_last, ((0,), (0,))).astype(BF16)
        d_scaled = d_scaled + dot(d_last, last_w, ((1,), (1,)))
        return d_scaled, d_in, d_in_last, d_state

    def out_grad(normed, grad_half):
        return dot(normed, grad_half, ((0,), (0,))).astype(BF16)

    aux = seg_rows = None
    done = {}

    def send_out(layer, d_out):
        done["out", layer] = d_out

    def work():
        nonlocal aux, seg_rows
        pack0, gain0 = layer_params(links.mine_of_core(packed, packed_other))
        pack1, gain1 = layer_params(links.mine_of_core(packed_other, packed))
        ends = jnp.cumsum(all_lengths, axis=1)
        positions = jnp.arange(rows, dtype=jnp.int32)
        segments = jnp.sum((positions[None, :, None] >= ends[:, None, :]).astype(jnp.int32), axis=2)
        aux, seg_rows = make_aux(segments, rows, taps), segments.astype(F32)[:, None, :]
        came_tokens = links.swap_row(sent_tokens)
        pack0, pack1, gain0, gain1, aux, seg_rows = yield [pack0, pack1, gain0, gain1, aux, seg_rows]
        big["pack", 0], big["pack", 1] = pack0, pack1
        (came_tokens,) = yield [came_tokens]
        tokens_all = links.in_row_order(inputs, came_tokens, 0)
        scaled = scaled_of(tokens_all, gain0)
        sent_cot, _ = lax.optimization_barrier((cotangent, came_tokens))
        came_cot = links.swap_row(sent_cot)
        tokens_all, scaled = yield [tokens_all, scaled]
        yield [scaled]
        cot_all = links.in_row_order(cotangent, came_cot, 0)
        cot_half = links.cut(cot_all, 1, core)
        cot_all, cot_half = yield [cot_all, cot_half]
        while ("in", 0) not in big:
            yield [scaled]
        wide_w, last_w = big["in", 0]
        if direct:
            wide_w, last_w, big["out", 0] = yield [wide_w, last_w, big["out", 0]]
        else:
            wide_w, last_w = yield [wide_w, last_w]
        big["in", 0] = wide_w, last_w
        proj, last, bc = yield from project(0, scaled)
        outs, gated, squares = mix(0, proj, last, bc)
        bc, outs, gated, squares = yield [bc, outs, gated, squares]
        (squares,) = yield [over_all(squares)]
        inverse = inverse_of(squares)
        normed = normed_of(0, gated, inverse)
        while ("out", 0) not in big:
            yield [normed]
        branch = dot(normed, big["out", 0]).astype(BF16)
        came = links.swap_row(branch)
        normed, inverse, branch = yield [normed, inverse, branch]
        kept0 = {"scaled": scaled, "proj": proj, "last": last, "bc": bc, "outs": outs, "inverse": inverse}
        big["out_whole", 0] = out_whole(big["out", 0])
        came, big["out_whole", 0] = yield [came, big["out_whole", 0]]
        normed0 = normed
        while ("in", 1) not in big or ("out", 1) not in big:
            yield [came]
        branch = branch.astype(F32) + came.astype(F32)
        first = (links.cut(tokens_all, 1, core).astype(F32) + branch).astype(BF16)
        first = links.in_core_order(first, links.swap_core(first), 1)
        scaled = scaled_of(first, gain1)
        big["out_whole", 1] = out_whole(big["out", 1])
        proj, last, bc = yield from project(1, scaled)
        d_normed = dot(cot_all, big["out_whole", 1], ((1,), (1,)))
        outs, gated, squares = mix(1, proj, last, bc)
        gain = big["pack", 1][taps + 1 : taps + 2, :inner]
        meet = to_rows(jnp.sum(gated * gain * d_normed, axis=1))
        both_sums = over_all(jnp.concatenate([squares, meet], axis=0))
        bc, outs, gated, d_normed, both_sums = yield [bc, outs, gated, d_normed, both_sums]
        squares, meet = both_sums[: squares.shape[0]], both_sums[squares.shape[0] :]
        inverse = inverse_of(squares)
        kept1 = {"scaled": scaled, "proj": proj, "last": last, "bc": bc, "outs": outs, "inverse": inverse}
        found = back_mix(1, kept1, d_normed, inverse * inverse * meet)
        d_main, d_dt, d_bc, d_wide1, d_narrow1 = yield list(found)
        normed1 = normed_of(1, gated, inverse)
        d_out = out_grad(normed1, cot_half)
        d_scaled, d_in, d_in_last, d_state1 = yield from back_project(1, kept1, d_main, d_dt, d_bc)
        d_scaled, d_in, d_in_last, d_out = yield [d_scaled, d_in, d_in_last, d_out]
        done["in", 1] = d_in, d_in_last
        send_out(1, d_out)
        small1 = jnp.sum(d_wide1, axis=0), jnp.sum(d_narrow1, axis=0), d_state1
        d_scaled = over_cores(d_scaled).astype(BF16)
        came = links.swap_row(d_scaled)
        (d_scaled,) = yield [d_scaled]
        (came,) = yield [came]
        d_scaled = d_scaled.astype(F32) + came.astype(F32)
        d_scaled = links.in_core_order(d_scaled, links.swap_core(d_scaled), 1)
        grad = (cot_all.astype(F32) + norm_back(first, gain1, d_scaled)).astype(BF16)
        gain_sum1 = gain_back(own_rows(first), own_rows(d_scaled))
        grad, gain_sum1 = yield [grad, gain_sum1]
        grad_half = links.cut(grad, 1, core)
        meet = to_rows(jnp.sum(branch * grad_half.astype(F32), axis=1))
        meet = meet + links.swap_core(meet)
        d_normed = dot(grad, big["out_whole", 0], ((1,), (1,)))
        d_normed, meet, grad_half = yield [d_normed, meet, grad_half]
        found = back_mix(0, kept0, d_normed, kept0["inverse"] * meet)
        d_main, d_dt, d_bc, d_wide0, d_narrow0 = yield list(found)
        d_out = out_grad(normed0, grad_half)
        d_scaled, d_in, d_in_last, d_state0 = yield from back_project(0, kept0, d_main, d_dt, d_bc)
        d_scaled, d_in, d_in_last, d_out = yield [d_scaled, d_in, d_in_last, d_out]
        done["in", 0] = d_in, d_in_last
        send_out(0, d_out)
        small0 = jnp.sum(d_wide0, axis=0), jnp.sum(d_narrow0, axis=0), d_state0
        while ("sum", 1) not in done:
            yield [d_scaled]
        far_upper = links.swap_row(done["sum", 1][: shard_rows // 2])
        d_scaled = over_cores(d_scaled)
        d_scaled, far_upper = yield [d_scaled, far_upper]
        came = links.swap_row(links.cut(d_scaled, 0, 1 - row).astype(BF16))
        partial = dot(normed1, big["out", 1])
        came, partial = yield [came, partial]
        far_lower = links.swap_row(done["sum", 1][shard_rows // 2 :])
        d_scaled = own_rows(d_scaled) + came.astype(F32)
        d_scaled = links.in_core_order(d_scaled, links.swap_core(d_scaled), 1)
        own_grad = own_rows(grad)
        grad_in = (own_grad.astype(F32) + norm_back(inputs, gain0, d_scaled)).astype(BF16)
        gain_sum0 = gain_back(inputs, d_scaled)
        done["input_grad"] = jnp.where(core == 0, grad_in, own_grad)[None]
        done["input_grad"], gain_sum0, far_lower = yield [done["input_grad"], gain_sum0, far_lower]
        done["far", 1] = jnp.concatenate([far_upper, far_lower], axis=0)
        came = links.swap_row(links.cut(partial, 0, 1 - row).astype(BF16))
        small = jnp.concatenate([pack_small(*small0, gain_sum0), pack_small(*small1, gain_sum1)], axis=0)
        small = small + links.swap_side(small)
        came, small = yield [came, small]
        second = own_rows(partial) + came.astype(F32) + links.cut(own_rows(first), 1, core).astype(F32)
        second = second.astype(BF16)
        second = links.in_core_order(second, links.swap_core(second), 1)
        done["phase_out"] = jnp.where(core == 0, own_rows(first), second)[None]
        small = yield from links.sum_line(small)
        done["phase_out"], small = yield [done["phase_out"], small]
        small_other = links.swap_row(small)
        done["small"] = spread_small(small, small_other)
        done["small"] = yield list(done["small"])

    gain_rows = width // inner

    def pack_small(wide_, narrow, d_state, gain):
        gain = gain.reshape(-1, inner)
        narrow_rows = jnp.concatenate([narrow[:2], d_state[: taps + 1]], axis=0)
        narrow_rows = jnp.pad(narrow_rows.reshape(1, -1), ((0, 0), (0, 2 * inner - narrow_rows.size)))
        return jnp.concatenate([wide_[: taps + 3], gain, narrow_rows.reshape(2, inner)], axis=0)

    def by_row(a, b):
        return jnp.where(row == 0, jnp.stack([a, b]), jnp.stack([b, a]))

    def spread_small(small, small_other):
        per = small.shape[0] // 2
        mine = links.mine_of_core(small[:per], small[per:])
        mine_other = links.mine_of_core(small_other[:per], small_other[per:])
        theirs = links.mine_of_core(small[per:], small[:per])
        theirs_other = links.mine_of_core(small_other[per:], small_other[:per])
        came = links.swap_core(jnp.stack([theirs, theirs_other]))
        own_parts, came_parts = by_row(mine, mine_other), by_row(came[0], came[1])
        quarters = jnp.where(core == 0, jnp.stack([own_parts, came_parts]), jnp.stack([came_parts, own_parts]))

        def spread_wide(x):
            lead = x.shape[2:-1]
            x = x.reshape((2, 2) + lead + (groups, span))
            x = jnp.moveaxis(x, (0, 1), (len(lead), len(lead) + 2))
            return x.reshape(lead + (inner_all,))

        def spread_heads(x):
            x = x.reshape((2, 2, groups, each))
            return jnp.moveaxis(x, 1, 2).reshape(1, heads_all)

        grad_norm = mine[taps + 3 : taps + 3 + gain_rows] + mine_other[taps + 3 : taps + 3 + gain_rows]
        narrow = quarters[:, :, taps + 3 + gain_rows :].reshape(2, 2, -1)
        narrow = narrow[:, :, : (taps + 3) * LANES].reshape(2, 2, taps + 3, LANES)
        states = jnp.moveaxis(narrow[:, :, 2:, LANES - state_own :], 2, 0).reshape(taps + 1, state_all)
        wide_full = spread_wide(quarters[:, :, : taps + 3])
        return [
            grad_norm.reshape(1, width),
            jnp.concatenate([wide_full[:taps], states[:taps]], axis=1)[None],
            jnp.concatenate([wide_full[taps : taps + 1], states[taps:]], axis=1),
            spread_heads(narrow[:, :, 0, :heads]),
            spread_heads(narrow[:, :, 1, :heads]),
            wide_full[taps + 1].reshape(1, heads_all, head_dim).sum(axis=-1),
            wide_full[taps + 2 : taps + 3],
        ]

    schedule = Schedule(work())

    def gather(layer):
        cuts = [(0, 2 * inner), (2 * inner, split)] + ([(split, split + half_width)] if direct else [])
        full = assemble(*schedule.run(links.gather(pieces[layer], layer == 0)), cuts, 2, core * (shards // 2 * shard_rows))
        if direct:
            big["out", layer] = full[2]
        else:
            big["out", layer] = out_gathered(layer)
        big["in", layer] = full[:2]

    def scatter(layer):
        while ("in", layer) not in done:
            schedule.round([])
        parts = list(done["in", layer])
        if direct:
            parts.append(done["out", layer])
        else:
            sums = done["out", layer].reshape(2, 1, inner, half_width)
            sums = links.in_row_order(sums, jnp.zeros_like(sums), 1).reshape(4 * inner, half_width)
            sums = lax.psum_scatter(sums, "fsdp", scatter_dimension=0, tiled=True)
            done["out_sum", layer] = (sums.astype(F32) + links.swap_row(sums).astype(F32)).astype(BF16)
        by_core = (lambda f: jnp.where(core == 0, f, (f + shards // 2) % shards)) if direct else (lambda f: f)
        laid = [lambda f: f, lambda f: f, by_core]
        parts = [(x.reshape(-1, shard_rows, x.shape[-1]), f) for x, f in zip(parts, laid)]
        done["sum", layer] = schedule.run(links.scatter(shard_rows, parts))

    def out_gathered(layer):
        full = lax.all_gather(out_pieces[layer], "fsdp", axis=0, tiled=True)
        return pick_row(full.reshape(2, 2, inner, half_width), 1).reshape(2 * inner, half_width)

    gather(0)
    gather(1)
    scatter(1)
    scatter(0)
    while schedule.work is not None:
        schedule.round([])

    low0, low1, far1 = done["sum", 0], done["sum", 1], done["far", 1]
    theirs = links.swap_core(links.mine_of_core(low1, low0))
    far0 = links.swap_row(low0)
    quarters = [links.mine_of_core(low0, low1), links.mine_of_core(far0, far1)]
    quarters += [theirs, links.swap_core(links.mine_of_core(far1, far0))]
    if direct:
        grad_in_w, grad_out_w = join(where, quarters, sizes)
    else:
        (grad_in_w,) = join(where, quarters, sizes)
        out0, out1 = done["out_sum", 0], done["out_sum", 1]
        theirs = links.swap_core(links.mine_of_core(out1, out0))
        grad_out_w = links.in_core_order(links.mine_of_core(out0, out1), theirs, 1).astype(F32)[None]
    grad_norm, grad_conv_w, grad_conv_b, grad_dt, grad_a, grad_skip, grad_out_gain = done["small"]
    return (
        done["phase_out"], done["input_grad"], grad_norm, grad_in_w, grad_conv_w, grad_conv_b,
        grad_dt, grad_a, grad_skip, grad_out_gain, grad_out_w,
    )


def solution(mesh):
    return jax.shard_map(
        functools.partial(body, dict(mesh.shape)),
        mesh=mesh,
        in_specs=(
            P(("fsdp", "dp"), None),
            P(("fsdp", "dp"), None),
            P("section", None),
            P("section", "fsdp", None),
            P("section", None, None),
            P("section", None),
            P("section", None),
            P("section", None),
            P("section", None),
            P("section", None),
            P("section", "fsdp", None),
            P(("fsdp", "dp"), None),
        ),
        out_specs=(
            P("section", ("fsdp", "dp"), None),
            P("section", ("fsdp", "dp"), None),
            P("section", None),
            P("section", "fsdp", None),
            P("section", None, None),
            P("section", None),
            P("section", None),
            P("section", None),
            P("section", None),
            P("section", None),
            P("section", "fsdp", None),
        ),
        check_vma=False,
    )
```

```python
import functools

import jax
import jax.numpy as jnp
from jax import lax
from jax.experimental import pallas as pl
from jax.experimental.pallas import tpu as pltpu
from jax.sharding import PartitionSpec as P

F32 = jnp.float32
BF16 = jnp.bfloat16
LANES = 128
HALF = 64
VMEM_LIMIT = 40 * 1024 * 1024
VMEM_ALL = 60 * 1024 * 1024
VMEM_ADD = 16 * 1024 * 1024
ROOM = 12


def dot(a, b, dims=((1,), (0,)), precision=None):
    return lax.dot_general(a, b, (dims, ((), ())), precision=precision, preferred_element_type=F32)


def dot_exact(a, b, dims=((1,), (0,))):
    return dot(a, b, dims, lax.Precision.HIGHEST)


def silu_parts(x):
    gate = 1.0 / (1.0 + jnp.exp(-x))
    return gate, x * gate


def softplus(x):
    return jnp.maximum(x, 0.0) + jnp.log1p(jnp.exp(-jnp.abs(x)))


def conv_mixed(conv_in, aux, conv_w, conv_b):
    taps = conv_w.shape[0]
    mixed = conv_b + conv_w[taps - 1 : taps] * conv_in
    shifted = []
    for back in range(1, taps):
        moved = pltpu.roll(conv_in, back, 0) * aux[:, back : back + 1]
        shifted.append(moved)
        mixed = mixed + conv_w[taps - 1 - back : taps - back] * moved
    return mixed, shifted


def conv_back(d_mixed, conv_in, shifted, aux, conv_w):
    taps = conv_w.shape[0]
    rows = d_mixed.shape[0]
    d_in = conv_w[taps - 1 : taps] * d_mixed
    d_w = [None] * taps
    d_w[taps - 1] = jnp.sum(d_mixed * conv_in, axis=0, keepdims=True)
    for back in range(1, taps):
        ahead = pltpu.roll(d_mixed, rows - back, 0) * aux[:, taps - 1 + back : taps + back]
        d_in = d_in + conv_w[taps - 1 - back : taps - back] * ahead
        d_w[taps - 1 - back] = jnp.sum(d_mixed * shifted[back - 1], axis=0, keepdims=True)
    return d_in, d_w, jnp.sum(d_mixed, axis=0, keepdims=True)


def decays(last, dt_bias, neg_rate, aux, seg_row):
    rows = last.shape[0]
    step = softplus(last + dt_bias)
    row = lax.broadcasted_iota(jnp.int32, (rows, rows), 0)
    col = lax.broadcasted_iota(jnp.int32, (rows, rows), 1)
    lower = row >= col
    log_decay = dot_exact(lower.astype(F32), neg_rate * step)
    allowed = lower & (aux[:, 0:1] == seg_row)
    return step, log_decay, allowed, lower


def pair_masks(rows):
    lane = lax.broadcasted_iota(jnp.int32, (rows, LANES), 1)
    return (lane < HALF).astype(F32), (lane >= HALF).astype(F32)


def unpack(packed, taps, heads):
    inner = heads * HALF
    conv_w, conv_b = packed[:taps, :], packed[taps : taps + 1, :]
    out_gain, skip = packed[taps + 1 : taps + 2, :inner], packed[taps + 2 : taps + 3, :inner]
    dt_bias, neg_rate = packed[taps + 3 : taps + 4, :LANES], packed[taps + 3 : taps + 4, LANES : 2 * LANES]
    return conv_w, conv_b, dt_bias, neg_rate, skip, out_gain


def ahead_kernel(heads, taps, proj, last, bc, aux, seg_row, packed, outs_ref, gated_ref, square_ref):
    rows = proj.shape[0]
    conv_w, conv_b, dt_bias, neg_rate, skip, _ = unpack(packed, taps, heads)
    inner = heads * HALF
    aux_v = aux[...]
    values_mixed, _ = conv_mixed(proj[:, inner : 2 * inner], aux_v, conv_w[:, :inner], conv_b[:, :inner])
    _, values = silu_parts(values_mixed)
    state_mixed, _ = conv_mixed(bc[...], aux_v, conv_w[:, inner:], conv_b[:, inner:])
    _, state = silu_parts(state_mixed)
    in_state, out_state = state[:, :LANES].astype(BF16), state[:, LANES:].astype(BF16)
    step, log_decay, allowed, _ = decays(
        last[...], dt_bias, neg_rate, aux_v, seg_row[0]
    )
    step_t, log_t = step.T, log_decay.T
    inter = dot(out_state, in_state, ((1,), (1,)))
    first, second = pair_masks(rows)
    squares = jnp.zeros((rows, 1), F32)
    for pair in range(heads // 2):
        weights = []
        for h in (2 * pair, 2 * pair + 1):
            gap = log_decay[:, h : h + 1] - log_t[h : h + 1]
            decay = jnp.exp(jnp.where(allowed, gap, -1e30))
            weights.append((inter * decay * step_t[h : h + 1]).astype(BF16))
        at = slice(pair * LANES, (pair + 1) * LANES)
        own = values[:, at]
        low = own.astype(BF16).astype(F32)
        both = jnp.concatenate([low * first, low * second], axis=0).astype(BF16)
        carried = dot(jnp.concatenate(weights, axis=1), both)
        outs = carried + skip[:, at] * own
        _, gate = silu_parts(proj[:, at])
        gated = outs * gate
        outs_ref[:, at] = outs
        gated_ref[:, at] = gated
        squares = squares + jnp.sum(gated * gated, axis=1, keepdims=True)
    square_ref[...] = jnp.broadcast_to(squares, square_ref.shape)


def back_kernel(
    heads, taps, proj, last_ref, bc, aux, seg_row, packed, outs, d_normed, scale, *results
):
    d_main_ref, d_dt_ref, d_state_ref, d_wide_ref, d_narrow_ref = results
    rows = proj.shape[0]
    conv_w, conv_b, dt_bias, neg_rate, skip, out_gain = unpack(packed, taps, heads)
    inner = heads * HALF
    aux_v = aux[...]
    values_in = proj[:, inner : 2 * inner]
    values_mixed, values_shifted = conv_mixed(values_in, aux_v, conv_w[:, :inner], conv_b[:, :inner])
    values_gate, values = silu_parts(values_mixed)
    state_mixed, _ = conv_mixed(bc[...], aux_v, conv_w[:, inner:], conv_b[:, inner:])
    _, state = silu_parts(state_mixed)
    in_state, out_state = state[:, :LANES].astype(BF16), state[:, LANES:].astype(BF16)
    last = last_ref[...]
    step, log_decay, allowed, lower = decays(last, dt_bias, neg_rate, aux_v, seg_row[0])
    step_t, log_t = step.T, log_decay.T
    inter = dot(out_state, in_state, ((1,), (1,)))
    first, second = pair_masks(rows)
    lane = lax.broadcasted_iota(jnp.int32, (rows, LANES), 1)
    sub = lax.broadcasted_iota(jnp.int32, (LANES, rows), 0)
    inverse, shrink = scale[:, 0:1], scale[:, 1:2]
    d_inter = jnp.zeros((rows, rows), F32)
    row_sums = jnp.zeros((rows, LANES), F32)
    col_sums = jnp.zeros((LANES, rows), F32)
    d_skip, d_gain, d_values = [], [], []
    for pair in range(heads // 2):
        at = slice(pair * LANES, (pair + 1) * LANES)
        own = values[:, at]
        low = own.astype(BF16)
        gate_in = proj[:, at]
        sig, gate = silu_parts(gate_in)
        outs_at = outs[:, at]
        gated = outs_at * gate
        dn = d_normed[:, at]
        d_gain.append(jnp.sum(gated * inverse * dn, axis=0, keepdims=True))
        d_gated = inverse * (out_gain[:, at] * dn) - gated * shrink
        d_outs = d_gated * gate
        d_main_ref[:, at] = (d_gated * outs_at * (sig * (1.0 + gate_in * (1.0 - sig)))).astype(BF16)
        d_skip.append(jnp.sum(d_outs * own, axis=0, keepdims=True))
        d_both = jnp.concatenate([d_outs * first, d_outs * second], axis=0).astype(BF16)
        d_weights = dot(d_both, low, ((1,), (1,)))
        weights = []
        for k, h in enumerate((2 * pair, 2 * pair + 1)):
            gap = log_decay[:, h : h + 1] - log_t[h : h + 1]
            decay = jnp.exp(jnp.where(allowed, gap, -1e30))
            step_row = step_t[h : h + 1]
            weights.append((inter * decay * step_row).astype(BF16))
            part = d_weights[k * rows : (k + 1) * rows] * decay
            d_inter = d_inter + part * step_row
            part = part * inter
            col = jnp.sum(part, axis=0, keepdims=True)
            col_sums = jnp.where(sub == h, col, col_sums)
            row_sum = jnp.sum(part * step_row, axis=1, keepdims=True)
            row_sums = jnp.where(lane == h, row_sum, row_sums)
        d_low = dot(jnp.concatenate(weights, axis=0), d_both, ((0,), (0,)))
        d_values.append(skip[:, at] * d_outs + d_low)
    d_values = jnp.concatenate(d_values, axis=1)
    d_mixed = d_values * (values_gate * (1.0 + values_mixed * (1.0 - values_gate)))
    d_in, d_w, d_b = conv_back(d_mixed, values_in, values_shifted, aux_v, conv_w[:, :inner])
    d_main_ref[:, inner : 2 * inner] = d_in.astype(BF16)
    low_inter = d_inter.astype(BF16)
    d_state_ref[:, :LANES] = dot(low_inter, out_state, ((0,), (0,)))
    d_state_ref[:, LANES:] = dot(low_inter, in_state)
    direct = col_sums.T
    d_log = row_sums - direct * step
    d_pace = dot_exact(lower.astype(F32), d_log, ((0,), (0,)))
    d_step = direct + d_pace * neg_rate
    d_last = jnp.where(lane < heads, d_step * (1.0 / (1.0 + jnp.exp(-(last + dt_bias)))), 0.0)
    d_dt_ref[...] = d_last
    wide = d_w + [d_b, jnp.concatenate(d_skip, axis=1), jnp.concatenate(d_gain, axis=1)]
    wide.append(jnp.zeros((d_wide_ref.shape[1] - len(wide), inner), F32))
    d_wide_ref[0] = jnp.concatenate(wide, axis=0)
    d_rate = jnp.sum(d_pace * neg_rate * step, axis=0, keepdims=True)
    narrow = [
        jnp.sum(d_last, axis=0, keepdims=True),
        jnp.where(lane[:1] < heads, d_rate, 0.0),
        jnp.zeros((d_narrow_ref.shape[1] - 2, LANES), F32),
    ]
    d_narrow_ref[0] = jnp.concatenate(narrow, axis=0)


def state_back_kernel(taps, d_act, last, aux, packed, d_dt, d_proj_ref, d_sums_ref):
    aux_v = aux[...]
    last_v = last[...]
    conv_w, conv_b = packed[8 : 8 + taps, :LANES], packed[8 + taps : 9 + taps, :LANES]
    mixed, shifted = conv_mixed(last_v, aux_v, conv_w, conv_b)
    sig, _ = silu_parts(mixed)
    d_mixed = d_act[...] * (sig * (1.0 + mixed * (1.0 - sig)))
    d_in, d_w, d_b = conv_back(d_mixed, last_v, shifted, aux_v, conv_w)
    lane = lax.broadcasted_iota(jnp.int32, last_v.shape, 1)
    d_proj_ref[...] = jnp.where(lane < HALF, d_dt[...], d_in).astype(BF16)
    sums = d_w + [d_b]
    sums.append(jnp.zeros((d_sums_ref.shape[0] - len(sums), LANES), F32))
    d_sums_ref[...] = jnp.concatenate(sums, axis=0)


def rows_spec(rows, width):
    return pl.BlockSpec((rows, width), lambda i: (i, 0))


def whole_spec(shape):
    return pl.BlockSpec(shape, lambda i: (0,) * len(shape))


def ahead_call(heads, taps, rows, proj, last, bc, aux, seg_rows, packed):
    total = proj.shape[0]
    inner = heads * HALF
    count = total // rows
    return pl.pallas_call(
        functools.partial(ahead_kernel, heads, taps),
        grid=(count,),
        in_specs=[
            rows_spec(rows, proj.shape[1]),
            rows_spec(rows, LANES),
            rows_spec(rows, bc.shape[1]),
            rows_spec(rows, aux.shape[1]),
            pl.BlockSpec((1, 1, rows), lambda i: (i, 0, 0)),
            whole_spec(packed.shape),
        ],
        out_specs=[rows_spec(rows, inner), rows_spec(rows, inner), rows_spec(rows, LANES)],
        out_shape=[
            jax.ShapeDtypeStruct((total, inner), F32),
            jax.ShapeDtypeStruct((total, inner), F32),
            jax.ShapeDtypeStruct((total, LANES), F32),
        ],
        compiler_params=pltpu.CompilerParams(vmem_limit_bytes=VMEM_LIMIT),
        cost_estimate=pl.CostEstimate(
            flops=count * 1_000_000_000, bytes_accessed=count * 2_000_000, transcendentals=count * 400_000
        ),
    )(proj, last, bc, aux, seg_rows, packed)


def back_call(heads, taps, rows, proj, last, bc, aux, seg_rows, packed, outs, d_normed, scale):
    total = proj.shape[0]
    inner = heads * HALF
    count = total // rows
    return pl.pallas_call(
        functools.partial(back_kernel, heads, taps),
        grid=(count,),
        in_specs=[
            rows_spec(rows, proj.shape[1]),
            rows_spec(rows, LANES),
            rows_spec(rows, bc.shape[1]),
            rows_spec(rows, aux.shape[1]),
            pl.BlockSpec((1, 1, rows), lambda i: (i, 0, 0)),
            whole_spec(packed.shape),
            rows_spec(rows, inner),
            rows_spec(rows, inner),
            rows_spec(rows, 2),
        ],
        out_specs=[
            rows_spec(rows, 2 * inner),
            rows_spec(rows, LANES),
            rows_spec(rows, bc.shape[1]),
            pl.BlockSpec((1, 8, inner), lambda i: (i, 0, 0)),
            pl.BlockSpec((1, 8, LANES), lambda i: (i, 0, 0)),
        ],
        out_shape=[
            jax.ShapeDtypeStruct((total, 2 * inner), BF16),
            jax.ShapeDtypeStruct((total, LANES), F32),
            jax.ShapeDtypeStruct((total, bc.shape[1]), F32),
            jax.ShapeDtypeStruct((count, 8, inner), F32),
            jax.ShapeDtypeStruct((count, 8, LANES), F32),
        ],
        compiler_params=pltpu.CompilerParams(vmem_limit_bytes=VMEM_LIMIT),
        cost_estimate=pl.CostEstimate(
            flops=count * 2_000_000_000, bytes_accessed=count * 3_000_000, transcendentals=count * 600_000
        ),
    )(proj, last, bc, aux, seg_rows, packed, outs, d_normed, scale)


def state_back_call(taps, d_act, last, aux, packed, d_dt):
    args = (d_act, last, aux, packed, d_dt)
    return pl.pallas_call(
        functools.partial(state_back_kernel, taps),
        grid=(1,),
        in_specs=[whole_spec(x.shape) for x in args],
        out_specs=[whole_spec(last.shape), whole_spec((8, LANES))],
        out_shape=[jax.ShapeDtypeStruct(last.shape, BF16), jax.ShapeDtypeStruct((8, LANES), F32)],
        compiler_params=pltpu.CompilerParams(vmem_limit_bytes=VMEM_LIMIT),
        cost_estimate=pl.CostEstimate(flops=100_000_000, bytes_accessed=1_500_000, transcendentals=70_000),
    )(*args)


def make_aux(seg, rows, taps):
    blocks = seg.shape[0]
    columns = [seg.astype(F32)]
    for k in range(1, taps):
        before = jnp.pad(seg, ((0, 0), (k, 0)), constant_values=-1)[:, :rows]
        columns.append((before == seg).astype(F32))
    for k in range(1, taps):
        after = jnp.pad(seg, ((0, 0), (0, k)), constant_values=-1)[:, k:]
        columns.append((after == seg).astype(F32))
    columns += [jnp.zeros_like(columns[0])] * (8 - len(columns))
    return jnp.stack(columns, axis=-1).reshape(blocks * rows, 8)


def ring_owner(at, line):
    at = lax.rem(at + 2 * line, 2 * line)
    return jnp.where(at < line, 2 * at, 4 * line - 2 * at - 1)


def ring_add_kernel(count, upper, has_sums, owners, *refs):
    ups, downs = refs[:count], refs[count : 2 * count]
    sums = refs[2 * count : 2 * count + 2] if has_sums else None
    outs = refs[2 * count + 2 * has_sums :]
    low = 0
    for up, down in zip(ups, downs):
        high = low + up.shape[2]
        for way, part in enumerate((up, down)):
            value = part[0]
            if has_sums:
                value = (value.astype(F32) + sums[way][:, low:high].astype(F32)).astype(BF16)
            if len(outs) == 2:
                outs[way][:, low:high] = value
            elif way == 0:
                outs[0][:upper, low:high] = value
            else:
                outs[0][upper:, low:high] = value
        low = high


def ring_add(parts, owners, upper, sums, final):
    shard_rows = parts[0].shape[1]
    lower = shard_rows - upper
    width = sum(x.shape[2] for x in parts)
    count = len(parts)
    specs = []
    for k, x in enumerate(parts):
        specs.append(pl.BlockSpec((1, upper, x.shape[2]), functools.partial(lambda k, i, own: (own[2 * k], 0, 0), k)))
    for k, x in enumerate(parts):
        at = upper // lower
        specs.append(
            pl.BlockSpec((1, lower, x.shape[2]), functools.partial(lambda k, at, i, own: (own[2 * k + 1], at, 0), k, at))
        )
    whole = lambda rows: pl.BlockSpec((rows, width), lambda i, own: (0, 0))
    if sums is not None:
        specs += [whole(upper), whole(lower)]
    outs = [shard_rows] if final else [upper, lower]
    return pl.pallas_call(
        functools.partial(ring_add_kernel, count, upper, sums is not None),
        grid_spec=pltpu.PrefetchScalarGridSpec(
            num_scalar_prefetch=1, grid=(1,), in_specs=specs, out_specs=[whole(r) for r in outs]
        ),
        out_shape=[jax.ShapeDtypeStruct((r, width), BF16) for r in outs],
        compiler_params=pltpu.CompilerParams(vmem_limit_bytes=VMEM_ADD),
        cost_estimate=pl.CostEstimate(flops=0, bytes_accessed=1_000_000, transcendentals=0),
    )(jnp.stack(owners).astype(jnp.int32), *parts, *parts, *(sums or ()))


def outer_kernel(a, b, out):
    out[...] = dot(a[...], b[...], ((0,), (0,))).astype(BF16)


def outer(a, b, block, room):
    rows, height = a.shape
    return pl.pallas_call(
        outer_kernel,
        grid=(height // block,),
        in_specs=[pl.BlockSpec((rows, block), lambda i: (0, i)), whole_spec(b.shape)],
        out_specs=pl.BlockSpec((block, b.shape[1]), lambda i: (i, 0)),
        out_shape=jax.ShapeDtypeStruct((room * height, b.shape[1]), BF16),
        compiler_params=pltpu.CompilerParams(vmem_limit_bytes=VMEM_LIMIT),
        cost_estimate=pl.CostEstimate(flops=0, bytes_accessed=1_000_000, transcendentals=0),
    )(a, b)


def assemble_kernel(cuts, turned, starts, *refs):
    made = len(cuts) + (turned is not None)
    outs, sems = refs[-1 - made : -1], refs[-1]
    sources = refs[: -1 - made]

    def copies(run):
        for k, source in enumerate(sources):
            for n, (low, high) in enumerate(cuts):
                start = starts[k + len(sources) * (n == turned)]
                sem = sems.at[k * len(cuts) + n]

                def copy_to(out, at, condition):
                    at = pl.multiple_of(jnp.clip(at, 0, out.shape[0] - source.shape[0]), 16)
                    copy = pltpu.make_async_copy(source.at[:, low:high], out.at[pl.ds(at, source.shape[0])], sem)
                    if condition is None:
                        run(copy)
                    else:
                        pl.when(condition)(functools.partial(run, copy))

                if n == turned:
                    half = outs[n].shape[0]
                    copy_to(outs[n], start, start < half)
                    copy_to(outs[n + 1], start - half, start >= half)
                else:
                    copy_to(outs[n], start, None)

    copies(lambda copy: copy.start())
    copies(lambda copy: copy.wait())


def assemble(starts, sources, cuts, turned=None, turn=0):
    total = sum(x.shape[0] for x in sources)
    starts = starts + [lax.rem(start + total - turn, total) for start in starts]
    shapes = [(total, high - low) for low, high in cuts]
    if turned is not None:
        shapes[turned : turned + 1] = [(total // 2, shapes[turned][1])] * 2
    return pl.pallas_call(
        functools.partial(assemble_kernel, cuts, turned),
        in_specs=[pl.BlockSpec(memory_space=pltpu.SMEM)] + [pl.BlockSpec(memory_space=pl.ANY)] * len(sources),
        out_specs=[pl.BlockSpec(memory_space=pltpu.VMEM)] * len(shapes),
        out_shape=[jax.ShapeDtypeStruct(shape, BF16) for shape in shapes],
        scratch_shapes=[pltpu.SemaphoreType.DMA((len(sources) * len(cuts),))],
        compiler_params=pltpu.CompilerParams(vmem_limit_bytes=VMEM_ALL),
        cost_estimate=pl.CostEstimate(
            flops=0, bytes_accessed=4 * total * sources[0].shape[1], transcendentals=0
        ),
    )(jnp.stack(starts).astype(jnp.int32), *sources)


def quarter_kernel(sizes, where, in_w, out_w, own_ref, other_ref):
    inner_all, state_all, groups, each, heads_all = sizes
    span = each * HALF
    inner = inner_all // 4
    row, core = where[2], where[3]
    tail = in_w[:, 2 * inner_all :]
    spare, depth = LANES - state_all // 4, tail.shape[1]
    for part, ref in ((core, own_ref), (1 - core, other_ref)):
        for base in range(2):
            for group in range(groups):
                pieces = []
                for c in range(2):
                    at = base * inner_all + c * inner_all // 2 + group * 2 * span
                    both = in_w[:, at : at + 2 * span]
                    pieces.append(jnp.where(row == 0, both[:, :span], both[:, span:]))
                ref[:, base * inner + group * span : base * inner + (group + 1) * span] = jnp.where(
                    part == 0, pieces[0], pieces[1]
                )
        source = lax.broadcasted_iota(jnp.int32, (depth, LANES), 0)
        lane = lax.broadcasted_iota(jnp.int32, (depth, LANES), 1)
        group = sum((lane >= g * each).astype(jnp.int32) for g in range(1, groups))
        head = state_all + part * (heads_all // 2) + (2 * group + row) * each + lane - group * each
        state = part * (state_all // 2) + row * (state_all // 4) + lane - spare
        wanted = jnp.where(lane < groups * each, head, jnp.where(lane >= spare, state, -1))
        ref[:, 2 * inner : 2 * inner + LANES] = dot(tail, (source == wanted).astype(BF16)).astype(BF16)
        if out_w is not None:
            half_rows, half = out_w.shape[0] // 2, out_w.shape[1] // 2
            mine = jnp.where(row == 0, out_w[:half_rows, :], out_w[half_rows:, :])
            ref[:, 2 * inner + LANES :] = jnp.where(part == 0, mine[:, :half], mine[:, half:])


def quarters_of(where, in_w, out_w, sizes):
    inner = sizes[0] // 4
    width = 2 * inner + LANES + (0 if out_w is None else out_w.shape[1] // 2)
    spec = pl.BlockSpec(memory_space=pltpu.VMEM)
    kernel = functools.partial(quarter_kernel, sizes)
    args = [where, in_w, out_w]
    if out_w is None:
        args = args[:2]
        inner_kernel = kernel
        kernel = lambda a, b, c, d: inner_kernel(a, b, None, c, d)
    return pl.pallas_call(
        kernel,
        in_specs=[pl.BlockSpec(memory_space=pltpu.SMEM)] + [spec] * (len(args) - 1),
        out_specs=[spec, spec],
        out_shape=[jax.ShapeDtypeStruct((in_w.shape[0], width), BF16)] * 2,
        compiler_params=pltpu.CompilerParams(vmem_limit_bytes=VMEM_LIMIT),
        cost_estimate=pl.CostEstimate(flops=0, bytes_accessed=10_000_000, transcendentals=0),
    )(*args)


def join_kernel(sizes, where, *refs):
    inner_all, state_all, groups, each, heads_all = sizes
    span = each * HALF
    inner = inner_all // 4
    row, core = where[2], where[3]
    has_out = len(refs) > 5
    in_ref = refs[4]
    split = 2 * inner + LANES

    def quarter(sources, c, r, low, high):
        mine, far, came, came_far = sources
        own = jnp.where(row == r, mine[:, low:high], far[:, low:high])
        theirs = jnp.where(row == r, came[:, low:high], came_far[:, low:high])
        return jnp.where(core == c, own, theirs)

    tails = 0.0
    spare, depth = LANES - state_all // 4, state_all + heads_all
    lane = lax.broadcasted_iota(jnp.int32, (LANES, depth), 0)
    target = lax.broadcasted_iota(jnp.int32, (LANES, depth), 1)
    group = sum((lane >= g * each).astype(jnp.int32) for g in range(1, groups))
    for c in range(2):
        for base in range(2):
            for g in range(groups):
                low = base * inner + g * span
                both = [quarter(refs[:4], c, r, low, low + span).astype(F32) for r in range(2)]
                at = base * inner_all + c * inner_all // 2 + g * 2 * span
                in_ref[0, :, at : at + 2 * span] = jnp.concatenate(both, axis=1)
        for r in range(2):
            head = state_all + c * (heads_all // 2) + (2 * group + r) * each + lane - group * each
            state = c * (state_all // 2) + r * (state_all // 4) + lane - spare
            wanted = jnp.where(lane < groups * each, head, jnp.where(lane >= spare, state, -1))
            chosen = (target == wanted).astype(BF16)
            tails = tails + dot(quarter(refs[:4], c, r, 2 * inner, 2 * inner + LANES), chosen)
            if has_out:
                half_rows, half = refs[0].shape[0], refs[0].shape[1] - split
                low = quarter(refs[:4], c, r, split, split + half).astype(F32)
                refs[5][0, r * half_rows : (r + 1) * half_rows, c * half : (c + 1) * half] = low
    in_ref[0, :, 2 * inner_all :] = tails


def join(where, quarters, sizes):
    rows, width = quarters[0].shape
    inner_all, state_all, groups, each, heads_all = sizes
    split = inner_all // 2 + LANES
    shapes = [jax.ShapeDtypeStruct((1, rows, 2 * inner_all + state_all + heads_all), F32)]
    if width > split:
        shapes.append(jax.ShapeDtypeStruct((1, 2 * rows, 2 * (width - split)), F32))
    spec = pl.BlockSpec(memory_space=pltpu.VMEM)
    return pl.pallas_call(
        functools.partial(join_kernel, sizes),
        in_specs=[pl.BlockSpec(memory_space=pltpu.SMEM)] + [spec] * len(quarters),
        out_specs=[spec] * len(shapes),
        out_shape=shapes,
        compiler_params=pltpu.CompilerParams(vmem_limit_bytes=VMEM_LIMIT),
        cost_estimate=pl.CostEstimate(flops=0, bytes_accessed=12_000_000, transcendentals=0),
    )(where, *quarters)


class Links:
    def __init__(self, mesh_shape):
        self.line = mesh_shape["fsdp"] // 2
        at = self.fsdp = lax.axis_index("fsdp")
        self.at = jnp.where(at % 2 == 0, at // 2, 2 * self.line - 1 - at // 2)
        ring = [2 * p for p in range(self.line)] + [2 * p + 1 for p in reversed(range(self.line))]
        self.ahead = [(ring[k - 1], ring[k]) for k in range(len(ring))]
        self.behind = [(after, before) for before, after in self.ahead]
        self.row, self.core = lax.axis_index("dp"), lax.axis_index("section")

    def swap_core(self, x):
        return lax.ppermute(x, "section", [(0, 1), (1, 0)])

    def swap_row(self, x):
        return lax.ppermute(x, "dp", [(0, 1), (1, 0)])

    def swap_side(self, x):
        return lax.ppermute(x, "fsdp", [(2 * p + s, 2 * p + 1 - s) for p in range(self.line) for s in range(2)])

    def mine_of_core(self, first, second):
        return jnp.where(self.core == 0, first, second)

    def in_row_order(self, own, other, axis):
        return jnp.where(
            self.row == 0, jnp.concatenate([own, other], axis), jnp.concatenate([other, own], axis)
        )

    def in_core_order(self, own, other, axis):
        return jnp.where(
            self.core == 0, jnp.concatenate([own, other], axis), jnp.concatenate([other, own], axis)
        )

    def cut(self, x, axis, which, parts=2):
        size = x.shape[axis] // parts
        return lax.dynamic_slice_in_dim(x, which * size, size, axis)

    def upper(self, shard_rows):
        return (shard_rows + 31) // 32 * 16

    def gather(self, piece, apart):
        shard_rows = piece.shape[0]
        upper = self.upper(shard_rows)
        up, down = piece[:upper], piece[upper:]
        sources, starts = [piece], [ring_owner(self.at, self.line) * shard_rows]
        mark = None
        sent_up, sent_down = lax.ppermute(up, "fsdp", self.ahead), lax.ppermute(down, "fsdp", self.behind)
        for hop in range(1, 2 * self.line):
            last = hop == 2 * self.line - 1
            if apart:
                up, mark = yield [sent_up, sent_up if mark is None else mark]
                sent_up = None if last else lax.ppermute(up, "fsdp", self.ahead)
                down, mark = lax.optimization_barrier((sent_down, mark))
                sent_down = None if last else lax.ppermute(down, "fsdp", self.behind)
            else:
                up, down = yield [sent_up, sent_down]
                if not last:
                    sent_up = lax.ppermute(up, "fsdp", self.ahead)
                    sent_down = lax.ppermute(down, "fsdp", self.behind)
            sources += [up, down]
            starts.append(ring_owner(self.at - hop, self.line) * shard_rows)
            starts.append(ring_owner(self.at + hop, self.line) * shard_rows + upper)
        return starts, sources

    def scatter(self, shard_rows, parts):
        upper = self.upper(shard_rows)
        sums = None
        for hop in range(1, 2 * self.line):
            owners = []
            for _, f in parts:
                owners += [f(ring_owner(self.at - hop, self.line)), f(ring_owner(self.at + hop, self.line))]
            up, down = ring_add([x for x, _ in parts], owners, upper, sums, False)
            sums = yield [lax.ppermute(up, "fsdp", self.ahead), lax.ppermute(down, "fsdp", self.behind)]
        owners = [f(ring_owner(self.at, self.line)) for _, f in parts for _ in range(2)]
        return ring_add([x for x, _ in parts], owners, upper, sums, True)[0]

    def sum_line(self, x):
        size = self.line
        if size & (size - 1):
            return lax.psum(x, "fsdp") / 2
        by = 1
        while by < size:
            pairs = [(2 * p + s, 2 * (p ^ by) + s) for p in range(size) for s in range(2)]
            x = x + lax.ppermute(x, "fsdp", pairs)
            by *= 2
            if by < size:
                (x,) = yield [x]
        return x


class Schedule:
    def __init__(self, work):
        self.work, self.sent = work, None

    def round(self, parts):
        extra = []
        if self.work is not None:
            try:
                extra = list(self.work.send(self.sent))
            except StopIteration:
                self.work = None
        joined = lax.optimization_barrier(tuple(parts) + tuple(extra))
        self.sent = list(joined[len(parts) :])
        return list(joined[: len(parts)])

    def run(self, moves):
        sent = None
        while True:
            try:
                parts = moves.send(sent)
            except StopIteration as stop:
                return stop.value
            sent = self.round(parts)


def body(mesh_shape, inputs, seq_lengths, norm_gain, in_w, conv_w, conv_b, dt_bias, a_log, skip, out_gain, out_w, cotangent):
    links = Links(mesh_shape)
    core, row = links.core, links.row
    shards = mesh_shape["fsdp"]
    width = inputs.shape[1]
    half_width = width // 2
    own_tokens = inputs.shape[0]
    tokens = 2 * own_tokens
    rows = own_tokens // seq_lengths.shape[0]
    inner_all = out_gain.shape[1]
    heads_all = a_log.shape[1]
    head_dim = inner_all // heads_all
    taps, channels = conv_w.shape[1:]
    state_all = channels - inner_all
    state_own = state_all // 4
    heads = heads_all // 4
    inner = inner_all // 4
    split = 2 * inner + LANES
    shard_rows = in_w.shape[1]
    direct = heads_all % shards == 0 and (heads_all // shards) % 2 == 0
    groups = shards // 2 if direct else 1
    each = heads // groups
    span = each * head_dim
    sizes = (inner_all, state_all, groups, each, heads_all)

    def pick_row(x, axis):
        return jnp.where(row == 0, lax.index_in_dim(x, 0, axis, False), lax.index_in_dim(x, 1, axis, False))

    def pick(x, axis):
        return links.mine_of_core(lax.index_in_dim(x, 0, axis, False), lax.index_in_dim(x, 1, axis, False))

    def wide_part(x):
        x = pick(x.reshape(x.shape[0], 2, groups, 2, span), 1)
        return pick_row(x, 2).reshape(x.shape[0], inner)

    def head_part(x):
        x = pick(x.reshape(x.shape[0], 2, groups, 2, each), 1)
        return pick_row(x, 2).reshape(x.shape[0], heads)

    def state_part(x):
        x = pick(x.reshape(x.shape[0], 2, 2, state_own), 1)
        return pick_row(x, 1)

    def wide_row(x):
        return jnp.pad(x, ((0, 0), (0, channels - x.shape[1])))

    zero = jnp.int32(0)
    where = jnp.stack([zero, zero, row, core]).astype(jnp.int32)
    own_part, other_part = quarters_of(where, in_w[0], out_w[0] if direct else None, sizes)
    came_part = links.swap_core(other_part)
    both = (links.mine_of_core(own_part, came_part), links.mine_of_core(came_part, own_part))
    if not direct:
        out_first, out_second = out_w[0][:, :half_width], out_w[0][:, half_width:]
        kept = links.mine_of_core(out_first, out_second)
        came = links.swap_core(links.mine_of_core(out_second, out_first))
        out_pieces = (links.mine_of_core(kept, came), links.mine_of_core(came, kept))
    pieces = list(both)

    packed = jnp.concatenate(
        [conv_w[0], conv_b, wide_row(out_gain), wide_row(norm_gain), wide_row(dt_bias), wide_row(a_log), wide_row(skip)],
        axis=0,
    )
    packed_other = links.swap_core(packed)
    all_lengths = links.in_row_order(seq_lengths, links.swap_row(seq_lengths), 0)
    sent_tokens, pieces[0], all_lengths, packed_other = lax.optimization_barrier(
        (inputs, pieces[0], all_lengths, packed_other)
    )

    def layer_params(pack):
        cw, cb = pack[:taps], pack[taps : taps + 1]
        og, ng = pack[taps + 1 : taps + 2, :inner_all], pack[taps + 2 : taps + 3, :width]
        dt, al, sk = (pack[taps + 3 + k : taps + 4 + k, :heads_all] for k in range(3))
        lanes = inner + state_all
        fill = lambda x: jnp.pad(x, ((0, 0), (0, lanes - x.shape[1])))
        conv = jnp.concatenate([cw, cb], axis=0)
        narrow = jnp.concatenate([head_part(dt), -jnp.exp(head_part(al))], axis=0)
        narrow = jnp.pad(narrow, ((0, 0), (0, LANES - heads))).reshape(1, 2 * LANES)
        own_state = jnp.pad(state_part(conv[:, inner_all:]), ((0, 0), (LANES - state_own, 0)))
        rows_ = [
            jnp.concatenate([wide_part(conv[:, :inner_all]), conv[:, inner_all:]], axis=1),
            fill(wide_part(og)),
            fill(jnp.repeat(head_part(sk), head_dim, axis=1)),
            fill(narrow),
            fill(own_state),
        ]
        return fill(jnp.concatenate([jnp.concatenate(rows_, axis=0), jnp.zeros((16 - 2 * taps - 5, lanes), F32)], axis=0)), ng

    blocks = tokens // rows
    big = {}

    def to_rows(x):
        return x.reshape(-1, LANES)

    def norm_of(u):
        return lax.rsqrt(jnp.mean(u * u, axis=-1, keepdims=True) + 1e-05)

    def over_cores(x):
        return links.cut(x, 1, core) + links.swap_core(links.cut(x, 1, 1 - core))

    def own_rows(x):
        return links.cut(x, 0, row)

    def norm_back(u, gain, d_scaled):
        u = u.astype(F32)
        inverse = norm_of(u)
        meet = jnp.mean(u * gain * d_scaled, axis=1, keepdims=True)
        return inverse * gain * d_scaled - u * (inverse * inverse * inverse * meet)

    def gain_back(u, d_scaled):
        u = u.astype(F32)
        return jnp.sum(u * norm_of(u) * d_scaled, axis=0, keepdims=True)

    def scaled_of(u, gain):
        u = u.astype(F32)
        return (u * norm_of(u) * gain).astype(BF16)

    def out_whole(pieces):
        kept, sent = pieces if direct else (links.cut(pieces, 0, core), links.cut(pieces, 0, 1 - core))
        return links.in_core_order(kept, links.swap_core(sent), 1)

    def project(layer, scaled):
        wide_w, last_w = big["in", layer]
        last = dot(scaled, last_w)
        came = links.swap_row(last[:, LANES - state_own :])
        proj = dot(scaled, wide_w)
        proj, last, came = yield [proj, last, came]
        part = links.in_row_order(last[:, LANES - state_own :], came, 1)
        bc = links.in_core_order(part, links.swap_core(part), 1)
        return proj, last, bc

    def mix(layer, proj, last, bc):
        outs, gated, squares = ahead_call(heads, taps, rows, proj, last, bc, aux, seg_rows, big["pack", layer])
        return outs, gated, to_rows(squares[:, 0])

    def over_all(x):
        x = x + links.swap_core(x)
        return x + links.swap_row(x)

    def inverse_of(squares):
        return lax.rsqrt(squares / inner_all + 1e-05)

    def as_columns(*rows_):
        return jnp.stack([x.reshape(tokens) for x in rows_]).T

    def normed_of(layer, gated, inverse):
        gain = big["pack", layer][taps + 1 : taps + 2, :inner]
        normed = (gated * inverse.reshape(tokens, 1) * gain).astype(BF16)
        other = links.swap_core(normed)
        return jnp.concatenate([normed, other], axis=1) if direct else links.in_core_order(normed, other, 1)

    def out_project(normed, weights):
        if direct:
            return dot(normed[:, :inner], weights[0]) + dot(normed[:, inner:], weights[1])
        return dot(normed, weights)

    def back_mix(layer, kept, d_normed, meet):
        scale = as_columns(kept["inverse"], kept["inverse"] * meet / inner_all)
        return back_call(
            heads, taps, rows, kept["proj"], kept["last"], kept["bc"], aux, seg_rows, big["pack", layer],
            kept["outs"], d_normed, scale,
        )

    def back_project(layer, kept, d_main, d_dt, d_bc):
        wide_w, last_w = big["in", layer]
        d_bc = over_cores(d_bc)
        d_scaled = dot(d_main, wide_w, ((1,), (1,)))
        d_bc, d_scaled = yield [d_bc, d_scaled]
        d_bc = links.cut(d_bc, 1, row) + links.swap_row(links.cut(d_bc, 1, 1 - row))
        d_in = outer(kept["scaled"], d_main, width // 3, ROOM)
        d_bc, d_in = yield [d_bc, d_in]
        d_bc = jnp.pad(d_bc, ((0, 0), (LANES - d_bc.shape[1], 0)))
        d_last, d_state = state_back_call(taps, d_bc, kept["last"], aux, big["pack", layer], d_dt)
        d_in_last = dot(kept["scaled"], d_last, ((0,), (0,))).astype(BF16)
        d_scaled = d_scaled + dot(d_last, last_w, ((1,), (1,)))
        return d_scaled, d_in, d_in_last, d_state

    def out_grad(normed, grad_half):
        return dot(normed, grad_half, ((0,), (0,))).astype(BF16)

    aux = seg_rows = None
    done = {}

    def send_out(layer, d_out):
        done["out", layer] = d_out

    def work():
        nonlocal aux, seg_rows
        pack0, gain0 = layer_params(links.mine_of_core(packed, packed_other))
        pack1, gain1 = layer_params(links.mine_of_core(packed_other, packed))
        ends = jnp.cumsum(all_lengths, axis=1)
        positions = jnp.arange(rows, dtype=jnp.int32)
        segments = jnp.sum((positions[None, :, None] >= ends[:, None, :]).astype(jnp.int32), axis=2)
        aux, seg_rows = make_aux(segments, rows, taps), segments.astype(F32)[:, None, :]
        came_tokens = links.swap_row(sent_tokens)
        pack0, pack1, gain0, gain1, aux, seg_rows = yield [pack0, pack1, gain0, gain1, aux, seg_rows]
        big["pack", 0], big["pack", 1] = pack0, pack1
        (came_tokens,) = yield [came_tokens]
        tokens_all = links.in_row_order(inputs, came_tokens, 0)
        scaled = scaled_of(tokens_all, gain0)
        sent_cot, _ = lax.optimization_barrier((cotangent, came_tokens))
        came_cot = links.swap_row(sent_cot)
        tokens_all, scaled = yield [tokens_all, scaled]
        yield [scaled]
        cot_all = links.in_row_order(cotangent, came_cot, 0)
        cot_half = links.cut(cot_all, 1, core)
        cot_all, cot_half = yield [cot_all, cot_half]
        while ("in", 0) not in big:
            yield [scaled]
        wide_w, last_w = big["in", 0]
        if direct:
            wide_w, last_w, *big["out", 0] = yield [wide_w, last_w, *big["out", 0]]
        else:
            wide_w, last_w = yield [wide_w, last_w]
        big["in", 0] = wide_w, last_w
        proj, last, bc = yield from project(0, scaled)
        outs, gated, squares = mix(0, proj, last, bc)
        bc, outs, gated, squares = yield [bc, outs, gated, squares]
        (squares,) = yield [over_all(squares)]
        inverse = inverse_of(squares)
        normed = normed_of(0, gated, inverse)
        while ("out", 0) not in big:
            yield [normed]
        branch = out_project(normed, big["out", 0]).astype(BF16)
        came = links.swap_row(branch)
        normed, inverse, branch = yield [normed, inverse, branch]
        kept0 = {"scaled": scaled, "proj": proj, "last": last, "bc": bc, "outs": outs, "inverse": inverse}
        big["out_whole", 0] = out_whole(big["out", 0])
        came, big["out_whole", 0] = yield [came, big["out_whole", 0]]
        normed0 = normed
        while ("in", 1) not in big or ("out", 1) not in big:
            yield [came]
        branch = branch.astype(F32) + came.astype(F32)
        first = (links.cut(tokens_all, 1, core).astype(F32) + branch).astype(BF16)
        first = links.in_core_order(first, links.swap_core(first), 1)
        scaled = scaled_of(first, gain1)
        big["out_whole", 1] = out_whole(big["out", 1])
        proj, last, bc = yield from project(1, scaled)
        d_normed = dot(cot_all, big["out_whole", 1], ((1,), (1,)))
        outs, gated, squares = mix(1, proj, last, bc)
        gain = big["pack", 1][taps + 1 : taps + 2, :inner]
        meet = to_rows(jnp.sum(gated * gain * d_normed, axis=1))
        both_sums = over_all(jnp.concatenate([squares, meet], axis=0))
        bc, outs, gated, d_normed, both_sums = yield [bc, outs, gated, d_normed, both_sums]
        squares, meet = both_sums[: squares.shape[0]], both_sums[squares.shape[0] :]
        inverse = inverse_of(squares)
        kept1 = {"scaled": scaled, "proj": proj, "last": last, "bc": bc, "outs": outs, "inverse": inverse}
        found = back_mix(1, kept1, d_normed, inverse * inverse * meet)
        d_main, d_dt, d_bc, d_wide1, d_narrow1 = yield list(found)
        normed1 = normed_of(1, gated, inverse)
        d_out = out_grad(normed1, cot_half)
        d_scaled, d_in, d_in_last, d_state1 = yield from back_project(1, kept1, d_main, d_dt, d_bc)
        d_scaled, d_in, d_in_last, d_out = yield [d_scaled, d_in, d_in_last, d_out]
        done["in", 1] = d_in, d_in_last
        send_out(1, d_out)
        small1 = jnp.sum(d_wide1, axis=0), jnp.sum(d_narrow1, axis=0), d_state1
        d_scaled = over_cores(d_scaled).astype(BF16)
        came = links.swap_row(d_scaled)
        (d_scaled,) = yield [d_scaled]
        (came,) = yield [came]
        d_scaled = d_scaled.astype(F32) + came.astype(F32)
        d_scaled = links.in_core_order(d_scaled, links.swap_core(d_scaled), 1)
        grad = (cot_all.astype(F32) + norm_back(first, gain1, d_scaled)).astype(BF16)
        gain_sum1 = gain_back(own_rows(first), own_rows(d_scaled))
        grad, gain_sum1 = yield [grad, gain_sum1]
        grad_half = links.cut(grad, 1, core)
        meet = to_rows(jnp.sum(branch * grad_half.astype(F32), axis=1))
        meet = meet + links.swap_core(meet)
        d_normed = dot(grad, big["out_whole", 0], ((1,), (1,)))
        d_normed, meet, grad_half = yield [d_normed, meet, grad_half]
        found = back_mix(0, kept0, d_normed, kept0["inverse"] * meet)
        d_main, d_dt, d_bc, d_wide0, d_narrow0 = yield list(found)
        d_out = out_grad(normed0, grad_half)
        d_scaled, d_in, d_in_last, d_state0 = yield from back_project(0, kept0, d_main, d_dt, d_bc)
        d_scaled, d_in, d_in_last, d_out = yield [d_scaled, d_in, d_in_last, d_out]
        done["in", 0] = d_in, d_in_last
        send_out(0, d_out)
        small0 = jnp.sum(d_wide0, axis=0), jnp.sum(d_narrow0, axis=0), d_state0
        while ("sum", 1) not in done:
            yield [d_scaled]
        far_upper = links.swap_row(done["sum", 1][: shard_rows // 2])
        d_scaled = over_cores(d_scaled)
        d_scaled, far_upper = yield [d_scaled, far_upper]
        came = links.swap_row(links.cut(d_scaled, 0, 1 - row).astype(BF16))
        partial = out_project(normed1, big["out", 1])
        came, partial = yield [came, partial]
        far_lower = links.swap_row(done["sum", 1][shard_rows // 2 :])
        d_scaled = own_rows(d_scaled) + came.astype(F32)
        d_scaled = links.in_core_order(d_scaled, links.swap_core(d_scaled), 1)
        own_grad = own_rows(grad)
        grad_in = (own_grad.astype(F32) + norm_back(inputs, gain0, d_scaled)).astype(BF16)
        gain_sum0 = gain_back(inputs, d_scaled)
        done["input_grad"] = jnp.where(core == 0, grad_in, own_grad)[None]
        done["input_grad"], gain_sum0, far_lower = yield [done["input_grad"], gain_sum0, far_lower]
        done["far", 1] = jnp.concatenate([far_upper, far_lower], axis=0)
        came = links.swap_row(links.cut(partial, 0, 1 - row).astype(BF16))
        small = jnp.concatenate([pack_small(*small0, gain_sum0), pack_small(*small1, gain_sum1)], axis=0)
        small = small + links.swap_side(small)
        came, small = yield [came, small]
        second = own_rows(partial) + came.astype(F32) + links.cut(own_rows(first), 1, core).astype(F32)
        second = second.astype(BF16)
        second = links.in_core_order(second, links.swap_core(second), 1)
        done["phase_out"] = jnp.where(core == 0, own_rows(first), second)[None]
        small = yield from links.sum_line(small)
        done["phase_out"], small = yield [done["phase_out"], small]
        small_other = links.swap_row(small)
        done["small"] = spread_small(small, small_other)
        done["small"] = yield list(done["small"])

    gain_rows = width // inner

    def pack_small(wide_, narrow, d_state, gain):
        gain = gain.reshape(-1, inner)
        narrow_rows = jnp.concatenate([narrow[:2], d_state[: taps + 1]], axis=0)
        narrow_rows = jnp.pad(narrow_rows.reshape(1, -1), ((0, 0), (0, 2 * inner - narrow_rows.size)))
        return jnp.concatenate([wide_[: taps + 3], gain, narrow_rows.reshape(2, inner)], axis=0)

    def by_row(a, b):
        return jnp.where(row == 0, jnp.stack([a, b]), jnp.stack([b, a]))

    def spread_small(small, small_other):
        per = small.shape[0] // 2
        mine = links.mine_of_core(small[:per], small[per:])
        mine_other = links.mine_of_core(small_other[:per], small_other[per:])
        theirs = links.mine_of_core(small[per:], small[:per])
        theirs_other = links.mine_of_core(small_other[per:], small_other[:per])
        came = links.swap_core(jnp.stack([theirs, theirs_other]))
        own_parts, came_parts = by_row(mine, mine_other), by_row(came[0], came[1])
        quarters = jnp.where(core == 0, jnp.stack([own_parts, came_parts]), jnp.stack([came_parts, own_parts]))

        def spread_wide(x):
            lead = x.shape[2:-1]
            x = x.reshape((2, 2) + lead + (groups, span))
            x = jnp.moveaxis(x, (0, 1), (len(lead), len(lead) + 2))
            return x.reshape(lead + (inner_all,))

        def spread_heads(x):
            x = x.reshape((2, 2, groups, each))
            return jnp.moveaxis(x, 1, 2).reshape(1, heads_all)

        grad_norm = mine[taps + 3 : taps + 3 + gain_rows] + mine_other[taps + 3 : taps + 3 + gain_rows]
        narrow = quarters[:, :, taps + 3 + gain_rows :].reshape(2, 2, -1)
        narrow = narrow[:, :, : (taps + 3) * LANES].reshape(2, 2, taps + 3, LANES)
        states = jnp.moveaxis(narrow[:, :, 2:, LANES - state_own :], 2, 0).reshape(taps + 1, state_all)
        wide_full = spread_wide(quarters[:, :, : taps + 3])
        return [
            grad_norm.reshape(1, width),
            jnp.concatenate([wide_full[:taps], states[:taps]], axis=1)[None],
            jnp.concatenate([wide_full[taps : taps + 1], states[taps:]], axis=1),
            spread_heads(narrow[:, :, 0, :heads]),
            spread_heads(narrow[:, :, 1, :heads]),
            wide_full[taps + 1].reshape(1, heads_all, head_dim).sum(axis=-1),
            wide_full[taps + 2 : taps + 3],
        ]

    schedule = Schedule(work())

    def gather(layer):
        cuts = [(0, 2 * inner), (2 * inner, split)] + ([(split, split + half_width)] if direct else [])
        full = assemble(*schedule.run(links.gather(pieces[layer], layer == 0)), cuts, 2 if direct else None, core * (shards // 2 * shard_rows))
        if direct:
            big["out", layer] = full[2:]
        else:
            big["out", layer] = out_gathered(layer)
        big["in", layer] = full[:2]

    def scatter(layer):
        while ("in", layer) not in done:
            schedule.round([])
        parts = list(done["in", layer])
        if direct:
            parts.append(done["out", layer])
        else:
            sums = done["out", layer].reshape(2, 1, inner, half_width)
            sums = links.in_row_order(sums, jnp.zeros_like(sums), 1).reshape(4 * inner, half_width)
            sums = lax.psum_scatter(sums, "fsdp", scatter_dimension=0, tiled=True)
            done["out_sum", layer] = (sums.astype(F32) + links.swap_row(sums).astype(F32)).astype(BF16)
        by_core = (lambda f: jnp.where(core == 0, f, (f + shards // 2) % shards)) if direct else (lambda f: f)
        laid = [lambda f: f, lambda f: f, by_core]
        parts = [(x.reshape(-1, shard_rows, x.shape[-1]), f) for x, f in zip(parts, laid)]
        done["sum", layer] = schedule.run(links.scatter(shard_rows, parts))

    def out_gathered(layer):
        full = lax.all_gather(out_pieces[layer], "fsdp", axis=0, tiled=True)
        return pick_row(full.reshape(2, 2, inner, half_width), 1).reshape(2 * inner, half_width)

    gather(0)
    gather(1)
    scatter(1)
    scatter(0)
    while schedule.work is not None:
        schedule.round([])

    low0, low1, far1 = done["sum", 0], done["sum", 1], done["far", 1]
    theirs = links.swap_core(links.mine_of_core(low1, low0))
    far0 = links.swap_row(low0)
    quarters = [links.mine_of_core(low0, low1), links.mine_of_core(far0, far1)]
    quarters += [theirs, links.swap_core(links.mine_of_core(far1, far0))]
    if direct:
        grad_in_w, grad_out_w = join(where, quarters, sizes)
    else:
        (grad_in_w,) = join(where, quarters, sizes)
        out0, out1 = done["out_sum", 0], done["out_sum", 1]
        theirs = links.swap_core(links.mine_of_core(out1, out0))
        grad_out_w = links.in_core_order(links.mine_of_core(out0, out1), theirs, 1).astype(F32)[None]
    grad_norm, grad_conv_w, grad_conv_b, grad_dt, grad_a, grad_skip, grad_out_gain = done["small"]
    return (
        done["phase_out"], done["input_grad"], grad_norm, grad_in_w, grad_conv_w, grad_conv_b,
        grad_dt, grad_a, grad_skip, grad_out_gain, grad_out_w,
    )


def solution(mesh):
    return jax.shard_map(
        functools.partial(body, dict(mesh.shape)),
        mesh=mesh,
        in_specs=(
            P(("fsdp", "dp"), None),
            P(("fsdp", "dp"), None),
            P("section", None),
            P("section", "fsdp", None),
            P("section", None, None),
            P("section", None),
            P("section", None),
            P("section", None),
            P("section", None),
            P("section", None),
            P("section", "fsdp", None),
            P(("fsdp", "dp"), None),
        ),
        out_specs=(
            P("section", ("fsdp", "dp"), None),
            P("section", ("fsdp", "dp"), None),
            P("section", None),
            P("section", "fsdp", None),
            P("section", None, None),
            P("section", None),
            P("section", None),
            P("section", None),
            P("section", None),
            P("section", None),
            P("section", "fsdp", None),
        ),
        check_vma=False,
    )
```
